128 devices in a mesh: section: 2 (over core), dp: 64 (over y, z, x).
Axes of the slice: x: 4, y: 4, z: 4, core: 2. Of those that a mesh axis runs over, the one named last changes fastest.
Arguments:
- tokens: bfloat16 [128, 128, 768], P('dp'), may hold values from -6 to 6
- context: bfloat16 [128, 512, 768], P('dp'), may hold values from -6 to 6
- out_cot: bfloat16 [128, 128, 768], P('dp'), may hold values from -6 to 6
- group_id: int32 [128], P('dp'), may hold values from 0 to 7
- ctx_len: int32 [128], P('dp'), may hold values from 128 to 512
- fut_len: int32 [128], P('dp'), may hold values from 64 to 128
- loss_weight: int32 [128, 128], P('dp'), may hold values from 0 to 3
- norm_gain1: float32 [2, 768], P('section'), may hold values from 0.5 to 1.5
- norm_bias1: float32 [2, 768], P('section'), may hold values from -2 to 2
- w_query: bfloat16 [2, 768, 768], P('section'), may hold values from -0.21875 to 0.21875
- w_keyval: bfloat16 [2, 768, 1536], P('section'), may hold values from -0.21875 to 0.21875
- w_out: bfloat16 [2, 768, 768], P('section'), may hold values from -0.625 to 0.625
- norm_gain2: float32 [2, 768], P('section'), may hold values from 0.5 to 1.5
- norm_bias2: float32 [2, 768], P('section'), may hold values from -2 to 2
- w_up: bfloat16 [2, 768, 3072], P('section'), may hold values from -0.21875 to 0.21875
- up_bias: float32 [2, 3072], P('section'), may hold values from -3 to 3
- w_down: bfloat16 [2, 3072, 768], P('section'), may hold values from -0.109375 to 0.109375
Outputs:
- activations: bfloat16 [2, 128, 128, 768], P('section', 'dp')
- input_grads: bfloat16 [2, 128, 128, 768], P('section', 'dp')
- grad_norm_gain1: float32 [2, 768], P('section', 'dp')
- grad_norm_bias1: float32 [2, 768], P('section', 'dp')
- grad_query: float32 [2, 768, 768], P('section', 'dp')
- grad_keyval: float32 [2, 768, 1536], P('section', 'dp')
- grad_out: float32 [2, 768, 768], P('section', 'dp')
- grad_norm_gain2: float32 [2, 768], P('section', 'dp')
- grad_norm_bias2: float32 [2, 768], P('section', 'dp')
- grad_up: float32 [2, 768, 3072], P('section', 'dp')
- grad_up_bias: float32 [2, 3072], P('section', 'dp')
- grad_down: float32 [2, 3072, 768], P('section', 'dp')
The draws below stay inside these ranges and needn't reach their ends.
All inputs are finite; a program needn't handle non-finite values.
Results may differ from the reference program's by a relative error of at most 0.025.
Values may be sent and summed in bfloat16 or wider, within the bound.
A program may use at most 256 MiB of HBM per device.

```python
import math
import jax
import jax.numpy as jnp
import numpy as np
from jax import lax

D = 768
HEADS = 12
HEAD_DIM = 64
FF = 3072
FUT = 128
CTX = 512
GROUPS = 8
SEQS = 128


def plant(entries, own_key, least, high):
    extent = entries.shape
    spot = [jax.random.randint(jax.random.fold_in(own_key, axis), (), 0, extent[axis]) for axis in range(len(extent))]
    entries = entries.at[tuple(spot)].set(least)
    longest = extent.index(max(extent))
    spot[longest] = (spot[longest] + 1) % extent[longest]
    return entries.at[tuple(spot)].set(high)


def shard_levels(stream_key, extent, split, low, largest):
    loudness = 1.0
    for axis_at, shards_of in split:
        steps = jax.random.uniform(jax.random.fold_in(jax.random.fold_in(stream_key, 6), axis_at), (shards_of,), jnp.float32, low / len(split), largest / len(split))
        loudness = loudness * jnp.repeat(jnp.exp(steps), extent[axis_at] // shards_of).reshape((-1,) + (1,) * (len(extent) - 1 - axis_at))
    return loudness


def rank_table(count, slope):
    portions = [(1 << 20) // math.isqrt(grade ** slope) + 1 for grade in range(1, count + 1)]
    deviation = 1 + sum(portions) // (1 << 30)
    return np.cumsum(np.array([max(1, weight // deviation) for weight in portions]))


def ranked(key, dims, number_of, lean):
    listing = rank_table(number_of, lean)
    lot = jax.random.randint(jax.random.fold_in(key, 1), dims, 0, int(listing[number_of - 1]))
    rank = jnp.searchsorted(jnp.asarray(listing, jnp.int32), lot, side="right")
    return jax.random.permutation(jax.random.fold_in(key, 2), number_of)[rank].astype(jnp.int32)


def bell_draw(rng, dims, deviation, most, shards=(), kind=jnp.bfloat16):
    entries = deviation * jax.random.normal(rng, dims, jnp.float32)
    if shards:
        entries = entries * shard_levels(rng, dims, shards, -0.22, 0.18)
    return jnp.clip(entries, -most, most).astype(kind)


def setup_inputs(seed: int = 0) -> dict:
    arg_keys = jax.random.split(jax.random.key(seed), 18)
    return {
        "tokens": bell_draw(arg_keys[0], (SEQS, FUT, D), 1.0, 6.0, ((0, 64),)),
        "context": bell_draw(arg_keys[1], (SEQS, CTX, D), 1.0, 6.0, ((0, 64),)),
        "out_cot": bell_draw(arg_keys[2], (SEQS, FUT, D), 1.0, 6.0, ((0, 64),)),
        "group_id": plant(ranked(arg_keys[3], (SEQS,), GROUPS, 2), jax.random.fold_in(arg_keys[3], 3), 0, GROUPS - 1).astype(jnp.int32),
        "ctx_len": plant(jax.random.randint(arg_keys[4], (SEQS,), CTX // 4, CTX + 1), jax.random.fold_in(arg_keys[4], 1), CTX // 4, CTX).astype(jnp.int32),
        "fut_len": plant(jax.random.randint(arg_keys[5], (SEQS,), FUT // 2, FUT + 1), jax.random.fold_in(arg_keys[5], 1), FUT // 2, FUT).astype(jnp.int32),
        "loss_weight": plant(jax.random.randint(arg_keys[6], (SEQS, FUT), 0, 4), jax.random.fold_in(arg_keys[6], 1), 0, 3).astype(jnp.int32),
        "norm_gain1": jnp.clip(1.0 + 0.1 * jax.random.normal(arg_keys[7], (2, D), jnp.float32), 0.5, 1.5),
        "norm_bias1": bell_draw(arg_keys[8], (2, D), 0.3, 2.0, ((0, 2),), jnp.float32),
        "w_query": bell_draw(arg_keys[9], (2, D, D), D ** -0.5, 0.21875, ((0, 2),)),
        "w_keyval": bell_draw(arg_keys[10], (2, D, 2 * D), D ** -0.5, 0.21875, ((0, 2),)),
        "w_out": bell_draw(arg_keys[11], (2, D, D), (D // 8) ** -0.5, 0.625, ((0, 2),)),
        "norm_gain2": jnp.clip(1.0 + 0.1 * jax.random.normal(arg_keys[12], (2, D), jnp.float32), 0.5, 1.5),
        "norm_bias2": bell_draw(arg_keys[13], (2, D), 0.3, 2.0, ((0, 2),), jnp.float32),
        "w_up": bell_draw(arg_keys[14], (2, D, FF), D ** -0.5, 0.21875, ((0, 2),)),
        "up_bias": bell_draw(arg_keys[15], (2, FF), 0.5, 3.0, ((0, 2),), jnp.float32),
        "w_down": bell_draw(arg_keys[16], (2, FF, D), FF ** -0.5, 0.109375, ((0, 2),)),
    }


@jax.custom_vjp
def low(v):
    return lax.optimization_barrier(v.astype(jnp.bfloat16)).astype(jnp.float32)

@jax.custom_vjp
def low_back(v):
    return v

def low_keep(v):
    return (low(v), None)

def low_pass(kept, grad):
    return (grad,)

def back_keep(v):
    return (v, None)

def back_low(kept, grad):
    return (low(grad),)
low.defvjp(low_keep, low_pass)
low_back.defvjp(back_keep, back_low)
sequence_block_fn = 16

def layer_norm(value, gain, shift_term):
    centre = value - lax.optimization_barrier(jnp.mean(value, axis=-1, keepdims=True))
    spread = lax.optimization_barrier(jnp.mean(centre * centre, axis=-1, keepdims=True))
    return centre * lax.rsqrt(spread + 1e-05) * gain + shift_term

def layer(params, x, ctx, clen, cross, matmul_precision):
    gain1, bias1, wq, key_value_weight, wo, gain2, bias2, wu, bu, wd = params
    if not cross:
        x = low_back(x)
    nseq, rows, width = x.shape
    normed = low(layer_norm(x, gain1, bias1))
    query = low(low_back(jnp.einsum('sfd,de->sfe', normed, wq, precision=matmul_precision)))
    context_source = ctx if cross else normed
    key_value_pair = low(low_back(jnp.einsum('cmt,ti->cmi', context_source, key_value_weight, precision=matmul_precision)))
    cols = context_source.shape[1]
    keys = key_value_pair[..., :width].reshape(nseq, cols, HEADS, HEAD_DIM)
    values = key_value_pair[..., width:].reshape(nseq, cols, HEADS, HEAD_DIM)
    qheads = query.reshape(nseq, rows, HEADS, HEAD_DIM)
    scores = jnp.einsum('sfhd,slhd->shfl', qheads, keys, precision=matmul_precision) / jnp.sqrt(jnp.float32(HEAD_DIM))
    scores = low_back(scores)
    if cross:
        counted = jnp.arange(cols)[None, None, None, :] < clen[:, None, None, None]
    else:
        counted = jnp.arange(cols)[None, None, None, :] <= jnp.arange(rows)[None, None, :, None]
    scores = jnp.where(counted, scores, -1000000000.0)
    probs = low(jax.nn.softmax(scores, axis=-1))
    mixed = jnp.einsum('shfl,slhd->sfhd', probs, values, precision=matmul_precision).reshape(nseq, rows, width)
    mixed = low(low_back(mixed))
    second = x + jnp.einsum('sfd,de->sfe', mixed, wo, precision=matmul_precision)
    normed2 = low(layer_norm(second, gain2, bias2))
    upper = low_back(jnp.einsum('sfd,de->sfe', normed2, wu, precision=matmul_precision) + bu)
    hidden = low(jax.nn.gelu(upper, approximate=True))
    result = second + jnp.einsum('sfe,ed->sfd', hidden, wd, precision=matmul_precision)
    return low(result)

def loss_scale(group_id, fut_len, loss_weight, combine):
    rows = loss_weight.shape[1]
    live = (jnp.arange(rows)[None, :] < fut_len[:, None]).astype(jnp.float32)
    weighted = loss_weight.astype(jnp.float32) * live
    per_seq = lax.optimization_barrier(jnp.sum(weighted, axis=1))
    onehot = (group_id[:, None] == jnp.arange(GROUPS)[None, :]).astype(jnp.float32)
    totals = combine(lax.optimization_barrier(jnp.sum(onehot * per_seq[:, None], axis=0)))
    every = jnp.sum(totals)
    factor = every / (GROUPS * jnp.maximum(totals, 1.0))
    return weighted * lax.optimization_barrier(jnp.sum(onehot * factor[None, :], axis=1))[:, None]

def run(params, x, ctx, clen, cross):
    blocks = x.shape[0] // sequence_block_fn

    def step(carry, item):
        xb, cb, lb = item
        return (carry, layer(params, xb, cb, lb, cross, lax.Precision.HIGHEST))
    _, outs = lax.scan(jax.checkpoint(step), jnp.zeros((), jnp.float32), (x.reshape((blocks, sequence_block_fn) + x.shape[1:]), ctx.reshape((blocks, sequence_block_fn) + ctx.shape[1:]), clen.reshape(blocks, sequence_block_fn)))
    return outs.reshape(x.shape)

def reference(tokens, context, out_cot, group_id, ctx_len, fut_len, loss_weight, norm_gain1, norm_bias1, w_query, w_keyval, w_out, norm_gain2, norm_bias2, w_up, up_bias, w_down):
    weights = (norm_gain1, norm_bias1, w_query, w_keyval, w_out, norm_gain2, norm_bias2, w_up, up_bias, w_down)
    first = tuple((w[0].astype(jnp.float32) for w in weights))
    second = tuple((w[1].astype(jnp.float32) for w in weights))
    ctx = context.astype(jnp.float32)
    coef = loss_scale(group_id, fut_len, loss_weight, lambda v: v)
    hid, pull_one = jax.vjp(lambda p, x: run(p, x, ctx, ctx_len, True), first, tokens.astype(jnp.float32))
    top, pull_two = jax.vjp(lambda p, x: run(p, x, ctx, ctx_len, False), second, hid)
    grad_two, grad_hid = pull_two(coef[:, :, None] * out_cot.astype(jnp.float32))
    grad_one, grad_tok = pull_one(grad_hid)
    acts = jnp.stack([hid, top]).astype(jnp.bfloat16)
    ins = jnp.stack([grad_tok, grad_hid]).astype(jnp.bfloat16)
    g = tuple((jnp.stack([a, b]) for a, b in zip(grad_one, grad_two)))
    return (acts, ins, g[0], g[1], g[2], g[3], g[4], g[5], g[6], g[7], g[8], g[9])
```

```python
import math

import jax
import jax.numpy as jnp
from jax import lax
from jax.experimental import pallas as pl
from jax.experimental.pallas import tpu as pltpu
from jax.sharding import PartitionSpec as P

MESH = pl.DeviceIdType.MESH
BF = jnp.bfloat16
F32 = jnp.float32
GROUPS = 8
D = 768
FF = 3072
SEQ = 128
ROWS = 256
CTX = 512
PAIRS = 6
T = 256
GELU_C = math.sqrt(2.0 / math.pi)
GELU_A = 0.044715


def mm(a, b):
    return jnp.dot(a, b, preferred_element_type=F32)


def mm_nt(a, b):
    return lax.dot_general(a, b, (((1,), (1,)), ((), ())), preferred_element_type=F32)


def mm_tn(a, b):
    return lax.dot_general(a, b, (((0,), (0,)), ((), ())), preferred_element_type=F32)


def loop(n, body, unroll=1):
    def step(i, carry):
        body(i)
        return carry

    lax.fori_loop(0, n, step, 0, unroll=unroll)


def tile(i, size=T):
    return pl.ds(pl.multiple_of(i * size, size), size)


BUFS = dict(
    wq=((D, D), BF),
    wkv=((D, 2 * D), BF),
    wo=((D, D), BF),
    wu=((D, FF), BF),
    wd=((FF, D), BF),
    xb=((ROWS, D), BF),
    ctx=((2 * CTX, D), BF),
    ctxt=((D, 2 * CTX), BF),
    n1=((ROWS, D), BF),
    q=((ROWS, D), BF),
    kv=((2 * CTX, 2 * D), BF),
    p=((2 * PAIRS, ROWS, CTX), BF),
    o=((ROWS, D), BF),
    s2t=((2, D, ROWS), BF),
    n2=((ROWS, D), BF),
    n2t=((D, ROWS), BF),
    x2=((ROWS, D), F32),
    xh1=((ROWS, D), F32),
    xh2=((ROWS, D), F32),
    rs1=((ROWS, 1), F32),
    rs2=((ROWS, 1), F32),
    gp=((4, ROWS, D), BF),
    hm=((4, ROWS, D), BF),
    hmt=((FF, ROWS), BF),
    dyb=((ROWS, D), BF),
    dx=((ROWS, D), F32),
    dn=((ROWS, D), F32),
    do=((ROWS, D), BF),
    d4=((4, ROWS, 384), BF),
    dkvt=((2 * D, 2 * CTX), BF),
    vec=((8, D), F32),
    rvec=((3, 3, 8, D), F32),
    tot=((8, 128), F32),
    rtot=((3, 3, 8, 128), F32),
    rxh=((D, 4 * ROWS), BF),
    rxy=((4 * ROWS, D), BF),
    rxn=((D, 4 * ROWS), BF),
    rxd=((4 * ROWS, D), BF),
    gd=((4, 4, 48, D), BF),
    rd1=((3, 4, 48, D), BF),
    hd=((4, 48, D), BF),
    rd2=((3, 48, D), BF),
    fd=((48, D), F32),
    rfd=((48, D), F32),
    gu=((4, 192, D), BF),
    ru1=((3, 192, D), BF),
    hu=((4, 48, D), BF),
    ru2=((3, 48, D), BF),
    fu=((4, 16, D), BF),
    ru3=((4, 16, D), BF),
    rxa=((D, 4 * ROWS), BF),
    rxb=((4 * ROWS, 384), BF),
    gq=((4, 192, D), BF),
    rq1=((3, 192, D), BF),
    hq=((4, 64, D), BF),
    rq2=((3, 64, D), BF),
    fq=((4, 16, D), BF),
    rq3=((4, 16, D), BF),
    gk=((2, 4, 4, 48, D), BF),
    rk1=((2, 3, 4, 48, D), BF),
    hk=((2, 4, 48, D), BF),
    rk2=((2, 3, 48, D), BF),
    fk=((2, 4, 16, D), BF),
    rk3=((2, 3, 16, D), BF),
    pad=((208, D), F32),
)
KEYS = {}
for _name, _n in dict(
    tot=9, act=1, back=1, a=4, n=4, h=4, y=4, u=4, b=4, a2=4, b2=4,
    d1=4, d2=4, d3=1, u1=4, u2=4, u3=4, q1=4, q2=4, q3=4,
    k1=8, k2=8, k3=8, v=9, load=8,
).items():
    KEYS[_name] = sum(KEYS.values()) if not KEYS else _total
    _total = KEYS[_name] + _n
N_SEMS = _total
NAMES = list(BUFS)


def kernel(*refs):
    (gid, clen, flen, lw, tokens, ctx_in, cot_in, g1, b1, g2, b2, bu, wq_in, wkv_in, wo_in, wu_in, wd_in) = refs[:17]
    (acts, ins, og1, ob1, oq, okv, oo, og2, ob2, oup, oub, odn) = refs[17:29]
    b = dict(zip(NAMES, refs[29 : 29 + len(NAMES)]))
    ssem, rsem = refs[29 + len(NAMES) :]

    sec = lax.axis_index("section")
    dp = lax.axis_index("dp")
    at = {"y": dp // 16, "z": (dp // 4) % 4, "x": dp % 4}
    step = {"y": 16, "z": 4, "x": 1}
    other = 1 - sec

    def peer(axis, r):
        p = lax.rem(at[axis] + r, 4)
        return p, dp + (p - at[axis]) * step[axis]

    barrier = pltpu.get_barrier_semaphore()
    pl.semaphore_signal(barrier, inc=1, device_id=(other, dp), device_id_type=MESH)
    for axis in "xyz":
        for r in (1, 2, 3):
            to = peer(axis, r)[1]
            for core in (sec, other):
                pl.semaphore_signal(barrier, inc=1, device_id=(core, to), device_id_type=MESH)

    def branch(mine):
        cross = mine == 0
        pending = []

        def send(key, i, src, dst, device):
            k = KEYS[key] + i
            copy = pltpu.make_async_remote_copy(
                src_ref=src, dst_ref=dst, send_sem=ssem.at[k], recv_sem=rsem.at[k],
                device_id=device, device_id_type=MESH,
            )
            copy.start()
            pending.append(copy)

        def recv(key, i, ref):
            k = KEYS[key] + i
            pltpu.make_async_remote_copy(
                src_ref=ref, dst_ref=ref, send_sem=ssem.at[k], recv_sem=rsem.at[k],
                device_id=(other, dp), device_id_type=MESH,
            ).wait_recv()

        def local(key, i, src, dst):
            copy = pltpu.make_async_copy(src, dst, rsem.at[KEYS[key] + i])
            copy.start()
            return copy

        loads = {}

        def load(name, i, src, dst):
            loads[name] = local("load", i, src, dst)

        if cross:
            load("x", 0, tokens, b["xb"])
            load("wq", 3, wq_in, b["wq"])
            load("ctx", 1, ctx_in, b["ctx"])
            load("wkv", 2, wkv_in, b["wkv"])
        else:
            load("cot", 0, cot_in, b["do"])
            load("wq", 3, wq_in, b["wq"])
            load("wkv", 2, wkv_in, b["wkv"])
        load("wo", 4, wo_in, b["wo"])
        load("wu", 5, wu_in, b["wu"])
        load("wd", 6, wd_in, b["wd"])

        lane = lax.broadcasted_iota(jnp.int32, (1, 128), 1)
        first_head = lane < 64
        mask_a = first_head.astype(F32).astype(BF)
        mask_b = 1.0 - mask_a

        def stacked(v):
            return jnp.concatenate([v * mask_a, v * mask_b], axis=0)

        def merged(v):
            return jnp.where(first_head, v[:SEQ], v[SEQ:])

        def norm(src, gain, bias, xh, rs, n, nt):
            def body(i):
                rows = tile(i, 32)
                v = src[rows, :].astype(F32)
                centre = v - jnp.mean(v, axis=-1, keepdims=True)
                spread = jnp.mean(centre * centre, axis=-1, keepdims=True)
                scale = lax.rsqrt(spread + 1e-05)
                hat = centre * scale
                xh[rows, :] = hat
                rs[rows, :] = scale
                n[rows, :] = (hat * gain[...] + bias[...]).astype(BF)

            loop(8, body, 2)
            for j in range(3):
                nt[j * T : (j + 1) * T, :] = n[:, j * T : (j + 1) * T].T

        def norm_back(xh, rs, gain, row, done):
            def body(i, carry):
                sum_g, sum_b = carry
                rows = tile(i, 32)
                grad = b["dn"][rows, :]
                hat = xh[rows, :]
                sum_g = sum_g + (grad * hat).reshape(4, 8, D).sum(0)
                sum_b = sum_b + grad.reshape(4, 8, D).sum(0)
                scaled = grad * gain[...]
                mean = jnp.mean(scaled, axis=-1, keepdims=True)
                along = jnp.mean(scaled * hat, axis=-1, keepdims=True)
                done(rows, b["dx"][rows, :] + rs[rows, :] * (scaled - mean - hat * along))
                return sum_g, sum_b

            zero = jnp.zeros((8, D), F32)
            sum_g, sum_b = lax.fori_loop(0, 8, body, (zero, zero))
            b["vec"][row : row + 1, :] = sum_g.sum(0, keepdims=True)
            b["vec"][row + 1 : row + 2, :] = sum_b.sum(0, keepdims=True)

        def gather_to(axis, key, src_of, dst_of, core):
            for r in (1, 3, 2):
                p, to = peer(axis, r)
                send(key, r, src_of(p), dst_of(r), (core, to))
            if core is other:
                send(key, 0, src_of(at[axis]), dst_of(0), (core, dp))
                return None
            return local(key, 0, src_of(at[axis]), dst_of(0))

        def cols(ref):
            return lambda r: ref.at[:, pl.ds(r * ROWS, ROWS)]

        def rows_of(ref):
            return lambda r: ref.at[pl.ds(r * ROWS, ROWS)]

        def scatter(axis, key, src_of, dst_of, base=0, core=sec):
            for r in (1, 3, 2):
                p, to = peer(axis, r)
                send(key, base + r, src_of(p), dst_of(r - 1), (core, to))

        def recv3(key, dst_of, base=0):
            for r in (1, 3, 2):
                recv(key, base + r, dst_of(r - 1))

        if not cross:
            weighted, ids = [], []
            total = jnp.zeros((1, 128), F32)
            for s in range(2):
                w = jnp.where(lane < flen[s], lw[s : s + 1, :].astype(F32), 0.0)
                total = total + jnp.where(lane == gid[s], jnp.sum(w, axis=1, keepdims=True), 0.0)
                weighted.append(w)
            b["tot"][...] = jnp.broadcast_to(total, (8, 128))
        pl.semaphore_wait(barrier, 19)
        if not cross:
            for a, axis in enumerate("xyz"):
                for r in (1, 2, 3):
                    _, to = peer(axis, r)
                    send("tot", 3 * a + r - 1, b["tot"], b["rtot"].at[a, r - 1], (sec, to))
                for r in (1, 2, 3):
                    recv("tot", 3 * a + r - 1, b["rtot"].at[a, r - 1])
                for copy in pending:
                    copy.wait_send()
                pending.clear()
                b["tot"][...] += b["rtot"][a, 0] + b["rtot"][a, 1] + b["rtot"][a, 2]
            totals = b["tot"][0:1, :]
            every = jnp.sum(totals, axis=1, keepdims=True)
            factors = every / (GROUPS * jnp.maximum(totals, 1.0))
            loads["cot"].wait()
            diagonal = lax.broadcasted_iota(jnp.int32, (SEQ, SEQ), 0) == lax.broadcasted_iota(
                jnp.int32, (SEQ, SEQ), 1
            )
            for s in range(2):
                factor = jnp.sum(jnp.where(lane == gid[s], factors, 0.0), axis=1, keepdims=True)
                picked = jnp.where(diagonal, weighted[s], 0.0).astype(BF)
                rows = slice(s * SEQ, (s + 1) * SEQ)
                grad = mm(picked, b["do"][rows, :]) * factor
                b["dx"][rows, :] = grad
                b["dyb"][rows, :] = grad.astype(BF)
            gather_to("y", "y", lambda p: b["dyb"], rows_of(b["rxy"]), other)

        if cross:
            loads["x"].wait()
        else:
            recv("act", 0, b["xb"])
        norm(b["xb"], g1, b1, b["xh1"], b["rs1"], b["n1"], b["s2t"].at[0])

        loads["wq"].wait()

        def query(i):
            b["q"][:, tile(i)] = (mm(b["n1"][...], b["wq"][:, tile(i)]).astype(BF) * 0.125).astype(BF)

        loop(3, query)

        loads["wkv"].wait()
        if cross:
            loads["ctx"].wait()

            def keyval(i):
                for m in range(4):
                    rows = slice(m * T, (m + 1) * T)
                    b["kv"][rows, tile(i)] = mm(b["ctx"][rows, :], b["wkv"][:, tile(i)]).astype(BF)
        else:

            def keyval(i):
                b["kv"][0:ROWS, tile(i)] = mm(b["n1"][...], b["wkv"][:, tile(i)]).astype(BF)

        loop(6, keyval)
        keys = CTX if cross else SEQ

        def blocks(i):
            s, j = i // PAIRS, i % PAIRS
            rows, krows = tile(s, SEQ), tile(s, keys)
            kcols = tile(j, 128)
            vcols = pl.ds(pl.multiple_of(D + j * 128, 128), 128)
            return s, j, rows, krows, kcols, vcols

        def attend(i):
            s, j, rows, krows, kcols, vcols = blocks(i)
            scores = mm_nt(stacked(b["q"][rows, kcols]), b["kv"][krows, kcols])
            col = lax.broadcasted_iota(jnp.int32, (ROWS, keys), 1)
            if cross:
                counted = col < clen[s]
            else:
                row = lax.broadcasted_iota(jnp.int32, (ROWS, keys), 0)
                counted = col <= jnp.where(row < SEQ, row, row - SEQ)
            scores = jnp.where(counted, scores, -1e9)
            e = jnp.exp(scores - jnp.max(scores, axis=-1, keepdims=True))
            probs = (e / jnp.sum(e, axis=-1, keepdims=True)).astype(BF)
            b["p"][i, :, 0:keys] = probs
            b["o"][rows, kcols] = merged(mm(probs, b["kv"][krows, vcols])).astype(BF)

        loop(2 * PAIRS, attend)
        for j in range(3):
            b["s2t"][1, j * T : (j + 1) * T, :] = b["o"][:, j * T : (j + 1) * T].T
        if cross:
            own_a = gather_to("z", "a", lambda p: b["s2t"].at[p // 2], cols(b["rxa"]), sec)
        else:
            own_a = gather_to("z", "a", lambda p: b["s2t"].at[p // 2], cols(b["rxa"]), sec)
            own_a2 = gather_to("z", "a2", lambda p: b["s2t"].at[0], cols(b["ctxt"]), sec)

        loads["wo"].wait()

        def project(i):
            b["x2"][:, tile(i)] = b["xb"][:, tile(i)].astype(F32) + mm(b["o"][...], b["wo"][:, tile(i)])

        loop(3, project)
        norm(b["x2"], g2, b2, b["xh2"], b["rs2"], b["n2"], b["n2t"])
        gather_to("x", "n", lambda p: b["n2t"], cols(b["rxn"]), other)

        loads["wu"].wait()

        def up(i):
            u = mm(b["n2"][...], b["wu"][:, tile(i)]) + bu[:, tile(i)]
            square = u * u
            th = jnp.tanh(GELU_C * u * (1.0 + GELU_A * square))
            half = 0.5 * (1.0 + th)
            hidden = (u * half).astype(BF)
            slope = half + 0.5 * u * (1.0 - th * th) * (GELU_C * (1.0 + 3.0 * GELU_A * square))
            k, at_cols = i // 3, tile(i % 3)
            b["hm"][k, :, at_cols] = hidden
            b["gp"][k, :, at_cols] = slope.astype(BF)
            b["hmt"][tile(i), :] = hidden.T

        loop(12, up)
        gather_to("y", "h", lambda p: b["hmt"].at[tile(p, D)], cols(b["rxh"]), other)

        loads["wd"].wait()

        def down(i):
            y = b["x2"][:, tile(i)]
            for k in range(4):
                y = y + mm(b["hm"][k], b["wd"][k * D : (k + 1) * D, tile(i)])
            acts[:, tile(i)] = y.astype(BF)

        loop(3, down)
        if cross:
            send("act", 0, acts, b["xb"], (other, dp))

        def add4(own, parts):
            total = own.astype(F32)
            for part in parts:
                total = total + part.astype(F32)
            return total

        def down_a():
            for r in range(4):
                recv("h", r, cols(b["rxh"])(r))
                recv("y", r, rows_of(b["rxy"])(r))

            def body(i):
                v = mm(b["rxh"][...], b["rxy"][:, tile(i)]).astype(BF)
                b["gd"][:, :, :, tile(i)] = v.reshape(4, 4, 48, T)

            loop(3, body)
            scatter("x", "d1", lambda p: b["gd"].at[:, p], lambda r: b["rd1"].at[r])

        def down_b():
            recv3("d1", lambda r: b["rd1"].at[r])

            def body(i):
                b["hd"][i] = add4(b["gd"][i, at["x"]], [b["rd1"][r, i] for r in range(3)]).astype(BF)

            loop(4, body)
            scatter("z", "d2", lambda p: b["hd"].at[p], lambda r: b["rd2"].at[r])

        def down_c():
            recv3("d2", lambda r: b["rd2"].at[r])
            b["fd"][...] = add4(b["hd"][at["z"]], [b["rd2"][r] for r in range(3)])
            send("d3", 0, b["fd"], b["rfd"], (other, dp))

        def up_a():
            for r in range(4):
                recv("n", r, cols(b["rxn"])(r))
                recv("u", r, rows_of(b["rxd"])(r))

            def body(i):
                v = mm(b["rxn"][...], b["rxd"][:, tile(i)]).astype(BF)
                b["gu"][:, :, tile(i)] = v.reshape(4, 192, T)

            loop(3, body)
            scatter("y", "u1", lambda p: b["gu"].at[p], lambda r: b["ru1"].at[r])

        def up_b():
            recv3("u1", lambda r: b["ru1"].at[r])

            def body(i):
                rows = tile(i, 48)
                b["hu"][i] = add4(b["gu"][at["y"], rows], [b["ru1"][r, rows] for r in range(3)]).astype(BF)

            loop(4, body)
            scatter("z", "u2", lambda p: b["hu"].at[p], lambda r: b["ru2"].at[r])

        def up_c():
            recv3("u2", lambda r: b["ru2"].at[r])
            b["pad"][0:48, :] = add4(b["hu"][at["z"]], [b["ru2"][r] for r in range(3)])
            for j in range(4):
                b["fu"][j] = b["pad"][12 * j : 12 * j + 16, :].astype(BF)
            for r in (1, 3, 2, 0):
                p, to = peer("x", r)
                send("u3", r, b["fu"].at[p], b["ru3"].at[at["x"]], (other, to))

        width = 384 if cross else D

        def part(ref, *index):
            return ref.at[index + (slice(None), pl.ds(0, width))]

        def qo_a():
            own_a.wait()
            own_b.wait()
            for r in range(1, 4):
                recv("a", r, cols(b["rxa"])(r))
                recv("b", r, rows_of(b["rxb"])(r))
            if not cross:
                own_a2.wait()
                own_b2.wait()
                for r in range(1, 4):
                    recv("a2", r, cols(b["ctxt"])(r))
                    recv("b2", r, b["dkvt"].at[pl.ds(r * ROWS, ROWS), pl.ds(0, 384)])

            def body(i):
                rows = tile(i, 192)
                b["gq"][i, :, 0:384] = mm(b["rxa"][rows, :], b["rxb"][...]).astype(BF)
                if not cross:
                    b["gq"][i, :, 384:768] = mm(b["ctxt"][rows, :], b["dkvt"][0:1024, 0:384]).astype(BF)

            loop(4, body)
            scatter("y", "q1", lambda p: part(b["gq"], p), lambda r: part(b["rq1"], r))

        def qo_b():
            recv3("q1", lambda r: part(b["rq1"], r))

            def body(i):
                rows = tile(i, 48)
                b["pad"][rows, 0:width] = add4(
                    b["gq"][at["y"], rows, 0:width], [b["rq1"][r, rows, 0:width] for r in range(3)]
                )

            loop(4, body)
            for j in range(4):
                for k in range(4):
                    start = 48 * k + 12 * j
                    b["hq"][j, 16 * k : 16 * k + 16, 0:width] = b["pad"][start : start + 16, 0:width].astype(BF)
            scatter("x", "q2", lambda p: part(b["hq"], p), lambda r: part(b["rq2"], r))

        def qo_c():
            recv3("q2", lambda r: part(b["rq2"], r))
            total = add4(b["hq"][at["x"], :, 0:width], [b["rq2"][r, :, 0:width] for r in range(3)])
            b["fq"][:, :, 0:width] = total.astype(BF).reshape(4, 16, width)
            for r in (1, 3, 2):
                p, to = peer("z", r)
                send("q3", r, part(b["fq"], p), part(b["rq3"], at["z"]), (sec, to))
            b["rq3"][at["z"], :, 0:width] = b["fq"][at["z"], :, 0:width]

        def qo_d():
            for r in (1, 3, 2):
                recv("q3", r, part(b["rq3"], 0))
            for k in range(2):
                at_cols = slice(384 * k, 384 * (k + 1))
                oq[:, at_cols] = b["rq3"][k, :, 0:384].astype(F32)[:12]
                oo[:, at_cols] = b["rq3"][2 + k, :, 0:384].astype(F32)[:12]
            if not cross:
                for k in range(4):
                    okv[:, 384 * k : 384 * (k + 1)] = b["rq3"][k, :, 384:768].astype(F32)[:12]

        def kv_a():
            for h in range(2):

                def body(i):
                    v = mm_nt(b["ctxt"][...], b["dkvt"][tile(3 * h + i), :]).astype(BF)
                    b["gk"][h, :, :, :, tile(i)] = v.reshape(4, 4, 48, T)

                loop(3, body)
                scatter("z", "k1", lambda p: b["gk"].at[h, :, p], lambda r: b["rk1"].at[h, r], 4 * h)

        def kv_b(h):
            recv3("k1", lambda r: b["rk1"].at[h, r], 4 * h)

            def body(i):
                b["hk"][h, i] = add4(b["gk"][h, i, at["z"]], [b["rk1"][h, r, i] for r in range(3)]).astype(BF)

            loop(4, body)
            scatter("y", "k2", lambda p: b["hk"].at[h, p], lambda r: b["rk2"].at[h, r], 4 * h)

        def kv_c(h):
            recv3("k2", lambda r: b["rk2"].at[h, r], 4 * h)
            b["pad"][0:48, :] = add4(b["hk"][h, at["y"]], [b["rk2"][h, r] for r in range(3)])
            for j in range(4):
                b["fk"][h, j] = b["pad"][12 * j : 12 * j + 16, :].astype(BF)
            scatter("x", "k3", lambda p: b["fk"].at[h, p], lambda r: b["rk3"].at[h, r], 4 * h)

        def kv_d(h):
            recv3("k3", lambda r: b["rk3"].at[h, r], 4 * h)
            total = add4(b["fk"][h, at["x"]], [b["rk3"][h, r] for r in range(3)])
            okv[:, h * D : (h + 1) * D] = total[:12]

        def vec_send(a):
            for r in (1, 2, 3):
                _, to = peer("xyz"[a], r)
                send("v", 3 * a + r - 1, b["vec"], b["rvec"].at[a, r - 1], (sec, to))

        def vec_add(a):
            for r in (1, 2, 3):
                recv("v", 3 * a + r - 1, b["rvec"].at[a, r - 1])
            for copy in pending[-3:]:
                copy.wait_send()
            del pending[-3:]
            b["vec"][...] += b["rvec"][a, 0] + b["rvec"][a, 1] + b["rvec"][a, 2]

        def vec_out():
            shift = lax.rem(D - 12 * dp, D)
            rolled = pltpu.roll(b["vec"][...], shift, axis=1)
            for row, out in enumerate((og1, ob1, og2, ob2)):
                out[...] = rolled[row : row + 1, 0:12]
            bias_row = b["vec"][pl.ds(4 + at["y"], 1), :]
            shift = lax.rem(D - 48 * lax.rem(dp, 16), D)
            rolled = pltpu.roll(jnp.broadcast_to(bias_row, (8, D)), shift, axis=1)
            oub[...] = rolled[0:1, 0:48]

        b["pad"][192:208, :] = jnp.zeros((16, D), F32)
        b["pad"][48:64, :] = jnp.zeros((16, D), F32)
        if cross:
            for j in range(3):
                for m in range(4):
                    rows, at_cols = slice(m * T, (m + 1) * T), slice(j * T, (j + 1) * T)
                    b["ctxt"][at_cols, rows] = b["ctx"][rows, at_cols].T
            down_a()
            up_a()
            down_b()

        if cross:
            recv("back", 0, b["dyb"])
            b["dx"][...] = b["dyb"][...].astype(F32)
            gather_to("y", "y", lambda p: b["dyb"], rows_of(b["rxy"]), other)

        for k in range(4):

            def up_back(i):
                grad = mm_nt(b["dyb"][...], b["wd"][tile(3 * k + i), :])
                du = (b["gp"][k, :, tile(i)].astype(F32) * grad).astype(BF)
                b["hm"][k, :, tile(i)] = du
                b["vec"][4 + k : 5 + k, tile(i)] = jnp.sum(du.astype(F32), axis=0, keepdims=True)

            loop(3, up_back)
        gather_to("x", "u", lambda p: b["hm"].at[p], rows_of(b["rxd"]), other)

        def n2_back(i):
            grad = jnp.zeros((ROWS, T), F32)
            for k in range(4):
                grad = grad + mm_nt(b["hm"][k], b["wu"][tile(i), k * D : (k + 1) * D])
            b["dn"][:, tile(i)] = grad

        loop(3, n2_back)

        def done2(rows, value):
            b["dx"][rows, :] = value
            rounded = value.astype(BF)
            b["d4"][2, rows, :] = rounded[:, 0:384]
            b["d4"][3, rows, :] = rounded[:, 384:768]

        norm_back(b["xh2"], b["rs2"], g2, 2, done2)

        def out_back(i):
            rows = tile(i)
            grad = mm_nt(b["d4"][2], b["wo"][rows, 0:384]) + mm_nt(b["d4"][3], b["wo"][rows, 384:768])
            b["do"][:, tile(i)] = grad.astype(BF)

        loop(3, out_back)

        def attend_back(i):
            s, j, rows, krows, kcols, vcols = blocks(i)
            k2, v2 = b["kv"][krows, kcols], b["kv"][krows, vcols]
            do2 = stacked(b["do"][rows, kcols])
            q2 = stacked(b["q"][rows, kcols])
            probs = b["p"][i, :, 0:keys]
            wide = probs.astype(F32)
            grad = wide * mm_nt(do2, v2)
            ds = (grad - wide * jnp.sum(grad, axis=-1, keepdims=True)).astype(BF)
            half, at_cols = j // 3, tile(j % 3, 128)
            b["d4"][half, rows, at_cols] = (merged(mm(ds, k2)) * 0.125).astype(BF)
            if cross:
                b["dkvt"][tile(j, 128), krows] = mm_tn(q2, ds).astype(BF)
                b["dkvt"][vcols, krows] = mm_tn(do2, probs).astype(BF)
            else:
                krows4 = pl.ds(pl.multiple_of(half * ROWS + s * SEQ, SEQ), SEQ)
                vrows4 = pl.ds(pl.multiple_of((2 + half) * ROWS + s * SEQ, SEQ), SEQ)
                b["ctx"][krows4, at_cols] = mm_tn(ds, q2).astype(BF)
                b["ctx"][vrows4, at_cols] = mm_tn(probs, do2).astype(BF)

        loop(2 * PAIRS, attend_back)
        own_b = gather_to("z", "b", lambda p: b["d4"].at[p], rows_of(b["rxb"]), sec)
        if not cross:

            def kv_quarter(p):
                return b["ctx"].at[tile(p, ROWS), pl.ds(0, 384)]

            own_b2 = gather_to(
                "z", "b2", kv_quarter, lambda r: b["dkvt"].at[pl.ds(r * ROWS, ROWS), pl.ds(0, 384)], sec
            )

        def n1_back(i):
            rows = tile(i)
            grad = mm_nt(b["d4"][0], b["wq"][rows, 0:384]) + mm_nt(b["d4"][1], b["wq"][rows, 384:768])
            if not cross:
                for k in range(4):
                    quarter = b["ctx"][k * ROWS : (k + 1) * ROWS, 0:384]
                    grad = grad + mm_nt(quarter, b["wkv"][rows, 384 * k : 384 * (k + 1)])
            b["dn"][:, tile(i)] = grad

        loop(3, n1_back)

        def done1(rows, value):
            ins[rows, :] = value.astype(BF)

        norm_back(b["xh1"], b["rs1"], g1, 0, done1)
        if not cross:
            send("back", 0, ins, b["dyb"], (other, dp))

        if cross:
            kv_a()
            up_b()
            down_c()
            vec_send(0)
            vec_add(0)
            qo_a()
            up_c()
            vec_send(1)
            vec_add(1)
            kv_b(0)
            qo_b()
            kv_b(1)
            vec_send(2)
            vec_add(2)
            kv_c(0)
            qo_c()
            kv_c(1)
            vec_out()
            kv_d(0)
            kv_d(1)
            qo_d()
        else:
            qo_a()
            vec_send(0)
            vec_add(0)
            down_a()
            qo_b()
            vec_send(1)
            vec_add(1)
            up_a()
            qo_c()
            vec_send(2)
            vec_add(2)
            down_b()
            vec_out()
            qo_d()
            up_b()
            down_c()
            up_c()
        recv("d3", 0, b["rfd"])
        odn[...] = b["rfd"][...]
        for r in (1, 3, 2, 0):
            recv("u3", r, b["ru3"].at[0])
        for k in range(4):
            oup[:, k * D : (k + 1) * D] = b["ru3"][k].astype(F32)[:12]
        for copy in pending:
            copy.wait_send()

    pl.when(sec == 0)(lambda: branch(0))
    pl.when(sec == 1)(lambda: branch(1))


def on_device(
    tokens, context, out_cot, group_id, ctx_len, fut_len, loss_weight,
    norm_gain1, norm_bias1, w_query, w_keyval, w_out,
    norm_gain2, norm_bias2, w_up, up_bias, w_down,
):
    smem = pl.BlockSpec(memory_space=pltpu.SMEM)
    vmem = pl.BlockSpec(memory_space=pltpu.VMEM)
    hbm = pl.BlockSpec(memory_space=pl.ANY)
    shape = jax.ShapeDtypeStruct
    outs = pl.pallas_call(
        kernel,
        out_shape=(
            shape((ROWS, D), BF),
            shape((ROWS, D), BF),
            shape((1, 12), F32),
            shape((1, 12), F32),
            shape((12, D), F32),
            shape((12, 2 * D), F32),
            shape((12, D), F32),
            shape((1, 12), F32),
            shape((1, 12), F32),
            shape((12, FF), F32),
            shape((1, 48), F32),
            shape((48, D), F32),
        ),
        in_specs=[smem] * 3 + [vmem] + [hbm] * 3 + [vmem] * 5 + [hbm] * 5,
        out_specs=[vmem] * 12,
        scratch_shapes=[pltpu.VMEM(s, t) for s, t in BUFS.values()]
        + [pltpu.SemaphoreType.DMA((N_SEMS,)), pltpu.SemaphoreType.DMA((N_SEMS,))],
        compiler_params=pltpu.CompilerParams(
            collective_id=0, has_side_effects=True, vmem_limit_bytes=64 * 1024 * 1024 - 4096
        ),
    )(
        group_id, ctx_len, fut_len, loss_weight,
        tokens.reshape(ROWS, D), context.reshape(2 * CTX, D), out_cot.reshape(ROWS, D),
        norm_gain1, norm_bias1, norm_gain2, norm_bias2, up_bias,
        w_query[0], w_keyval[0], w_out[0], w_up[0], w_down[0],
    )
    acts, ins, gg1, gb1, gq, gkv, go, gg2, gb2, gup, gub, gdn = outs
    seqs = (1, 2, SEQ, D)
    return (
        acts.reshape(seqs), ins.reshape(seqs), gg1, gb1, gq[None], gkv[None], go[None],
        gg2, gb2, gup[None], gub, gdn[None],
    )


def solution(mesh):
    dp, sec = "dp", "section"
    vec, mat = P(sec, None), P(sec, None, None)
    return jax.shard_map(
        on_device,
        mesh=mesh,
        in_specs=(P(dp, None, None),) * 3 + (P(dp),) * 3 + (P(dp, None),)
        + (vec, vec, mat, mat, mat, vec, vec, mat, vec, mat),
        out_specs=(P(sec, dp, None, None),) * 2 + (P(sec, dp),) * 2 + (P(sec, dp, None),) * 3
        + (P(sec, dp),) * 2 + (P(sec, dp, None), P(sec, dp), P(sec, dp, None)),
        check_vma=False,
    )
```

```python
import math

import jax
import jax.numpy as jnp
from jax import lax
from jax.experimental import pallas as pl
from jax.experimental.pallas import tpu as pltpu
from jax.sharding import PartitionSpec as P

MESH = pl.DeviceIdType.MESH
BF = jnp.bfloat16
F32 = jnp.float32
GROUPS = 8
D = 768
FF = 3072
SEQ = 128
ROWS = 256
CTX = 512
PAIRS = 6
T = 256
GELU_C = math.sqrt(2.0 / math.pi)
GELU_A = 0.044715


def mm(a, b):
    return jnp.dot(a, b, preferred_element_type=F32)


def mm_nt(a, b):
    return lax.dot_general(a, b, (((1,), (1,)), ((), ())), preferred_element_type=F32)


def mm_tn(a, b):
    return lax.dot_general(a, b, (((0,), (0,)), ((), ())), preferred_element_type=F32)


def loop(n, body):
    for i in range(n):
        body(i)


def tile(i, size=T):
    if isinstance(i, int):
        return slice(i * size, (i + 1) * size)
    return pl.ds(pl.multiple_of(i * size, size), size)


BUFS = dict(
    wq=((D, D), BF),
    wkv=((D, 2 * D), BF),
    wo=((D, D), BF),
    wu=((D, FF), BF),
    wd=((FF, D), BF),
    xb=((ROWS, D), BF),
    ctx=((2 * CTX, D), BF),
    ctxt=((D, 2 * CTX), BF),
    n1=((ROWS, D), BF),
    q=((ROWS, D), BF),
    kv=((2 * CTX, 2 * D), BF),
    p=((2 * PAIRS, ROWS, CTX), BF),
    inv=((ROWS, D), F32),
    o=((ROWS, D), BF),
    s2t=((2, D, ROWS), BF),
    n2=((ROWS, D), BF),
    n2t=((D, ROWS), BF),
    x2=((ROWS, D), F32),
    xh1=((ROWS, D), F32),
    xh2=((ROWS, D), F32),
    rs1=((ROWS, 1), F32),
    rs2=((ROWS, 1), F32),
    gp=((4, ROWS, D), BF),
    hm=((4, ROWS, D), BF),
    hmt=((FF, ROWS), BF),
    dyb=((ROWS, D), BF),
    dx=((ROWS, D), F32),
    d4=((4, ROWS, 384), BF),
    dkvt=((2 * D, 2 * CTX), BF),
    vec=((8, D), F32),
    rvec=((3, 3, 8, D), F32),
    tot=((8, 128), F32),
    rtot=((3, 3, 8, 128), F32),
    rxh=((D, 4 * ROWS), BF),
    rxy=((4 * ROWS, D), BF),
    rxn=((D, 4 * ROWS), BF),
    rxd=((4 * ROWS, D), BF),
    gd=((4, 4, 48, D), BF),
    rd1=((3, 4, 48, D), BF),
    hd=((4, 48, D), BF),
    rd2=((3, 48, D), BF),
    rfd=((48, D), F32),
    gu=((4, 192, D), BF),
    ru1=((3, 192, D), BF),
    hu=((4, 48, D), BF),
    ru2=((3, 48, D), BF),
    fu=((4, 16, D), BF),
    ru3=((4, 16, D), BF),
    rxa=((D, 4 * ROWS), BF),
    rxb=((4 * ROWS, 384), BF),
    gq=((4, 192, D), BF),
    rq1=((3, 192, D), BF),
    hq=((4, 64, D), BF),
    rq2=((3, 64, D), BF),
    fq=((4, 16, D), BF),
    rq3=((4, 16, D), BF),
    gk=((2, 4, 4, 48, D), BF),
    rk1=((2, 3, 4, 48, D), BF),
    hk=((2, 4, 48, D), BF),
    rk2=((2, 3, 48, D), BF),
    fk=((2, 4, 16, D), BF),
    rk3=((2, 3, 16, D), BF),
)
KEYS = {}
for _name, _n in dict(
    tot=9, act=1, back=1, a=4, n=4, h=4, y=4, u=4, b=4, a2=4, b2=4,
    d1=4, d2=4, d3=1, u1=4, u2=4, u3=4, q1=4, q2=4, q3=4,
    k1=8, k2=8, k3=8, v=9, load=8,
).items():
    KEYS[_name] = sum(KEYS.values()) if not KEYS else _total
    _total = KEYS[_name] + _n
N_SEMS = _total
NAMES = list(BUFS)


def kernel(*refs):
    (gid, clen, flen, lw, tokens, ctx_in, cot_in, g1, b1, g2, b2, bu, wq_in, wkv_in, wo_in, wu_in, wd_in) = refs[:17]
    (acts, ins, og1, ob1, oq, okv, oo, og2, ob2, oup, oub, odn) = refs[17:29]
    b = dict(zip(NAMES, refs[29 : 29 + len(NAMES)]))
    b["do"] = b["n1"]
    b["dn"] = b["x2"]
    b["pad"] = b["x2"].at[pl.ds(0, 208)]
    b["fd"] = b["x2"].at[pl.ds(208, 48)]
    ssem, rsem = refs[29 + len(NAMES) :]

    sec = lax.axis_index("section")
    dp = lax.axis_index("dp")
    at = {"y": dp // 16, "z": (dp // 4) % 4, "x": dp % 4}
    step = {"y": 16, "z": 4, "x": 1}
    other = 1 - sec

    def peer(axis, r):
        p = lax.rem(at[axis] + r, 4)
        return p, dp + (p - at[axis]) * step[axis]

    barrier = pltpu.get_barrier_semaphore()
    pl.semaphore_signal(barrier, inc=1, device_id=(other, dp), device_id_type=MESH)
    for axis in "xyz":
        for r in (1, 2, 3):
            to = peer(axis, r)[1]
            for core in (sec, other):
                pl.semaphore_signal(barrier, inc=1, device_id=(core, to), device_id_type=MESH)

    def branch(mine):
        cross = mine == 0
        pending = []

        def send(key, i, src, dst, device):
            k = KEYS[key] + i
            copy = pltpu.make_async_remote_copy(
                src_ref=src, dst_ref=dst, send_sem=ssem.at[k], recv_sem=rsem.at[k],
                device_id=device, device_id_type=MESH,
            )
            copy.start()
            pending.append(copy)

        def recv(key, i, ref):
            k = KEYS[key] + i
            pltpu.make_async_remote_copy(
                src_ref=ref, dst_ref=ref, send_sem=ssem.at[k], recv_sem=rsem.at[k],
                device_id=(other, dp), device_id_type=MESH,
            ).wait_recv()

        def local(key, i, src, dst):
            copy = pltpu.make_async_copy(src, dst, rsem.at[KEYS[key] + i])
            copy.start()
            return copy

        loads = {}

        def load(name, i, src, dst):
            loads[name] = local("load", i, src, dst)

        if cross:
            load("x", 0, tokens, b["xb"])
            load("wq", 3, wq_in, b["wq"])
            load("ctx", 1, ctx_in, b["ctx"])
            load("wkv", 2, wkv_in, b["wkv"])
        else:
            load("cot", 0, cot_in, b["do"])
            load("wq", 3, wq_in, b["wq"])
            load("wkv", 2, wkv_in, b["wkv"])
        load("wo", 4, wo_in, b["wo"])
        load("wu", 5, wu_in, b["wu"])
        load("wd", 6, wd_in, b["wd"])

        lane = lax.broadcasted_iota(jnp.int32, (1, 128), 1)
        first_head = lane < 64
        mask_a = first_head.astype(F32).astype(BF)
        mask_b = 1.0 - mask_a

        def stacked(v):
            return jnp.concatenate([v * mask_a, v * mask_b], axis=0)

        def merged(v):
            return jnp.where(first_head, v[:SEQ], v[SEQ:])

        def norm(src, gain, bias, xh, rs, n, nt):
            def body(i):
                rows = tile(i, 32)
                v = src[rows, :].astype(F32)
                centre = v - jnp.mean(v, axis=-1, keepdims=True)
                spread = jnp.mean(centre * centre, axis=-1, keepdims=True)
                scale = lax.rsqrt(spread + 1e-05)
                hat = centre * scale
                xh[rows, :] = hat
                rs[rows, :] = scale
                n[rows, :] = (hat * gain[...] + bias[...]).astype(BF)

            loop(8, body)
            for j in range(3):
                nt[j * T : (j + 1) * T, :] = n[:, j * T : (j + 1) * T].T

        def norm_back(xh, rs, gain, row, done):
            def body(i, carry):
                sum_g, sum_b = carry
                rows = tile(i, 32)
                grad = b["dn"][rows, :]
                hat = xh[rows, :]
                sum_g = sum_g + (grad * hat).reshape(4, 8, D).sum(0)
                sum_b = sum_b + grad.reshape(4, 8, D).sum(0)
                scaled = grad * gain[...]
                mean = jnp.mean(scaled, axis=-1, keepdims=True)
                along = jnp.mean(scaled * hat, axis=-1, keepdims=True)
                done(rows, b["dx"][rows, :] + rs[rows, :] * (scaled - mean - hat * along))
                return sum_g, sum_b

            sums = (jnp.zeros((8, D), F32),) * 2
            for i in range(8):
                sums = body(i, sums)
            sum_g, sum_b = sums
            b["vec"][row : row + 1, :] = sum_g.sum(0, keepdims=True)
            b["vec"][row + 1 : row + 2, :] = sum_b.sum(0, keepdims=True)

        def gather_to(axis, key, src_of, dst_of, core):
            for r in (1, 3, 2):
                p, to = peer(axis, r)
                send(key, r, src_of(p), dst_of(r), (core, to))
            if core is other:
                send(key, 0, src_of(at[axis]), dst_of(0), (core, dp))
                return None
            return local(key, 0, src_of(at[axis]), dst_of(0))

        def cols(ref):
            return lambda r: ref.at[:, pl.ds(r * ROWS, ROWS)]

        def rows_of(ref):
            return lambda r: ref.at[pl.ds(r * ROWS, ROWS)]

        def scatter(axis, key, src_of, dst_of, base=0, core=sec):
            for r in (1, 3, 2):
                p, to = peer(axis, r)
                send(key, base + r, src_of(p), dst_of(r - 1), (core, to))

        def recv3(key, dst_of, base=0):
            for r in (1, 3, 2):
                recv(key, base + r, dst_of(r - 1))

        if not cross:
            weighted, ids = [], []
            total = jnp.zeros((1, 128), F32)
            for s in range(2):
                w = jnp.where(lane < flen[s], lw[s : s + 1, :].astype(F32), 0.0)
                total = total + jnp.where(lane == gid[s], jnp.sum(w, axis=1, keepdims=True), 0.0)
                weighted.append(w)
            b["tot"][...] = jnp.broadcast_to(total, (8, 128))
        pl.semaphore_wait(barrier, 19)
        if not cross:
            for a, axis in enumerate("xyz"):
                for r in (1, 2, 3):
                    _, to = peer(axis, r)
                    send("tot", 3 * a + r - 1, b["tot"], b["rtot"].at[a, r - 1], (sec, to))
                for r in (1, 2, 3):
                    recv("tot", 3 * a + r - 1, b["rtot"].at[a, r - 1])
                for copy in pending:
                    copy.wait_send()
                pending.clear()
                b["tot"][...] += b["rtot"][a, 0] + b["rtot"][a, 1] + b["rtot"][a, 2]
            totals = b["tot"][0:1, :]
            every = jnp.sum(totals, axis=1, keepdims=True)
            factors = every / (GROUPS * jnp.maximum(totals, 1.0))
            loads["cot"].wait()
            diagonal = lax.broadcasted_iota(jnp.int32, (SEQ, SEQ), 0) == lax.broadcasted_iota(
                jnp.int32, (SEQ, SEQ), 1
            )
            for s in range(2):
                factor = jnp.sum(jnp.where(lane == gid[s], factors, 0.0), axis=1, keepdims=True)
                picked = jnp.where(diagonal, weighted[s], 0.0).astype(BF)
                rows = slice(s * SEQ, (s + 1) * SEQ)
                grad = mm(picked, b["do"][rows, :]) * factor
                b["dx"][rows, :] = grad
                b["dyb"][rows, :] = grad.astype(BF)
            gather_to("y", "y", lambda p: b["dyb"], rows_of(b["rxy"]), other)

        if cross:
            loads["x"].wait()
        else:
            recv("act", 0, b["xb"])
        norm(b["xb"], g1, b1, b["xh1"], b["rs1"], b["n1"], b["s2t"].at[0])

        loads["wq"].wait()

        def query(i):
            b["q"][:, tile(i)] = (mm(b["n1"][...], b["wq"][:, tile(i)]).astype(BF) * 0.125).astype(BF)

        loop(3, query)

        loads["wkv"].wait()
        if cross:
            loads["ctx"].wait()

            def keyval(i):
                for m in range(4):
                    rows = slice(m * T, (m + 1) * T)
                    b["kv"][rows, tile(i)] = mm(b["ctx"][rows, :], b["wkv"][:, tile(i)]).astype(BF)
        else:

            def keyval(i):
                b["kv"][0:ROWS, tile(i)] = mm(b["n1"][...], b["wkv"][:, tile(i)]).astype(BF)

        loop(6, keyval)
        keys = CTX if cross else SEQ

        def blocks(i):
            s, j = i // PAIRS, i % PAIRS
            vcols = slice(D + 128 * j, D + 128 * (j + 1))
            return s, j, tile(s, SEQ), tile(s, keys), tile(j, 128), vcols

        if cross:
            key = lax.broadcasted_iota(jnp.int32, (1, keys), 1)
            masks = [jnp.where(key < clen[s], 0.0, -1e9) for s in range(2)]
        else:
            row = lax.broadcasted_iota(jnp.int32, (SEQ, keys), 0)
            mask = jnp.where(lax.broadcasted_iota(jnp.int32, (SEQ, keys), 1) <= row, 0.0, -1e9)
            masks = [jnp.concatenate([mask, mask], axis=0)] * 2
        ones = jnp.ones((keys, 128), BF)

        def attend(i):
            s, j, rows, krows, kcols, vcols = blocks(i)
            scores = mm_nt(stacked(b["q"][rows, kcols]), b["kv"][krows, kcols]) + masks[s]
            e = jnp.exp(scores - jnp.max(scores, axis=-1, keepdims=True))
            values = b["kv"][krows, vcols]
            if cross:
                e = e.astype(BF)
                b["p"][i] = e
                mixed = mm(e, jnp.concatenate([values, ones], axis=1))
                scale = 1.0 / merged(mixed[:, 128:])
                b["inv"][rows, kcols] = scale
                b["o"][rows, kcols] = (merged(mixed[:, :128]) * scale).astype(BF)
            else:
                probs = (e / jnp.sum(e, axis=-1, keepdims=True)).astype(BF)
                b["p"][i, :, 0:keys] = probs
                b["o"][rows, kcols] = merged(mm(probs, values)).astype(BF)

        loop(2 * PAIRS, attend)
        for j in range(3):
            b["s2t"][1, j * T : (j + 1) * T, :] = b["o"][:, j * T : (j + 1) * T].T
        if cross:
            own_a = gather_to("z", "a", lambda p: b["s2t"].at[p // 2], cols(b["rxa"]), sec)
        else:
            own_a = gather_to("z", "a", lambda p: b["s2t"].at[p // 2], cols(b["rxa"]), sec)
            own_a2 = gather_to("z", "a2", lambda p: b["s2t"].at[0], cols(b["ctxt"]), sec)

        loads["wo"].wait()

        def project(i):
            b["x2"][:, tile(i)] = b["xb"][:, tile(i)].astype(F32) + mm(b["o"][...], b["wo"][:, tile(i)])

        loop(3, project)
        norm(b["x2"], g2, b2, b["xh2"], b["rs2"], b["n2"], b["n2t"])
        gather_to("x", "n", lambda p: b["n2t"], cols(b["rxn"]), other)

        loads["wu"].wait()

        def up(i):
            u = mm(b["n2"][...], b["wu"][:, tile(i)]) + bu[:, tile(i)]
            square = u * u
            th = jnp.tanh(GELU_C * u * (1.0 + GELU_A * square))
            half = 0.5 * (1.0 + th)
            hidden = (u * half).astype(BF)
            slope = half + 0.5 * u * (1.0 - th * th) * (GELU_C * (1.0 + 3.0 * GELU_A * square))
            k, at_cols = i // 3, tile(i % 3)
            b["hm"][k, :, at_cols] = hidden
            b["gp"][k, :, at_cols] = slope.astype(BF)
            b["hmt"][tile(i), :] = hidden.T

        loop(12, up)
        gather_to("y", "h", lambda p: b["hmt"].at[tile(p, D)], cols(b["rxh"]), other)

        loads["wd"].wait()

        def down(i):
            y = b["x2"][:, tile(i)]
            for k in range(4):
                y = y + mm(b["hm"][k], b["wd"][k * D : (k + 1) * D, tile(i)])
            acts[:, tile(i)] = y.astype(BF)

        loop(3, down)
        if cross:
            send("act", 0, acts, b["xb"], (other, dp))

        def add4(own, parts):
            total = own.astype(F32)
            for part in parts:
                total = total + part.astype(F32)
            return total

        def down_a():
            for r in range(4):
                recv("h", r, cols(b["rxh"])(r))
                recv("y", r, rows_of(b["rxy"])(r))

            def body(i):
                v = mm(b["rxh"][...], b["rxy"][:, tile(i)]).astype(BF)
                b["gd"][:, :, :, tile(i)] = v.reshape(4, 4, 48, T)

            loop(3, body)
            scatter("x", "d1", lambda p: b["gd"].at[:, p], lambda r: b["rd1"].at[r])

        def down_b():
            recv3("d1", lambda r: b["rd1"].at[r])

            def body(i):
                b["hd"][i] = add4(b["gd"][i, at["x"]], [b["rd1"][r, i] for r in range(3)]).astype(BF)

            loop(4, body)
            scatter("z", "d2", lambda p: b["hd"].at[p], lambda r: b["rd2"].at[r])

        def down_c():
            recv3("d2", lambda r: b["rd2"].at[r])
            b["fd"][...] = add4(b["hd"][at["z"]], [b["rd2"][r] for r in range(3)])
            send("d3", 0, b["fd"], b["rfd"], (other, dp))

        def up_a():
            for r in range(4):
                recv("n", r, cols(b["rxn"])(r))
                recv("u", r, rows_of(b["rxd"])(r))

            def body(i):
                v = mm(b["rxn"][...], b["rxd"][:, tile(i)]).astype(BF)
                b["gu"][:, :, tile(i)] = v.reshape(4, 192, T)

            loop(3, body)
            scatter("y", "u1", lambda p: b["gu"].at[p], lambda r: b["ru1"].at[r])

        def up_b():
            recv3("u1", lambda r: b["ru1"].at[r])

            def body(i):
                rows = tile(i, 48)
                b["hu"][i] = add4(b["gu"][at["y"], rows], [b["ru1"][r, rows] for r in range(3)]).astype(BF)

            loop(4, body)
            scatter("z", "u2", lambda p: b["hu"].at[p], lambda r: b["ru2"].at[r])

        def up_c():
            recv3("u2", lambda r: b["ru2"].at[r])
            b["pad"][0:48, :] = add4(b["hu"][at["z"]], [b["ru2"][r] for r in range(3)])
            for j in range(4):
                b["fu"][j] = b["pad"][12 * j : 12 * j + 16, :].astype(BF)
            for r in (1, 3, 2, 0):
                p, to = peer("x", r)
                send("u3", r, b["fu"].at[p], b["ru3"].at[at["x"]], (other, to))

        width = 384 if cross else D

        def part(ref, *index):
            return ref.at[index + (slice(None), pl.ds(0, width))]

        def qo_a():
            own_a.wait()
            own_b.wait()
            for r in range(1, 4):
                recv("a", r, cols(b["rxa"])(r))
                recv("b", r, rows_of(b["rxb"])(r))
            if not cross:
                own_a2.wait()
                own_b2.wait()
                for r in range(1, 4):
                    recv("a2", r, cols(b["ctxt"])(r))
                    recv("b2", r, b["dkvt"].at[pl.ds(r * ROWS, ROWS), pl.ds(0, 384)])

            def body(i):
                rows = tile(i, 192)
                b["gq"][i, :, 0:384] = mm(b["rxa"][rows, :], b["rxb"][...]).astype(BF)
                if not cross:
                    b["gq"][i, :, 384:768] = mm(b["ctxt"][rows, :], b["dkvt"][0:1024, 0:384]).astype(BF)

            loop(4, body)
            scatter("y", "q1", lambda p: part(b["gq"], p), lambda r: part(b["rq1"], r))

        def qo_b():
            recv3("q1", lambda r: part(b["rq1"], r))

            def body(i):
                rows = tile(i, 48)
                b["pad"][rows, 0:width] = add4(
                    b["gq"][at["y"], rows, 0:width], [b["rq1"][r, rows, 0:width] for r in range(3)]
                )

            loop(4, body)
            for j in range(4):
                for k in range(4):
                    start = 48 * k + 12 * j
                    b["hq"][j, 16 * k : 16 * k + 16, 0:width] = b["pad"][start : start + 16, 0:width].astype(BF)
            scatter("x", "q2", lambda p: part(b["hq"], p), lambda r: part(b["rq2"], r))

        def qo_c():
            recv3("q2", lambda r: part(b["rq2"], r))
            total = add4(b["hq"][at["x"], :, 0:width], [b["rq2"][r, :, 0:width] for r in range(3)])
            b["fq"][:, :, 0:width] = total.astype(BF).reshape(4, 16, width)
            for r in (1, 3, 2):
                p, to = peer("z", r)
                send("q3", r, part(b["fq"], p), part(b["rq3"], at["z"]), (sec, to))
            b["rq3"][at["z"], :, 0:width] = b["fq"][at["z"], :, 0:width]

        def qo_d():
            for r in (1, 3, 2):
                recv("q3", r, part(b["rq3"], 0))
            for k in range(2):
                at_cols = slice(384 * k, 384 * (k + 1))
                oq[:, at_cols] = b["rq3"][k, :, 0:384].astype(F32)[:12]
                oo[:, at_cols] = b["rq3"][2 + k, :, 0:384].astype(F32)[:12]
            if not cross:
                for k in range(4):
                    okv[:, 384 * k : 384 * (k + 1)] = b["rq3"][k, :, 384:768].astype(F32)[:12]

        def kv_a():
            for h in range(2):

                def body(i):
                    v = mm_nt(b["ctxt"][...], b["dkvt"][tile(3 * h + i), :]).astype(BF)
                    b["gk"][h, :, :, :, tile(i)] = v.reshape(4, 4, 48, T)

                loop(3, body)
                scatter("z", "k1", lambda p: b["gk"].at[h, :, p], lambda r: b["rk1"].at[h, r], 4 * h)

        def kv_b(h):
            recv3("k1", lambda r: b["rk1"].at[h, r], 4 * h)

            def body(i):
                b["hk"][h, i] = add4(b["gk"][h, i, at["z"]], [b["rk1"][h, r, i] for r in range(3)]).astype(BF)

            loop(4, body)
            scatter("y", "k2", lambda p: b["hk"].at[h, p], lambda r: b["rk2"].at[h, r], 4 * h)

        def kv_c(h):
            recv3("k2", lambda r: b["rk2"].at[h, r], 4 * h)
            b["pad"][0:48, :] = add4(b["hk"][h, at["y"]], [b["rk2"][h, r] for r in range(3)])
            for j in range(4):
                b["fk"][h, j] = b["pad"][12 * j : 12 * j + 16, :].astype(BF)
            scatter("x", "k3", lambda p: b["fk"].at[h, p], lambda r: b["rk3"].at[h, r], 4 * h)

        def kv_d(h):
            recv3("k3", lambda r: b["rk3"].at[h, r], 4 * h)
            total = add4(b["fk"][h, at["x"]], [b["rk3"][h, r] for r in range(3)])
            okv[:, h * D : (h + 1) * D] = total[:12]

        def vec_send(a):
            for r in (1, 2, 3):
                _, to = peer("xyz"[a], r)
                send("v", 3 * a + r - 1, b["vec"], b["rvec"].at[a, r - 1], (sec, to))

        def vec_add(a):
            for r in (1, 2, 3):
                recv("v", 3 * a + r - 1, b["rvec"].at[a, r - 1])
            for copy in pending[-3:]:
                copy.wait_send()
            del pending[-3:]
            b["vec"][...] += b["rvec"][a, 0] + b["rvec"][a, 1] + b["rvec"][a, 2]

        def vec_out():
            shift = lax.rem(D - 12 * dp, D)
            rolled = pltpu.roll(b["vec"][...], shift, axis=1)
            for row, out in enumerate((og1, ob1, og2, ob2)):
                out[...] = rolled[row : row + 1, 0:12]
            bias_row = b["vec"][pl.ds(4 + at["y"], 1), :]
            shift = lax.rem(D - 48 * lax.rem(dp, 16), D)
            rolled = pltpu.roll(jnp.broadcast_to(bias_row, (8, D)), shift, axis=1)
            oub[...] = rolled[0:1, 0:48]

        if cross:
            for j in range(3):
                for m in range(4):
                    rows, at_cols = slice(m * T, (m + 1) * T), slice(j * T, (j + 1) * T)
                    b["ctxt"][at_cols, rows] = b["ctx"][rows, at_cols].T
            down_a()
            up_a()
            down_b()

        if cross:
            recv("back", 0, b["dyb"])
            b["dx"][...] = b["dyb"][...].astype(F32)
            gather_to("y", "y", lambda p: b["dyb"], rows_of(b["rxy"]), other)

        for k in range(4):

            def up_back(i):
                grad = mm_nt(b["dyb"][...], b["wd"][tile(3 * k + i), :])
                du = (b["gp"][k, :, tile(i)].astype(F32) * grad).astype(BF)
                b["hm"][k, :, tile(i)] = du
                b["vec"][4 + k : 5 + k, tile(i)] = jnp.sum(du.astype(F32), axis=0, keepdims=True)

            loop(3, up_back)
        gather_to("x", "u", lambda p: b["hm"].at[p], rows_of(b["rxd"]), other)

        def n2_back(i):
            grad = jnp.zeros((ROWS, T), F32)
            for k in range(4):
                grad = grad + mm_nt(b["hm"][k], b["wu"][tile(i), k * D : (k + 1) * D])
            b["dn"][:, tile(i)] = grad

        loop(3, n2_back)

        def done2(rows, value):
            b["dx"][rows, :] = value
            rounded = value.astype(BF)
            b["d4"][2, rows, :] = rounded[:, 0:384]
            b["d4"][3, rows, :] = rounded[:, 384:768]

        norm_back(b["xh2"], b["rs2"], g2, 2, done2)

        def out_back(i):
            rows = tile(i)
            grad = mm_nt(b["d4"][2], b["wo"][rows, 0:384]) + mm_nt(b["d4"][3], b["wo"][rows, 384:768])
            b["do"][:, tile(i)] = grad.astype(BF)

        loop(3, out_back)

        def attend_back(i):
            s, j, rows, krows, kcols, vcols = blocks(i)
            k2, v2 = b["kv"][krows, kcols], b["kv"][krows, vcols]
            q2 = stacked(b["q"][rows, kcols])
            probs = b["p"][i, :, 0:keys]
            grad = b["do"][rows, kcols].astype(F32)
            if cross:
                grad = grad * b["inv"][rows, kcols]
            along = grad * b["o"][rows, kcols].astype(F32)
            along = jnp.concatenate([jnp.where(first_head, along, 0.0), jnp.where(first_head, 0.0, along)], axis=0)
            along = jnp.sum(along, axis=-1, keepdims=True)
            do2 = stacked(grad.astype(BF))
            ds = (probs.astype(F32) * (mm_nt(do2, v2) - along)).astype(BF)
            half, at_cols = j // 3, tile(j % 3, 128)
            b["d4"][half, rows, at_cols] = (merged(mm(ds, k2)) * 0.125).astype(BF)
            if cross:
                b["dkvt"][tile(j, 128), krows] = mm_tn(q2, ds).astype(BF)
                b["dkvt"][vcols, krows] = mm_tn(do2, probs).astype(BF)
            else:
                b["ctx"][tile(2 * half + s, SEQ), at_cols] = mm_tn(ds, q2).astype(BF)
                b["ctx"][tile(4 + 2 * half + s, SEQ), at_cols] = mm_tn(probs, do2).astype(BF)

        loop(2 * PAIRS, attend_back)
        own_b = gather_to("z", "b", lambda p: b["d4"].at[p], rows_of(b["rxb"]), sec)
        if not cross:

            def kv_quarter(p):
                return b["ctx"].at[tile(p, ROWS), pl.ds(0, 384)]

            own_b2 = gather_to(
                "z", "b2", kv_quarter, lambda r: b["dkvt"].at[pl.ds(r * ROWS, ROWS), pl.ds(0, 384)], sec
            )

        def n1_back(i):
            rows = tile(i)
            grad = mm_nt(b["d4"][0], b["wq"][rows, 0:384]) + mm_nt(b["d4"][1], b["wq"][rows, 384:768])
            if not cross:
                for k in range(4):
                    quarter = b["ctx"][k * ROWS : (k + 1) * ROWS, 0:384]
                    grad = grad + mm_nt(quarter, b["wkv"][rows, 384 * k : 384 * (k + 1)])
            b["dn"][:, tile(i)] = grad

        loop(3, n1_back)

        def done1(rows, value):
            ins[rows, :] = value.astype(BF)

        norm_back(b["xh1"], b["rs1"], g1, 0, done1)
        if not cross:
            send("back", 0, ins, b["dyb"], (other, dp))

        if cross:
            kv_a()
            up_b()
            down_c()
            vec_send(0)
            vec_add(0)
            qo_a()
            up_c()
            vec_send(1)
            vec_add(1)
            kv_b(0)
            qo_b()
            kv_b(1)
            vec_send(2)
            vec_add(2)
            kv_c(0)
            qo_c()
            kv_c(1)
            vec_out()
            kv_d(0)
            kv_d(1)
            qo_d()
        else:
            qo_a()
            vec_send(0)
            vec_add(0)
            down_a()
            qo_b()
            vec_send(1)
            vec_add(1)
            up_a()
            qo_c()
            vec_send(2)
            vec_add(2)
            down_b()
            vec_out()
            qo_d()
            up_b()
            down_c()
            up_c()
        recv("d3", 0, b["rfd"])
        odn[...] = b["rfd"][...]
        for r in (1, 3, 2, 0):
            recv("u3", r, b["ru3"].at[0])
        for k in range(4):
            oup[:, k * D : (k + 1) * D] = b["ru3"][k].astype(F32)[:12]
        for copy in pending:
            copy.wait_send()

    pl.when(sec == 0)(lambda: branch(0))
    pl.when(sec == 1)(lambda: branch(1))


def on_device(
    tokens, context, out_cot, group_id, ctx_len, fut_len, loss_weight,
    norm_gain1, norm_bias1, w_query, w_keyval, w_out,
    norm_gain2, norm_bias2, w_up, up_bias, w_down,
):
    smem = pl.BlockSpec(memory_space=pltpu.SMEM)
    vmem = pl.BlockSpec(memory_space=pltpu.VMEM)
    hbm = pl.BlockSpec(memory_space=pl.ANY)
    shape = jax.ShapeDtypeStruct
    outs = pl.pallas_call(
        kernel,
        out_shape=(
            shape((ROWS, D), BF),
            shape((ROWS, D), BF),
            shape((1, 12), F32),
            shape((1, 12), F32),
            shape((12, D), F32),
            shape((12, 2 * D), F32),
            shape((12, D), F32),
            shape((1, 12), F32),
            shape((1, 12), F32),
            shape((12, FF), F32),
            shape((1, 48), F32),
            shape((48, D), F32),
        ),
        in_specs=[smem] * 3 + [vmem] + [hbm] * 3 + [vmem] * 5 + [hbm] * 5,
        out_specs=[vmem] * 12,
        scratch_shapes=[pltpu.VMEM(s, t) for s, t in BUFS.values()]
        + [pltpu.SemaphoreType.DMA((N_SEMS,)), pltpu.SemaphoreType.DMA((N_SEMS,))],
        compiler_params=pltpu.CompilerParams(
            collective_id=0, has_side_effects=True, vmem_limit_bytes=64 * 1024 * 1024 - 4096
        ),
    )(
        group_id, ctx_len, fut_len, loss_weight,
        tokens.reshape(ROWS, D), context.reshape(2 * CTX, D), out_cot.reshape(ROWS, D),
        norm_gain1, norm_bias1, norm_gain2, norm_bias2, up_bias,
        w_query[0], w_keyval[0], w_out[0], w_up[0], w_down[0],
    )
    acts, ins, gg1, gb1, gq, gkv, go, gg2, gb2, gup, gub, gdn = outs
    seqs = (1, 2, SEQ, D)
    return (
        acts.reshape(seqs), ins.reshape(seqs), gg1, gb1, gq[None], gkv[None], go[None],
        gg2, gb2, gup[None], gub, gdn[None],
    )


def solution(mesh):
    dp, sec = "dp", "section"
    vec, mat = P(sec, None), P(sec, None, None)
    return jax.shard_map(
        on_device,
        mesh=mesh,
        in_specs=(P(dp, None, None),) * 3 + (P(dp),) * 3 + (P(dp, None),)
        + (vec, vec, mat, mat, mat, vec, vec, mat, vec, mat),
        out_specs=(P(sec, dp, None, None),) * 2 + (P(sec, dp),) * 2 + (P(sec, dp, None),) * 3
        + (P(sec, dp),) * 2 + (P(sec, dp, None), P(sec, dp), P(sec, dp, None)),
        check_vma=False,
    )
```

```python
import math

import jax
import jax.numpy as jnp
from jax import lax
from jax.experimental import pallas as pl
from jax.experimental.pallas import tpu as pltpu
from jax.sharding import PartitionSpec as P

MESH = pl.DeviceIdType.MESH
BF = jnp.bfloat16
F32 = jnp.float32
GROUPS = 8
D = 768
FF = 3072
SEQ = 128
ROWS = 256
CTX = 512
PAIRS = 6
T = 256
GELU_C = math.sqrt(2.0 / math.pi)
GELU_A = 0.044715


def mm(a, b):
    return jnp.dot(a, b, preferred_element_type=F32)


def mm_nt(a, b):
    return lax.dot_general(a, b, (((1,), (1,)), ((), ())), preferred_element_type=F32)


def mm_tn(a, b):
    return lax.dot_general(a, b, (((0,), (0,)), ((), ())), preferred_element_type=F32)


def loop(n, body):
    for i in range(n):
        body(i)


def tile(i, size=T):
    if isinstance(i, int):
        return slice(i * size, (i + 1) * size)
    return pl.ds(pl.multiple_of(i * size, size), size)


BUFS = dict(
    wq=((D, D), BF),
    wkv=((D, 2 * D), BF),
    wo=((D, D), BF),
    wu=((D, FF), BF),
    wd=((FF, D), BF),
    xb=((ROWS, D), BF),
    ctx=((2 * CTX, D), BF),
    ctxt=((D, 2 * CTX), BF),
    n1=((ROWS, D), BF),
    q=((ROWS, D), BF),
    kv=((2 * CTX, 2 * D), BF),
    p=((2 * PAIRS, ROWS, CTX), BF),
    inv=((ROWS, D), F32),
    o=((ROWS, D), BF),
    s2t=((2, D, ROWS), BF),
    n2=((ROWS, D), BF),
    n2t=((D, ROWS), BF),
    x2=((ROWS, D), F32),
    xh1=((ROWS, D), F32),
    xh2=((ROWS, D), F32),
    rs1=((ROWS, 1), F32),
    rs2=((ROWS, 1), F32),
    gp=((4, ROWS, D), BF),
    hm=((4, ROWS, D), BF),
    hmt=((FF, ROWS), BF),
    dyb=((ROWS, D), BF),
    dx=((ROWS, D), F32),
    d4=((4, ROWS, 384), BF),
    dkvt=((2 * D, 2 * CTX), BF),
    vec=((8, D), F32),
    rvec=((3, 3, 8, D), F32),
    tot=((8, 128), F32),
    rtot=((3, 3, 8, 128), F32),
    rxh=((D, 4 * ROWS), BF),
    rxy=((4 * ROWS, D), BF),
    rxn=((D, 4 * ROWS), BF),
    rxd=((4 * ROWS, D), BF),
    gd=((4, 4, 48, D), BF),
    rd1=((3, 4, 48, D), BF),
    hd=((4, 48, D), BF),
    rd2=((3, 48, D), BF),
    rfd=((48, D), F32),
    gu=((4, 192, D), BF),
    ru1=((3, 192, D), BF),
    hu=((4, 48, D), BF),
    ru2=((3, 48, D), BF),
    fu=((4, 16, D), BF),
    ru3=((4, 16, D), BF),
    rxa=((D, 4 * ROWS), BF),
    rxb=((4 * ROWS, 384), BF),
    gq=((4, 192, D), BF),
    rq1=((3, 192, D), BF),
    hq=((4, 64, D), BF),
    rq2=((3, 64, D), BF),
    fq=((4, 16, D), BF),
    rq3=((4, 16, D), BF),
    gk=((2, 4, 4, 48, D), BF),
    rk1=((2, 3, 4, 48, D), BF),
    hk=((2, 4, 48, D), BF),
    rk2=((2, 3, 48, D), BF),
    fk=((2, 4, 16, D), BF),
    rk3=((2, 3, 16, D), BF),
)
KEYS = {}
for _name, _n in dict(
    tot=9, act=1, back=1, a=4, n=4, h=4, y=4, u=4, b=4, a2=4, b2=4,
    d1=4, d2=4, d3=1, u1=4, u2=4, u3=4, q1=4, q2=4, q3=4,
    k1=8, k2=8, k3=8, v=9, load=8,
).items():
    KEYS[_name] = sum(KEYS.values()) if not KEYS else _total
    _total = KEYS[_name] + _n
N_SEMS = _total
NAMES = list(BUFS)


def kernel(*refs):
    (gid, clen, flen, lw, tokens, ctx_in, cot_in, g1, b1, g2, b2, bu, wq_in, wkv_in, wo_in, wu_in, wd_in) = refs[:17]
    (acts, ins, og1, ob1, oq, okv, oo, og2, ob2, oup, oub, odn) = refs[17:29]
    b = dict(zip(NAMES, refs[29 : 29 + len(NAMES)]))
    b["do"] = b["n1"]
    b["dn"] = b["x2"]
    b["pad"] = b["x2"].at[pl.ds(0, 208)]
    b["fd"] = b["x2"].at[pl.ds(208, 48)]
    ssem, rsem = refs[29 + len(NAMES) :]

    sec = lax.axis_index("section")
    dp = lax.axis_index("dp")
    at = {"y": dp // 16, "z": (dp // 4) % 4, "x": dp % 4}
    step = {"y": 16, "z": 4, "x": 1}
    other = 1 - sec

    def peer(axis, r):
        p = lax.rem(at[axis] + r, 4)
        return p, dp + (p - at[axis]) * step[axis]

    barrier = pltpu.get_barrier_semaphore()
    pl.semaphore_signal(barrier, inc=1, device_id=(other, dp), device_id_type=MESH)
    for axis in "xyz":
        for r in (1, 2, 3):
            to = peer(axis, r)[1]
            for core in (sec, other):
                pl.semaphore_signal(barrier, inc=1, device_id=(core, to), device_id_type=MESH)

    def branch(mine):
        cross = mine == 0
        pending = []

        def send(key, i, src, dst, device):
            k = KEYS[key] + i
            copy = pltpu.make_async_remote_copy(
                src_ref=src, dst_ref=dst, send_sem=ssem.at[k], recv_sem=rsem.at[k],
                device_id=device, device_id_type=MESH,
            )
            copy.start()
            pending.append(copy)

        def recv(key, i, ref):
            k = KEYS[key] + i
            pltpu.make_async_remote_copy(
                src_ref=ref, dst_ref=ref, send_sem=ssem.at[k], recv_sem=rsem.at[k],
                device_id=(other, dp), device_id_type=MESH,
            ).wait_recv()

        def local(key, i, src, dst):
            copy = pltpu.make_async_copy(src, dst, rsem.at[KEYS[key] + i])
            copy.start()
            return copy

        loads = {}

        def load(name, i, src, dst):
            loads[name] = local("load", i, src, dst)

        if cross:
            load("x", 0, tokens, b["xb"])
            load("wq", 3, wq_in, b["wq"])
            load("ctx", 1, ctx_in, b["ctx"])
            load("wkv", 2, wkv_in, b["wkv"])
        else:
            load("cot", 0, cot_in, b["do"])
            load("wq", 3, wq_in, b["wq"])
            load("wkv", 2, wkv_in, b["wkv"])
        load("wo", 4, wo_in, b["wo"])
        load("wu", 5, wu_in, b["wu"])
        load("wd", 6, wd_in, b["wd"])

        lane = lax.broadcasted_iota(jnp.int32, (1, 128), 1)
        first_head = lane < 64
        mask_a = first_head.astype(F32).astype(BF)
        mask_b = 1.0 - mask_a

        def stacked(v):
            return jnp.concatenate([v * mask_a, v * mask_b], axis=0)

        def merged(v):
            return jnp.where(first_head, v[:SEQ], v[SEQ:])

        def norm(src, gain, bias, xh, rs, n, nt):
            def body(i):
                rows = tile(i, 32)
                v = src[rows, :].astype(F32)
                centre = v - jnp.mean(v, axis=-1, keepdims=True)
                spread = jnp.mean(centre * centre, axis=-1, keepdims=True)
                scale = lax.rsqrt(spread + 1e-05)
                hat = centre * scale
                xh[rows, :] = hat
                rs[rows, :] = scale
                n[rows, :] = (hat * gain[...] + bias[...]).astype(BF)

            loop(8, body)
            for j in range(3):
                nt[j * T : (j + 1) * T, :] = n[:, j * T : (j + 1) * T].T

        def norm_back(xh, rs, gain, row, done):
            def body(i, carry):
                sum_g, sum_b = carry
                rows = tile(i, 32)
                grad = b["dn"][rows, :]
                hat = xh[rows, :]
                sum_g = sum_g + (grad * hat).reshape(4, 8, D).sum(0)
                sum_b = sum_b + grad.reshape(4, 8, D).sum(0)
                scaled = grad * gain[...]
                mean = jnp.mean(scaled, axis=-1, keepdims=True)
                along = jnp.mean(scaled * hat, axis=-1, keepdims=True)
                done(rows, b["dx"][rows, :] + rs[rows, :] * (scaled - mean - hat * along))
                return sum_g, sum_b

            sums = (jnp.zeros((8, D), F32),) * 2
            for i in range(8):
                sums = body(i, sums)
            sum_g, sum_b = sums
            b["vec"][row : row + 1, :] = sum_g.sum(0, keepdims=True)
            b["vec"][row + 1 : row + 2, :] = sum_b.sum(0, keepdims=True)

        def gather_to(axis, key, src_of, dst_of, core):
            for r in (1, 3, 2):
                p, to = peer(axis, r)
                send(key, r, src_of(p), dst_of(r), (core, to))
            if core is other:
                send(key, 0, src_of(at[axis]), dst_of(0), (core, dp))
                return None
            return local(key, 0, src_of(at[axis]), dst_of(0))

        def cols(ref):
            return lambda r: ref.at[:, pl.ds(r * ROWS, ROWS)]

        def rows_of(ref):
            return lambda r: ref.at[pl.ds(r * ROWS, ROWS)]

        def scatter(axis, key, src_of, dst_of, base=0, core=sec):
            for r in (1, 3, 2):
                p, to = peer(axis, r)
                send(key, base + r, src_of(p), dst_of(r - 1), (core, to))

        def recv3(key, dst_of, base=0):
            for r in (1, 3, 2):
                recv(key, base + r, dst_of(r - 1))

        if not cross:
            weighted, ids = [], []
            total = jnp.zeros((1, 128), F32)
            for s in range(2):
                w = jnp.where(lane < flen[s], lw[s : s + 1, :].astype(F32), 0.0)
                total = total + jnp.where(lane == gid[s], jnp.sum(w, axis=1, keepdims=True), 0.0)
                weighted.append(w)
            b["tot"][...] = jnp.broadcast_to(total, (8, 128))
        pl.semaphore_wait(barrier, 19)
        if not cross:
            for a, axis in enumerate("xyz"):
                for r in (1, 2, 3):
                    _, to = peer(axis, r)
                    send("tot", 3 * a + r - 1, b["tot"], b["rtot"].at[a, r - 1], (sec, to))
                for r in (1, 2, 3):
                    recv("tot", 3 * a + r - 1, b["rtot"].at[a, r - 1])
                for copy in pending:
                    copy.wait_send()
                pending.clear()
                b["tot"][...] += b["rtot"][a, 0] + b["rtot"][a, 1] + b["rtot"][a, 2]
            totals = b["tot"][0:1, :]
            every = jnp.sum(totals, axis=1, keepdims=True)
            factors = every / (GROUPS * jnp.maximum(totals, 1.0))
            loads["cot"].wait()
            diagonal = lax.broadcasted_iota(jnp.int32, (SEQ, SEQ), 0) == lax.broadcasted_iota(
                jnp.int32, (SEQ, SEQ), 1
            )
            for s in range(2):
                factor = jnp.sum(jnp.where(lane == gid[s], factors, 0.0), axis=1, keepdims=True)
                picked = jnp.where(diagonal, weighted[s], 0.0).astype(BF)
                rows = slice(s * SEQ, (s + 1) * SEQ)
                grad = mm(picked, b["do"][rows, :]) * factor
                b["dx"][rows, :] = grad
                b["dyb"][rows, :] = grad.astype(BF)
            gather_to("y", "y", lambda p: b["dyb"], rows_of(b["rxy"]), other)

        if cross:
            loads["x"].wait()
        else:
            recv("act", 0, b["xb"])
        norm(b["xb"], g1, b1, b["xh1"], b["rs1"], b["n1"], b["s2t"].at[0])

        loads["wq"].wait()

        def query(i):
            b["q"][:, tile(i)] = (mm(b["n1"][...], b["wq"][:, tile(i)]).astype(BF) * 0.125).astype(BF)

        loop(3, query)

        loads["wkv"].wait()
        if cross:
            loads["ctx"].wait()

            def keyval(i):
                for m in range(4):
                    rows = slice(m * T, (m + 1) * T)
                    b["kv"][rows, tile(i)] = mm(b["ctx"][rows, :], b["wkv"][:, tile(i)]).astype(BF)
        else:

            def keyval(i):
                b["kv"][0:ROWS, tile(i)] = mm(b["n1"][...], b["wkv"][:, tile(i)]).astype(BF)

        loop(6, keyval)
        keys = CTX if cross else SEQ

        def blocks(i):
            s, j = i // PAIRS, i % PAIRS
            vcols = slice(D + 128 * j, D + 128 * (j + 1))
            return s, j, tile(s, SEQ), tile(s, keys), tile(j, 128), vcols

        if cross:
            key = lax.broadcasted_iota(jnp.int32, (1, keys), 1)
            masks = [jnp.where(key < clen[s], 0.0, -1e9) for s in range(2)]
        else:
            row = lax.broadcasted_iota(jnp.int32, (SEQ, keys), 0)
            mask = jnp.where(lax.broadcasted_iota(jnp.int32, (SEQ, keys), 1) <= row, 0.0, -1e9)
            masks = [jnp.concatenate([mask, mask], axis=0)] * 2
        ones = jnp.ones((keys, 128), BF)

        def attend(i):
            s, j, rows, krows, kcols, vcols = blocks(i)
            scores = mm_nt(stacked(b["q"][rows, kcols]), b["kv"][krows, kcols]) + masks[s]
            e = jnp.exp(scores - jnp.max(scores, axis=-1, keepdims=True))
            values = b["kv"][krows, vcols]
            if cross:
                e = e.astype(BF)
                b["p"][i] = e
                mixed = mm(e, jnp.concatenate([values, ones], axis=1))
                scale = 1.0 / merged(mixed[:, 128:])
                b["inv"][rows, kcols] = scale
                b["o"][rows, kcols] = (merged(mixed[:, :128]) * scale).astype(BF)
            else:
                probs = (e / jnp.sum(e, axis=-1, keepdims=True)).astype(BF)
                b["p"][i, :, 0:keys] = probs
                b["o"][rows, kcols] = merged(mm(probs, values)).astype(BF)

        loop(2 * PAIRS, attend)
        for j in range(3):
            b["s2t"][1, j * T : (j + 1) * T, :] = b["o"][:, j * T : (j + 1) * T].T
        if cross:
            own_a = gather_to("z", "a", lambda p: b["s2t"].at[p // 2], cols(b["rxa"]), sec)
        else:
            own_a = gather_to("z", "a", lambda p: b["s2t"].at[p // 2], cols(b["rxa"]), sec)
            own_a2 = gather_to("z", "a2", lambda p: b["s2t"].at[0], cols(b["ctxt"]), sec)

        loads["wo"].wait()

        def project(i):
            b["x2"][:, tile(i)] = b["xb"][:, tile(i)].astype(F32) + mm(b["o"][...], b["wo"][:, tile(i)])

        loop(3, project)
        norm(b["x2"], g2, b2, b["xh2"], b["rs2"], b["n2"], b["n2t"])
        gather_to("x", "n", lambda p: b["n2t"], cols(b["rxn"]), other)

        loads["wu"].wait()

        def up(i):
            u = mm(b["n2"][...], b["wu"][:, tile(i)]) + bu[:, tile(i)]
            square = u * u
            th = jnp.tanh(GELU_C * u * (1.0 + GELU_A * square))
            half = 0.5 * (1.0 + th)
            hidden = (u * half).astype(BF)
            slope = half + 0.5 * u * (1.0 - th * th) * (GELU_C * (1.0 + 3.0 * GELU_A * square))
            k, at_cols = i // 3, tile(i % 3)
            b["hm"][k, :, at_cols] = hidden
            b["gp"][k, :, at_cols] = slope.astype(BF)
            b["hmt"][tile(i), :] = hidden.T

        loop(12, up)
        gather_to("y", "h", lambda p: b["hmt"].at[tile(p, D)], cols(b["rxh"]), other)

        loads["wd"].wait()

        def down(i):
            y = b["x2"][:, tile(i)]
            for k in range(4):
                y = y + mm(b["hm"][k], b["wd"][k * D : (k + 1) * D, tile(i)])
            acts[:, tile(i)] = y.astype(BF)

        loop(3, down)
        if cross:
            send("act", 0, acts, b["xb"], (other, dp))

        def add4(own, parts):
            total = own.astype(F32)
            for part in parts:
                total = total + part.astype(F32)
            return total

        def down_a():
            for r in range(4):
                recv("h", r, cols(b["rxh"])(r))
                recv("y", r, rows_of(b["rxy"])(r))

            def body(i):
                v = mm(b["rxh"][...], b["rxy"][:, tile(i)]).astype(BF)
                b["gd"][:, :, :, tile(i)] = v.reshape(4, 4, 48, T)

            loop(3, body)
            scatter("x", "d1", lambda p: b["gd"].at[:, p], lambda r: b["rd1"].at[r])

        def down_b():
            recv3("d1", lambda r: b["rd1"].at[r])

            def body(i):
                b["hd"][i] = add4(b["gd"][i, at["x"]], [b["rd1"][r, i] for r in range(3)]).astype(BF)

            loop(4, body)
            scatter("z", "d2", lambda p: b["hd"].at[p], lambda r: b["rd2"].at[r])

        def down_c():
            recv3("d2", lambda r: b["rd2"].at[r])
            b["fd"][...] = add4(b["hd"][at["z"]], [b["rd2"][r] for r in range(3)])
            send("d3", 0, b["fd"], b["rfd"], (other, dp))

        def up_a():
            for r in range(4):
                recv("n", r, cols(b["rxn"])(r))
                recv("u", r, rows_of(b["rxd"])(r))

            def body(i):
                v = mm(b["rxn"][...], b["rxd"][:, tile(i)]).astype(BF)
                b["gu"][:, :, tile(i)] = v.reshape(4, 192, T)

            loop(3, body)
            scatter("y", "u1", lambda p: b["gu"].at[p], lambda r: b["ru1"].at[r])

        def up_b():
            recv3("u1", lambda r: b["ru1"].at[r])

            def body(i):
                rows = tile(i, 48)
                b["hu"][i] = add4(b["gu"][at["y"], rows], [b["ru1"][r, rows] for r in range(3)]).astype(BF)

            loop(4, body)
            scatter("z", "u2", lambda p: b["hu"].at[p], lambda r: b["ru2"].at[r])

        def up_c():
            recv3("u2", lambda r: b["ru2"].at[r])
            b["pad"][0:48, :] = add4(b["hu"][at["z"]], [b["ru2"][r] for r in range(3)])
            for j in range(4):
                b["fu"][j] = b["pad"][12 * j : 12 * j + 16, :].astype(BF)
            for r in (1, 3, 2, 0):
                p, to = peer("x", r)
                send("u3", r, b["fu"].at[p], b["ru3"].at[at["x"]], (other, to))

        width = 384 if cross else D

        def part(ref, *index):
            return ref.at[index + (slice(None), pl.ds(0, width))]

        def qo_a():
            own_a.wait()
            own_b.wait()
            for r in range(1, 4):
                recv("a", r, cols(b["rxa"])(r))
                recv("b", r, rows_of(b["rxb"])(r))
            if not cross:
                own_a2.wait()
                own_b2.wait()
                for r in range(1, 4):
                    recv("a2", r, cols(b["ctxt"])(r))
                    recv("b2", r, b["dkvt"].at[pl.ds(r * ROWS, ROWS), pl.ds(0, 384)])

            def body(i):
                rows = tile(i, 192)
                b["gq"][i, :, 0:384] = mm(b["rxa"][rows, :], b["rxb"][...]).astype(BF)
                if not cross:
                    b["gq"][i, :, 384:768] = mm(b["ctxt"][rows, :], b["dkvt"][0:1024, 0:384]).astype(BF)

            loop(4, body)
            scatter("y", "q1", lambda p: part(b["gq"], p), lambda r: part(b["rq1"], r))

        def qo_b():
            recv3("q1", lambda r: part(b["rq1"], r))

            def body(i):
                rows = tile(i, 48)
                b["pad"][rows, 0:width] = add4(
                    b["gq"][at["y"], rows, 0:width], [b["rq1"][r, rows, 0:width] for r in range(3)]
                )

            loop(4, body)
            for j in range(4):
                for k in range(4):
                    start = 48 * k + 12 * j
                    b["hq"][j, 16 * k : 16 * k + 16, 0:width] = b["pad"][start : start + 16, 0:width].astype(BF)
            scatter("x", "q2", lambda p: part(b["hq"], p), lambda r: part(b["rq2"], r))

        def qo_c():
            recv3("q2", lambda r: part(b["rq2"], r))
            total = add4(b["hq"][at["x"], :, 0:width], [b["rq2"][r, :, 0:width] for r in range(3)])
            b["fq"][:, :, 0:width] = total.astype(BF).reshape(4, 16, width)
            for r in (1, 3, 2):
                p, to = peer("z", r)
                send("q3", r, part(b["fq"], p), part(b["rq3"], at["z"]), (sec, to))
            b["rq3"][at["z"], :, 0:width] = b["fq"][at["z"], :, 0:width]

        def qo_d():
            for r in (1, 3, 2):
                recv("q3", r, part(b["rq3"], 0))
            for k in range(2):
                at_cols = slice(384 * k, 384 * (k + 1))
                oq[:, at_cols] = b["rq3"][k, :, 0:384].astype(F32)[:12]
                oo[:, at_cols] = b["rq3"][2 + k, :, 0:384].astype(F32)[:12]
            if not cross:
                for k in range(4):
                    okv[:, 384 * k : 384 * (k + 1)] = b["rq3"][k, :, 384:768].astype(F32)[:12]

        def kv_a():
            for h in range(2):

                def body(i):
                    v = mm_nt(b["ctxt"][...], b["dkvt"][tile(3 * h + i), :]).astype(BF)
                    b["gk"][h, :, :, :, tile(i)] = v.reshape(4, 4, 48, T)

                loop(3, body)
                scatter("z", "k1", lambda p: b["gk"].at[h, :, p], lambda r: b["rk1"].at[h, r], 4 * h)

        def kv_b(h):
            recv3("k1", lambda r: b["rk1"].at[h, r], 4 * h)

            def body(i):
                b["hk"][h, i] = add4(b["gk"][h, i, at["z"]], [b["rk1"][h, r, i] for r in range(3)]).astype(BF)

            loop(4, body)
            scatter("y", "k2", lambda p: b["hk"].at[h, p], lambda r: b["rk2"].at[h, r], 4 * h)

        def kv_c(h):
            recv3("k2", lambda r: b["rk2"].at[h, r], 4 * h)
            b["pad"][0:48, :] = add4(b["hk"][h, at["y"]], [b["rk2"][h, r] for r in range(3)])
            for j in range(4):
                b["fk"][h, j] = b["pad"][12 * j : 12 * j + 16, :].astype(BF)
            scatter("x", "k3", lambda p: b["fk"].at[h, p], lambda r: b["rk3"].at[h, r], 4 * h)

        def kv_d(h):
            recv3("k3", lambda r: b["rk3"].at[h, r], 4 * h)
            total = add4(b["fk"][h, at["x"]], [b["rk3"][h, r] for r in range(3)])
            okv[:, h * D : (h + 1) * D] = total[:12]

        def vec_send(a):
            for r in (1, 2, 3):
                _, to = peer("xyz"[a], r)
                send("v", 3 * a + r - 1, b["vec"], b["rvec"].at[a, r - 1], (sec, to))

        def vec_add(a):
            for r in (1, 2, 3):
                recv("v", 3 * a + r - 1, b["rvec"].at[a, r - 1])
            for copy in pending[-3:]:
                copy.wait_send()
            del pending[-3:]
            b["vec"][...] += b["rvec"][a, 0] + b["rvec"][a, 1] + b["rvec"][a, 2]

        def vec_out():
            shift = lax.rem(D - 12 * dp, D)
            rolled = pltpu.roll(b["vec"][...], shift, axis=1)
            for row, out in enumerate((og1, ob1, og2, ob2)):
                out[...] = rolled[row : row + 1, 0:12]
            bias_row = b["vec"][pl.ds(4 + at["y"], 1), :]
            shift = lax.rem(D - 48 * lax.rem(dp, 16), D)
            rolled = pltpu.roll(jnp.broadcast_to(bias_row, (8, D)), shift, axis=1)
            oub[...] = rolled[0:1, 0:48]

        if cross:
            for j in range(3):
                for m in range(4):
                    rows, at_cols = slice(m * T, (m + 1) * T), slice(j * T, (j + 1) * T)
                    b["ctxt"][at_cols, rows] = b["ctx"][rows, at_cols].T
            down_a()

        if cross:
            recv("back", 0, b["dyb"])
            b["dx"][...] = b["dyb"][...].astype(F32)
            gather_to("y", "y", lambda p: b["dyb"], rows_of(b["rxy"]), other)

        for k in range(4):

            def up_back(i):
                grad = mm_nt(b["dyb"][...], b["wd"][tile(3 * k + i), :])
                du = (b["gp"][k, :, tile(i)].astype(F32) * grad).astype(BF)
                b["hm"][k, :, tile(i)] = du
                b["vec"][4 + k : 5 + k, tile(i)] = jnp.sum(du.astype(F32), axis=0, keepdims=True)

            loop(3, up_back)
        gather_to("x", "u", lambda p: b["hm"].at[p], rows_of(b["rxd"]), other)

        if cross:
            up_a()

        def n2_back(i):
            grad = jnp.zeros((ROWS, T), F32)
            for k in range(4):
                grad = grad + mm_nt(b["hm"][k], b["wu"][tile(i), k * D : (k + 1) * D])
            b["dn"][:, tile(i)] = grad

        loop(3, n2_back)

        def done2(rows, value):
            b["dx"][rows, :] = value
            rounded = value.astype(BF)
            b["d4"][2, rows, :] = rounded[:, 0:384]
            b["d4"][3, rows, :] = rounded[:, 384:768]

        norm_back(b["xh2"], b["rs2"], g2, 2, done2)

        def out_back(i):
            rows = tile(i)
            grad = mm_nt(b["d4"][2], b["wo"][rows, 0:384]) + mm_nt(b["d4"][3], b["wo"][rows, 384:768])
            b["do"][:, tile(i)] = grad.astype(BF)

        loop(3, out_back)

        def attend_back(i):
            s, j, rows, krows, kcols, vcols = blocks(i)
            k2, v2 = b["kv"][krows, kcols], b["kv"][krows, vcols]
            q2 = stacked(b["q"][rows, kcols])
            probs = b["p"][i, :, 0:keys]
            grad = b["do"][rows, kcols].astype(F32)
            if cross:
                grad = grad * b["inv"][rows, kcols]
            along = grad * b["o"][rows, kcols].astype(F32)
            along = jnp.concatenate([jnp.where(first_head, along, 0.0), jnp.where(first_head, 0.0, along)], axis=0)
            along = jnp.sum(along, axis=-1, keepdims=True)
            do2 = stacked(grad.astype(BF))
            ds = (probs.astype(F32) * (mm_nt(do2, v2) - along)).astype(BF)
            half, at_cols = j // 3, tile(j % 3, 128)
            b["d4"][half, rows, at_cols] = (merged(mm(ds, k2)) * 0.125).astype(BF)
            if cross:
                b["dkvt"][tile(j, 128), krows] = mm_tn(q2, ds).astype(BF)
                b["dkvt"][vcols, krows] = mm_tn(do2, probs).astype(BF)
            else:
                b["ctx"][tile(2 * half + s, SEQ), at_cols] = mm_tn(ds, q2).astype(BF)
                b["ctx"][tile(4 + 2 * half + s, SEQ), at_cols] = mm_tn(probs, do2).astype(BF)

        loop(2 * PAIRS, attend_back)
        own_b = gather_to("z", "b", lambda p: b["d4"].at[p], rows_of(b["rxb"]), sec)
        if not cross:

            def kv_quarter(p):
                return b["ctx"].at[tile(p, ROWS), pl.ds(0, 384)]

            own_b2 = gather_to(
                "z", "b2", kv_quarter, lambda r: b["dkvt"].at[pl.ds(r * ROWS, ROWS), pl.ds(0, 384)], sec
            )

        def n1_back(i):
            rows = tile(i)
            grad = mm_nt(b["d4"][0], b["wq"][rows, 0:384]) + mm_nt(b["d4"][1], b["wq"][rows, 384:768])
            if not cross:
                for k in range(4):
                    quarter = b["ctx"][k * ROWS : (k + 1) * ROWS, 0:384]
                    grad = grad + mm_nt(quarter, b["wkv"][rows, 384 * k : 384 * (k + 1)])
            b["dn"][:, tile(i)] = grad

        loop(3, n1_back)

        def done1(rows, value):
            ins[rows, :] = value.astype(BF)

        norm_back(b["xh1"], b["rs1"], g1, 0, done1)
        if not cross:
            send("back", 0, ins, b["dyb"], (other, dp))

        if cross:
            kv_a()
            down_b()
            up_b()
            down_c()
            vec_send(0)
            vec_add(0)
            qo_a()
            up_c()
            vec_send(1)
            vec_add(1)
            kv_b(0)
            qo_b()
            kv_b(1)
            vec_send(2)
            vec_add(2)
            kv_c(0)
            qo_c()
            kv_c(1)
            vec_out()
            kv_d(0)
            kv_d(1)
            qo_d()
        else:
            qo_a()
            vec_send(0)
            vec_add(0)
            down_a()
            qo_b()
            vec_send(1)
            vec_add(1)
            up_a()
            qo_c()
            vec_send(2)
            vec_add(2)
            down_b()
            vec_out()
            qo_d()
            up_b()
            down_c()
            up_c()
        recv("d3", 0, b["rfd"])
        odn[...] = b["rfd"][...]
        for r in (1, 3, 2, 0):
            recv("u3", r, b["ru3"].at[0])
        for k in range(4):
            oup[:, k * D : (k + 1) * D] = b["ru3"][k].astype(F32)[:12]
        for copy in pending:
            copy.wait_send()

    pl.when(sec == 0)(lambda: branch(0))
    pl.when(sec == 1)(lambda: branch(1))


def deliver(*refs):
    given, outs, sems = refs[:12], refs[12:24], refs[24]
    copies = [pltpu.make_async_copy(given[i], outs[i], sems.at[i]) for i in range(2)]
    for copy in copies:
        copy.start()
    for a, out in zip(given[2:], outs[2:]):
        out[...] = a[...].reshape(out.shape)
    for copy in copies:
        copy.wait()


def on_device(
    tokens, context, out_cot, group_id, ctx_len, fut_len, loss_weight,
    norm_gain1, norm_bias1, w_query, w_keyval, w_out,
    norm_gain2, norm_bias2, w_up, up_bias, w_down,
):
    smem = pl.BlockSpec(memory_space=pltpu.SMEM)
    vmem = pl.BlockSpec(memory_space=pltpu.VMEM)
    hbm = pl.BlockSpec(memory_space=pl.ANY)
    shape = jax.ShapeDtypeStruct
    outs = pl.pallas_call(
        kernel,
        out_shape=(
            shape((ROWS, D), BF),
            shape((ROWS, D), BF),
            shape((1, 12), F32),
            shape((1, 12), F32),
            shape((12, D), F32),
            shape((12, 2 * D), F32),
            shape((12, D), F32),
            shape((1, 12), F32),
            shape((1, 12), F32),
            shape((12, FF), F32),
            shape((1, 48), F32),
            shape((48, D), F32),
        ),
        in_specs=[smem] * 3 + [vmem] + [hbm] * 3 + [vmem] * 5 + [hbm] * 5,
        out_specs=[vmem] * 12,
        scratch_shapes=[pltpu.VMEM(s, t) for s, t in BUFS.values()]
        + [pltpu.SemaphoreType.DMA((N_SEMS,)), pltpu.SemaphoreType.DMA((N_SEMS,))],
        compiler_params=pltpu.CompilerParams(
            collective_id=0, has_side_effects=True, vmem_limit_bytes=64 * 1024 * 1024 - 4096
        ),
    )(
        group_id, ctx_len, fut_len, loss_weight,
        tokens.reshape(ROWS, D), context.reshape(2 * CTX, D), out_cot.reshape(ROWS, D),
        norm_gain1, norm_bias1, norm_gain2, norm_bias2, up_bias,
        w_query[0], w_keyval[0], w_out[0], w_up[0], w_down[0],
    )
    outs = pl.pallas_call(
        deliver,
        out_shape=[
            shape((a.shape[0], 1, a.shape[1]) if a.shape[0] == 12 else a.shape, a.dtype) for a in outs
        ],
        in_specs=[hbm] * 2 + [vmem] * 10,
        out_specs=[hbm] * 2 + [vmem] * 10,
        scratch_shapes=[pltpu.SemaphoreType.DMA((2,))],
    )(*outs)
    acts, ins, gg1, gb1, gq, gkv, go, gg2, gb2, gup, gub, gdn = outs
    seqs = (1, 2, SEQ, D)
    rows = [g.reshape(1, 12, g.shape[-1]) for g in (gq, gkv, go, gup)]
    return (
        acts.reshape(seqs), ins.reshape(seqs), gg1, gb1, *rows[:3],
        gg2, gb2, rows[3], gub, gdn[None],
    )


def solution(mesh):
    dp, sec = "dp", "section"
    vec, mat = P(sec, None), P(sec, None, None)
    return jax.shard_map(
        on_device,
        mesh=mesh,
        in_specs=(P(dp, None, None),) * 3 + (P(dp),) * 3 + (P(dp, None),)
        + (vec, vec, mat, mat, mat, vec, vec, mat, vec, mat),
        out_specs=(P(sec, dp, None, None),) * 2 + (P(sec, dp),) * 2 + (P(sec, dp, None),) * 3
        + (P(sec, dp),) * 2 + (P(sec, dp, None), P(sec, dp), P(sec, dp, None)),
        check_vma=False,
    )
```

```python
import math

import jax
import jax.numpy as jnp
from jax import lax
from jax.experimental import pallas as pl
from jax.experimental.pallas import tpu as pltpu
from jax.sharding import PartitionSpec as P

MESH = pl.DeviceIdType.MESH
BF = jnp.bfloat16
F32 = jnp.float32
GROUPS = 8
D = 768
FF = 3072
SEQ = 128
ROWS = 256
CTX = 512
PAIRS = 6
T = 256
GELU_C = math.sqrt(2.0 / math.pi)
GELU_A = 0.044715


def mm(a, b):
    return jnp.dot(a, b, preferred_element_type=F32)


def mm_nt(a, b):
    return lax.dot_general(a, b, (((1,), (1,)), ((), ())), preferred_element_type=F32)


def mm_tn(a, b):
    return lax.dot_general(a, b, (((0,), (0,)), ((), ())), preferred_element_type=F32)


def loop(n, body):
    for i in range(n):
        body(i)


def tile(i, size=T):
    if isinstance(i, int):
        return slice(i * size, (i + 1) * size)
    return pl.ds(pl.multiple_of(i * size, size), size)


BUFS = dict(
    wq=((D, D), BF),
    wkv=((D, 2 * D), BF),
    wo=((D, D), BF),
    wu=((D, FF), BF),
    wd=((FF, D), BF),
    xb=((ROWS, D), BF),
    ctx=((2 * CTX, D), BF),
    ctxt=((D, 2 * CTX), BF),
    n1=((ROWS, D), BF),
    q=((ROWS, D), BF),
    kv=((2 * CTX, 2 * D), BF),
    p=((2 * PAIRS, ROWS, CTX), BF),
    inv=((ROWS, D), F32),
    o=((ROWS, D), BF),
    s2t=((2, D, ROWS), BF),
    n2=((ROWS, D), BF),
    n2t=((D, ROWS), BF),
    x2=((ROWS, D), F32),
    xh1=((ROWS, D), F32),
    xh2=((ROWS, D), F32),
    rs1=((ROWS, 1), F32),
    rs2=((ROWS, 1), F32),
    gp=((4, ROWS, D), BF),
    hm=((4, ROWS, D), BF),
    hmt=((FF, ROWS), BF),
    dyb=((ROWS, D), BF),
    dx=((ROWS, D), F32),
    d4=((4, ROWS, 384), BF),
    dkvt=((2 * D, 2 * CTX), BF),
    vec=((8, D), F32),
    rvec=((3, 3, 8, D), F32),
    tot=((8, 128), F32),
    rtot=((3, 3, 8, 128), F32),
    rxh=((D, 4 * ROWS), BF),
    rxy=((4 * ROWS, D), BF),
    rxn=((D, 4 * ROWS), BF),
    rxd=((4 * ROWS, D), BF),
    gd=((4, 4, 48, D), BF),
    rd1=((3, 4, 48, D), BF),
    hd=((4, 48, D), BF),
    rd2=((3, 48, D), BF),
    rfd=((48, D), F32),
    gu=((4, 192, D), BF),
    ru1=((3, 192, D), BF),
    hu=((4, 48, D), BF),
    ru2=((3, 48, D), BF),
    fu=((4, 16, D), BF),
    ru3=((4, 16, D), BF),
    rxa=((D, 4 * ROWS), BF),
    rxb=((4 * ROWS, 384), BF),
    gq=((4, 192, D), BF),
    rq1=((3, 192, D), BF),
    hq=((4, 64, D), BF),
    rq2=((3, 64, D), BF),
    fq=((4, 16, D), BF),
    rq3=((4, 16, D), BF),
    gk=((2, 4, 4, 48, D), BF),
    rk1=((2, 3, 4, 48, D), BF),
    hk=((2, 4, 48, D), BF),
    rk2=((2, 3, 48, D), BF),
    fk=((2, 4, 16, D), BF),
    rk3=((2, 3, 16, D), BF),
)
KEYS = {}
for _name, _n in dict(
    tot=9, act=1, back=1, a=4, n=4, h=4, y=4, u=4, b=4, a2=4, b2=4,
    d1=4, d2=4, d3=1, u1=4, u2=4, u3=4, q1=4, q2=4, q3=4,
    k1=8, k2=8, k3=8, v=9, load=8,
).items():
    KEYS[_name] = sum(KEYS.values()) if not KEYS else _total
    _total = KEYS[_name] + _n
N_SEMS = _total
NAMES = list(BUFS)


def kernel(*refs):
    (gid, clen, flen, lw, tokens, ctx_in, cot_in, g1, b1, g2, b2, bu, wq_in, wkv_in, wo_in, wu_in, wd_in) = refs[:17]
    (acts, ins, og1, ob1, oq, okv, oo, og2, ob2, oup, oub, odn) = refs[17:29]
    b = dict(zip(NAMES, refs[29 : 29 + len(NAMES)]))
    b["do"] = b["n1"]
    b["dn"] = b["x2"]
    b["pad"] = b["x2"].at[pl.ds(0, 208)]
    b["fd"] = b["x2"].at[pl.ds(208, 48)]
    ssem, rsem = refs[29 + len(NAMES) :]

    sec = lax.axis_index("section")
    dp = lax.axis_index("dp")
    at = {"y": dp // 16, "z": (dp // 4) % 4, "x": dp % 4}
    step = {"y": 16, "z": 4, "x": 1}
    other = 1 - sec

    def peer(axis, r):
        p = lax.rem(at[axis] + r, 4)
        return p, dp + (p - at[axis]) * step[axis]

    barrier = pltpu.get_barrier_semaphore()
    pl.semaphore_signal(barrier, inc=1, device_id=(other, dp), device_id_type=MESH)
    for axis in "xyz":
        for r in (1, 2, 3):
            to = peer(axis, r)[1]
            for core in (sec, other):
                pl.semaphore_signal(barrier, inc=1, device_id=(core, to), device_id_type=MESH)

    def branch(mine):
        cross = mine == 0
        pending = []

        def send(key, i, src, dst, device):
            k = KEYS[key] + i
            copy = pltpu.make_async_remote_copy(
                src_ref=src, dst_ref=dst, send_sem=ssem.at[k], recv_sem=rsem.at[k],
                device_id=device, device_id_type=MESH,
            )
            copy.start()
            pending.append(copy)

        def recv(key, i, ref):
            k = KEYS[key] + i
            pltpu.make_async_remote_copy(
                src_ref=ref, dst_ref=ref, send_sem=ssem.at[k], recv_sem=rsem.at[k],
                device_id=(other, dp), device_id_type=MESH,
            ).wait_recv()

        def local(key, i, src, dst):
            copy = pltpu.make_async_copy(src, dst, rsem.at[KEYS[key] + i])
            copy.start()
            return copy

        loads = {}

        def load(name, i, src, dst):
            loads[name] = local("load", i, src, dst)

        if cross:
            load("x", 0, tokens, b["xb"])
            load("wq", 3, wq_in, b["wq"])
            load("ctx", 1, ctx_in, b["ctx"])
            load("wkv", 2, wkv_in, b["wkv"])
        else:
            load("cot", 0, cot_in, b["do"])
            load("wq", 3, wq_in, b["wq"])
            load("wkv", 2, wkv_in, b["wkv"])
        load("wo", 4, wo_in, b["wo"])
        load("wu", 5, wu_in, b["wu"])
        load("wd", 6, wd_in, b["wd"])

        lane = lax.broadcasted_iota(jnp.int32, (1, 128), 1)
        first_head = lane < 64
        mask_a = first_head.astype(F32).astype(BF)
        mask_b = 1.0 - mask_a

        def stacked(v):
            return jnp.concatenate([v * mask_a, v * mask_b], axis=0)

        def merged(v):
            return jnp.where(first_head, v[:SEQ], v[SEQ:])

        def norm(src, gain, bias, xh, rs, n, nt):
            def body(i):
                rows = tile(i, 32)
                v = src[rows, :].astype(F32)
                centre = v - jnp.mean(v, axis=-1, keepdims=True)
                spread = jnp.mean(centre * centre, axis=-1, keepdims=True)
                scale = lax.rsqrt(spread + 1e-05)
                hat = centre * scale
                xh[rows, :] = hat
                rs[rows, :] = scale
                n[rows, :] = (hat * gain[...] + bias[...]).astype(BF)

            loop(8, body)
            for j in range(3):
                nt[j * T : (j + 1) * T, :] = n[:, j * T : (j + 1) * T].T

        def norm_back(xh, rs, gain, row, done):
            def body(i, carry):
                sum_g, sum_b = carry
                rows = tile(i, 32)
                grad = b["dn"][rows, :]
                hat = xh[rows, :]
                sum_g = sum_g + (grad * hat).reshape(4, 8, D).sum(0)
                sum_b = sum_b + grad.reshape(4, 8, D).sum(0)
                scaled = grad * gain[...]
                mean = jnp.mean(scaled, axis=-1, keepdims=True)
                along = jnp.mean(scaled * hat, axis=-1, keepdims=True)
                done(rows, b["dx"][rows, :] + rs[rows, :] * (scaled - mean - hat * along))
                return sum_g, sum_b

            sums = (jnp.zeros((8, D), F32),) * 2
            for i in range(8):
                sums = body(i, sums)
            sum_g, sum_b = sums
            b["vec"][row : row + 1, :] = sum_g.sum(0, keepdims=True)
            b["vec"][row + 1 : row + 2, :] = sum_b.sum(0, keepdims=True)

        def gather_to(axis, key, src_of, dst_of, core):
            for r in (1, 3, 2):
                p, to = peer(axis, r)
                send(key, r, src_of(p), dst_of(r), (core, to))
            if core is other:
                send(key, 0, src_of(at[axis]), dst_of(0), (core, dp))
                return None
            return local(key, 0, src_of(at[axis]), dst_of(0))

        def cols(ref):
            return lambda r: ref.at[:, pl.ds(r * ROWS, ROWS)]

        def rows_of(ref):
            return lambda r: ref.at[pl.ds(r * ROWS, ROWS)]

        def scatter(axis, key, src_of, dst_of, base=0, core=sec):
            for r in (1, 3, 2):
                p, to = peer(axis, r)
                send(key, base + r, src_of(p), dst_of(r - 1), (core, to))

        def recv3(key, dst_of, base=0):
            for r in (1, 3, 2):
                recv(key, base + r, dst_of(r - 1))

        if not cross:
            weighted, ids = [], []
            total = jnp.zeros((1, 128), F32)
            for s in range(2):
                w = jnp.where(lane < flen[s], lw[s : s + 1, :].astype(F32), 0.0)
                total = total + jnp.where(lane == gid[s], jnp.sum(w, axis=1, keepdims=True), 0.0)
                weighted.append(w)
            b["tot"][...] = jnp.broadcast_to(total, (8, 128))
        pl.semaphore_wait(barrier, 19)
        if not cross:
            for a, axis in enumerate("xyz"):
                for r in (1, 2, 3):
                    _, to = peer(axis, r)
                    send("tot", 3 * a + r - 1, b["tot"], b["rtot"].at[a, r - 1], (sec, to))
                for r in (1, 2, 3):
                    recv("tot", 3 * a + r - 1, b["rtot"].at[a, r - 1])
                for copy in pending:
                    copy.wait_send()
                pending.clear()
                b["tot"][...] += b["rtot"][a, 0] + b["rtot"][a, 1] + b["rtot"][a, 2]
            totals = b["tot"][0:1, :]
            every = jnp.sum(totals, axis=1, keepdims=True)
            factors = every / (GROUPS * jnp.maximum(totals, 1.0))
            loads["cot"].wait()
            diagonal = lax.broadcasted_iota(jnp.int32, (SEQ, SEQ), 0) == lax.broadcasted_iota(
                jnp.int32, (SEQ, SEQ), 1
            )
            for s in range(2):
                factor = jnp.sum(jnp.where(lane == gid[s], factors, 0.0), axis=1, keepdims=True)
                picked = jnp.where(diagonal, weighted[s], 0.0).astype(BF)
                rows = slice(s * SEQ, (s + 1) * SEQ)
                grad = mm(picked, b["do"][rows, :]) * factor
                b["dx"][rows, :] = grad
                b["dyb"][rows, :] = grad.astype(BF)
            gather_to("y", "y", lambda p: b["dyb"], rows_of(b["rxy"]), other)

        if cross:
            loads["x"].wait()
        else:
            recv("act", 0, b["xb"])
        norm(b["xb"], g1, b1, b["xh1"], b["rs1"], b["n1"], b["s2t"].at[0])

        loads["wq"].wait()

        def query(i):
            b["q"][:, tile(i)] = (mm(b["n1"][...], b["wq"][:, tile(i)]).astype(BF) * 0.125).astype(BF)

        loop(3, query)

        loads["wkv"].wait()
        if cross:
            loads["ctx"].wait()

            def keyval(i):
                for m in range(4):
                    rows = slice(m * T, (m + 1) * T)
                    b["kv"][rows, tile(i)] = mm(b["ctx"][rows, :], b["wkv"][:, tile(i)]).astype(BF)
        else:

            def keyval(i):
                b["kv"][0:ROWS, tile(i)] = mm(b["n1"][...], b["wkv"][:, tile(i)]).astype(BF)

        loop(6, keyval)
        keys = CTX if cross else SEQ

        def blocks(i):
            s, j = i // PAIRS, i % PAIRS
            vcols = slice(D + 128 * j, D + 128 * (j + 1))
            return s, j, tile(s, SEQ), tile(s, keys), tile(j, 128), vcols

        if cross:
            key = lax.broadcasted_iota(jnp.int32, (1, keys), 1)
            masks = [jnp.where(key < clen[s], 0.0, -1e9) for s in range(2)]
        else:
            row = lax.broadcasted_iota(jnp.int32, (SEQ, keys), 0)
            mask = jnp.where(lax.broadcasted_iota(jnp.int32, (SEQ, keys), 1) <= row, 0.0, -1e9)
            masks = [jnp.concatenate([mask, mask], axis=0)] * 2
        ones = jnp.ones((keys, 128), BF)

        def attend(i):
            s, j, rows, krows, kcols, vcols = blocks(i)
            scores = mm_nt(stacked(b["q"][rows, kcols]), b["kv"][krows, kcols]) + masks[s]
            e = jnp.exp(scores - jnp.max(scores, axis=-1, keepdims=True))
            values = b["kv"][krows, vcols]
            if cross:
                e = e.astype(BF)
                b["p"][i] = e
                mixed = mm(e, jnp.concatenate([values, ones], axis=1))
                scale = 1.0 / merged(mixed[:, 128:])
                b["inv"][rows, kcols] = scale
                b["o"][rows, kcols] = (merged(mixed[:, :128]) * scale).astype(BF)
            else:
                probs = (e / jnp.sum(e, axis=-1, keepdims=True)).astype(BF)
                b["p"][i, :, 0:keys] = probs
                b["o"][rows, kcols] = merged(mm(probs, values)).astype(BF)

        loop(2 * PAIRS, attend)
        for j in range(3):
            b["s2t"][1, j * T : (j + 1) * T, :] = b["o"][:, j * T : (j + 1) * T].T
        if cross:
            own_a = gather_to("z", "a", lambda p: b["s2t"].at[p // 2], cols(b["rxa"]), sec)
        else:
            own_a = gather_to("z", "a", lambda p: b["s2t"].at[p // 2], cols(b["rxa"]), sec)
            own_a2 = gather_to("z", "a2", lambda p: b["s2t"].at[0], cols(b["ctxt"]), sec)

        loads["wo"].wait()

        def project(i):
            b["x2"][:, tile(i)] = b["xb"][:, tile(i)].astype(F32) + mm(b["o"][...], b["wo"][:, tile(i)])

        loop(3, project)
        norm(b["x2"], g2, b2, b["xh2"], b["rs2"], b["n2"], b["n2t"])
        gather_to("x", "n", lambda p: b["n2t"], cols(b["rxn"]), other)

        loads["wu"].wait()

        def up(i):
            u = mm(b["n2"][...], b["wu"][:, tile(i)]) + bu[:, tile(i)]
            square = u * u
            th = jnp.tanh(GELU_C * u * (1.0 + GELU_A * square))
            half = 0.5 * (1.0 + th)
            hidden = (u * half).astype(BF)
            slope = half + 0.5 * u * (1.0 - th * th) * (GELU_C * (1.0 + 3.0 * GELU_A * square))
            k, at_cols = i // 3, tile(i % 3)
            b["hm"][k, :, at_cols] = hidden
            b["gp"][k, :, at_cols] = slope.astype(BF)
            b["hmt"][tile(i), :] = hidden.T

        loop(12, up)
        gather_to("y", "h", lambda p: b["hmt"].at[tile(p, D)], cols(b["rxh"]), other)

        loads["wd"].wait()

        def down(i):
            y = b["x2"][:, tile(i)]
            for k in range(4):
                y = y + mm(b["hm"][k], b["wd"][k * D : (k + 1) * D, tile(i)])
            acts[:, tile(i)] = y.astype(BF)

        loop(3, down)
        if cross:
            send("act", 0, acts, b["xb"], (other, dp))

        def add4(own, parts):
            total = own.astype(F32)
            for part in parts:
                total = total + part.astype(F32)
            return total

        def down_a():
            for r in range(4):
                recv("h", r, cols(b["rxh"])(r))
                recv("y", r, rows_of(b["rxy"])(r))

            def body(i):
                v = mm(b["rxh"][...], b["rxy"][:, tile(i)]).astype(BF)
                b["gd"][:, :, :, tile(i)] = v.reshape(4, 4, 48, T)

            loop(3, body)
            scatter("x", "d1", lambda p: b["gd"].at[:, p], lambda r: b["rd1"].at[r])

        def down_b():
            recv3("d1", lambda r: b["rd1"].at[r])

            def body(i):
                b["hd"][i] = add4(b["gd"][i, at["x"]], [b["rd1"][r, i] for r in range(3)]).astype(BF)

            loop(4, body)
            scatter("z", "d2", lambda p: b["hd"].at[p], lambda r: b["rd2"].at[r])

        def down_c():
            recv3("d2", lambda r: b["rd2"].at[r])
            b["fd"][...] = add4(b["hd"][at["z"]], [b["rd2"][r] for r in range(3)])
            send("d3", 0, b["fd"], b["rfd"], (other, dp))

        def up_a():
            for r in range(4):
                recv("n", r, cols(b["rxn"])(r))
                recv("u", r, rows_of(b["rxd"])(r))

            def body(i):
                v = mm(b["rxn"][...], b["rxd"][:, tile(i)]).astype(BF)
                b["gu"][:, :, tile(i)] = v.reshape(4, 192, T)

            loop(3, body)
            scatter("y", "u1", lambda p: b["gu"].at[p], lambda r: b["ru1"].at[r])

        def up_b():
            recv3("u1", lambda r: b["ru1"].at[r])

            def body(i):
                rows = tile(i, 48)
                b["hu"][i] = add4(b["gu"][at["y"], rows], [b["ru1"][r, rows] for r in range(3)]).astype(BF)

            loop(4, body)
            scatter("z", "u2", lambda p: b["hu"].at[p], lambda r: b["ru2"].at[r])

        def up_c():
            recv3("u2", lambda r: b["ru2"].at[r])
            b["pad"][0:48, :] = add4(b["hu"][at["z"]], [b["ru2"][r] for r in range(3)])
            for j in range(4):
                b["fu"][j] = b["pad"][12 * j : 12 * j + 16, :].astype(BF)
            for r in (1, 3, 2, 0):
                p, to = peer("x", r)
                send("u3", r, b["fu"].at[p], b["ru3"].at[at["x"]], (other, to))

        width = 384 if cross else D

        def part(ref, *index):
            return ref.at[index + (slice(None), pl.ds(0, width))]

        def qo_a():
            own_a.wait()
            own_b.wait()
            for r in range(1, 4):
                recv("a", r, cols(b["rxa"])(r))
                recv("b", r, rows_of(b["rxb"])(r))
            if not cross:
                own_a2.wait()
                own_b2.wait()
                for r in range(1, 4):
                    recv("a2", r, cols(b["ctxt"])(r))
                    recv("b2", r, b["dkvt"].at[pl.ds(r * ROWS, ROWS), pl.ds(0, 384)])

            def body(i):
                rows = tile(i, 192)
                b["gq"][i, :, 0:384] = mm(b["rxa"][rows, :], b["rxb"][...]).astype(BF)
                if not cross:
                    b["gq"][i, :, 384:768] = mm(b["ctxt"][rows, :], b["dkvt"][0:1024, 0:384]).astype(BF)

            loop(4, body)
            scatter("y", "q1", lambda p: part(b["gq"], p), lambda r: part(b["rq1"], r))

        def qo_b():
            recv3("q1", lambda r: part(b["rq1"], r))

            def body(i):
                rows = tile(i, 48)
                b["pad"][rows, 0:width] = add4(
                    b["gq"][at["y"], rows, 0:width], [b["rq1"][r, rows, 0:width] for r in range(3)]
                )

            loop(4, body)
            for j in range(4):
                for k in range(4):
                    start = 48 * k + 12 * j
                    b["hq"][j, 16 * k : 16 * k + 16, 0:width] = b["pad"][start : start + 16, 0:width].astype(BF)
            scatter("x", "q2", lambda p: part(b["hq"], p), lambda r: part(b["rq2"], r))

        def qo_c():
            recv3("q2", lambda r: part(b["rq2"], r))
            total = add4(b["hq"][at["x"], :, 0:width], [b["rq2"][r, :, 0:width] for r in range(3)])
            b["fq"][:, :, 0:width] = total.astype(BF).reshape(4, 16, width)
            for r in (1, 3, 2):
                p, to = peer("z", r)
                send("q3", r, part(b["fq"], p), part(b["rq3"], at["z"]), (sec, to))
            b["rq3"][at["z"], :, 0:width] = b["fq"][at["z"], :, 0:width]

        def qo_d():
            for r in (1, 3, 2):
                recv("q3", r, part(b["rq3"], 0))
            for k in range(2):
                at_cols = slice(384 * k, 384 * (k + 1))
                oq[:, at_cols] = b["rq3"][k, :, 0:384].astype(F32)[:12]
                oo[:, at_cols] = b["rq3"][2 + k, :, 0:384].astype(F32)[:12]
            if not cross:
                for k in range(4):
                    okv[:, 384 * k : 384 * (k + 1)] = b["rq3"][k, :, 384:768].astype(F32)[:12]

        def kv_a():
            for h in range(2):

                def body(i):
                    v = mm_nt(b["ctxt"][...], b["dkvt"][tile(3 * h + i), :]).astype(BF)
                    b["gk"][h, :, :, :, tile(i)] = v.reshape(4, 4, 48, T)

                loop(3, body)
                scatter("z", "k1", lambda p: b["gk"].at[h, :, p], lambda r: b["rk1"].at[h, r], 4 * h)

        def kv_b(h):
            recv3("k1", lambda r: b["rk1"].at[h, r], 4 * h)

            def body(i):
                b["hk"][h, i] = add4(b["gk"][h, i, at["z"]], [b["rk1"][h, r, i] for r in range(3)]).astype(BF)

            loop(4, body)
            scatter("y", "k2", lambda p: b["hk"].at[h, p], lambda r: b["rk2"].at[h, r], 4 * h)

        def kv_c(h):
            recv3("k2", lambda r: b["rk2"].at[h, r], 4 * h)
            b["pad"][0:48, :] = add4(b["hk"][h, at["y"]], [b["rk2"][h, r] for r in range(3)])
            for j in range(4):
                b["fk"][h, j] = b["pad"][12 * j : 12 * j + 16, :].astype(BF)
            scatter("x", "k3", lambda p: b["fk"].at[h, p], lambda r: b["rk3"].at[h, r], 4 * h)

        def kv_d(h):
            recv3("k3", lambda r: b["rk3"].at[h, r], 4 * h)
            total = add4(b["fk"][h, at["x"]], [b["rk3"][h, r] for r in range(3)])
            okv[:, h * D : (h + 1) * D] = total[:12]

        def vec_send(a):
            for r in (1, 2, 3):
                _, to = peer("xyz"[a], r)
                send("v", 3 * a + r - 1, b["vec"], b["rvec"].at[a, r - 1], (sec, to))

        def vec_add(a):
            for r in (1, 2, 3):
                recv("v", 3 * a + r - 1, b["rvec"].at[a, r - 1])
            for copy in pending[-3:]:
                copy.wait_send()
            del pending[-3:]
            b["vec"][...] += b["rvec"][a, 0] + b["rvec"][a, 1] + b["rvec"][a, 2]

        def vec_out():
            shift = lax.rem(D - 12 * dp, D)
            rolled = pltpu.roll(b["vec"][...], shift, axis=1)
            for row, out in enumerate((og1, ob1, og2, ob2)):
                out[...] = rolled[row : row + 1, 0:12]
            bias_row = b["vec"][pl.ds(4 + at["y"], 1), :]
            shift = lax.rem(D - 48 * lax.rem(dp, 16), D)
            rolled = pltpu.roll(jnp.broadcast_to(bias_row, (8, D)), shift, axis=1)
            oub[...] = rolled[0:1, 0:48]

        if cross:
            for j in range(3):
                for m in range(4):
                    rows, at_cols = slice(m * T, (m + 1) * T), slice(j * T, (j + 1) * T)
                    b["ctxt"][at_cols, rows] = b["ctx"][rows, at_cols].T
            down_a()

        if cross:
            recv("back", 0, b["dyb"])
            b["dx"][...] = b["dyb"][...].astype(F32)
            gather_to("y", "y", lambda p: b["dyb"], rows_of(b["rxy"]), other)

        for k in range(4):

            def up_back(i):
                grad = mm_nt(b["dyb"][...], b["wd"][tile(3 * k + i), :])
                du = (b["gp"][k, :, tile(i)].astype(F32) * grad).astype(BF)
                b["hm"][k, :, tile(i)] = du
                b["vec"][4 + k : 5 + k, tile(i)] = jnp.sum(du.astype(F32), axis=0, keepdims=True)

            loop(3, up_back)
        gather_to("x", "u", lambda p: b["hm"].at[p], rows_of(b["rxd"]), other)

        if cross:
            up_a()

        def n2_back(i):
            grad = jnp.zeros((ROWS, T), F32)
            for k in range(4):
                grad = grad + mm_nt(b["hm"][k], b["wu"][tile(i), k * D : (k + 1) * D])
            b["dn"][:, tile(i)] = grad

        loop(3, n2_back)

        def done2(rows, value):
            b["dx"][rows, :] = value
            rounded = value.astype(BF)
            b["d4"][2, rows, :] = rounded[:, 0:384]
            b["d4"][3, rows, :] = rounded[:, 384:768]

        norm_back(b["xh2"], b["rs2"], g2, 2, done2)

        def out_back(i):
            rows = tile(i)
            grad = mm_nt(b["d4"][2], b["wo"][rows, 0:384]) + mm_nt(b["d4"][3], b["wo"][rows, 384:768])
            b["do"][:, tile(i)] = grad.astype(BF)

        loop(3, out_back)

        def attend_back(i):
            s, j, rows, krows, kcols, vcols = blocks(i)
            k2, v2 = b["kv"][krows, kcols], b["kv"][krows, vcols]
            q2 = stacked(b["q"][rows, kcols])
            probs = b["p"][i, :, 0:keys]
            grad = b["do"][rows, kcols].astype(F32)
            if cross:
                grad = grad * b["inv"][rows, kcols]
            along = grad * b["o"][rows, kcols].astype(F32)
            along = jnp.concatenate([jnp.where(first_head, along, 0.0), jnp.where(first_head, 0.0, along)], axis=0)
            along = jnp.sum(along, axis=-1, keepdims=True)
            do2 = stacked(grad.astype(BF))
            ds = (probs.astype(F32) * (mm_nt(do2, v2) - along)).astype(BF)
            half, at_cols = j // 3, tile(j % 3, 128)
            b["d4"][half, rows, at_cols] = (merged(mm(ds, k2)) * 0.125).astype(BF)
            if cross:
                b["dkvt"][tile(j, 128), krows] = mm_tn(q2, ds).astype(BF)
                b["dkvt"][vcols, krows] = mm_tn(do2, probs).astype(BF)
            else:
                b["ctx"][tile(2 * half + s, SEQ), at_cols] = mm_tn(ds, q2).astype(BF)
                b["ctx"][tile(4 + 2 * half + s, SEQ), at_cols] = mm_tn(probs, do2).astype(BF)

        loop(2 * PAIRS, attend_back)
        own_b = gather_to("z", "b", lambda p: b["d4"].at[p], rows_of(b["rxb"]), sec)
        if not cross:

            def kv_quarter(p):
                return b["ctx"].at[tile(p, ROWS), pl.ds(0, 384)]

            own_b2 = gather_to(
                "z", "b2", kv_quarter, lambda r: b["dkvt"].at[pl.ds(r * ROWS, ROWS), pl.ds(0, 384)], sec
            )

        def n1_back(i):
            rows = tile(i)
            grad = mm_nt(b["d4"][0], b["wq"][rows, 0:384]) + mm_nt(b["d4"][1], b["wq"][rows, 384:768])
            if not cross:
                for k in range(4):
                    quarter = b["ctx"][k * ROWS : (k + 1) * ROWS, 0:384]
                    grad = grad + mm_nt(quarter, b["wkv"][rows, 384 * k : 384 * (k + 1)])
            b["dn"][:, tile(i)] = grad

        loop(3, n1_back)

        def done1(rows, value):
            ins[rows, :] = value.astype(BF)

        norm_back(b["xh1"], b["rs1"], g1, 0, done1)
        if not cross:
            send("back", 0, ins, b["dyb"], (other, dp))

        if cross:
            kv_a()
            down_b()
            up_b()
            down_c()
            vec_send(0)
            vec_add(0)
            qo_a()
            up_c()
            vec_send(1)
            vec_add(1)
            kv_b(0)
            qo_b()
            kv_b(1)
            vec_send(2)
            vec_add(2)
            kv_c(0)
            qo_c()
            kv_c(1)
            vec_out()
            kv_d(0)
            kv_d(1)
            qo_d()
        else:
            qo_a()
            vec_send(0)
            vec_add(0)
            down_a()
            qo_b()
            vec_send(1)
            vec_add(1)
            up_a()
            qo_c()
            vec_send(2)
            vec_add(2)
            down_b()
            vec_out()
            qo_d()
            up_b()
            down_c()
            up_c()
        recv("d3", 0, b["rfd"])
        odn[...] = b["rfd"][...]
        for r in (1, 3, 2, 0):
            recv("u3", r, b["ru3"].at[0])
        for k in range(4):
            oup[:, k * D : (k + 1) * D] = b["ru3"][k].astype(F32)[:12]
        for copy in pending:
            copy.wait_send()

    pl.when(sec == 0)(lambda: branch(0))
    pl.when(sec == 1)(lambda: branch(1))


def deliver(*refs):
    for a, out in zip(refs[:12], refs[12:]):
        out[...] = a[...].reshape(out.shape)


def on_device(
    tokens, context, out_cot, group_id, ctx_len, fut_len, loss_weight,
    norm_gain1, norm_bias1, w_query, w_keyval, w_out,
    norm_gain2, norm_bias2, w_up, up_bias, w_down,
):
    smem = pl.BlockSpec(memory_space=pltpu.SMEM)
    vmem = pl.BlockSpec(memory_space=pltpu.VMEM)
    hbm = pl.BlockSpec(memory_space=pl.ANY)
    shape = jax.ShapeDtypeStruct
    outs = pl.pallas_call(
        kernel,
        out_shape=(
            shape((ROWS, D), BF),
            shape((ROWS, D), BF),
            shape((1, 12), F32),
            shape((1, 12), F32),
            shape((12, D), F32),
            shape((12, 2 * D), F32),
            shape((12, D), F32),
            shape((1, 12), F32),
            shape((1, 12), F32),
            shape((12, FF), F32),
            shape((1, 48), F32),
            shape((48, D), F32),
        ),
        in_specs=[smem] * 3 + [vmem] + [hbm] * 3 + [vmem] * 5 + [hbm] * 5,
        out_specs=[vmem] * 12,
        scratch_shapes=[pltpu.VMEM(s, t) for s, t in BUFS.values()]
        + [pltpu.SemaphoreType.DMA((N_SEMS,)), pltpu.SemaphoreType.DMA((N_SEMS,))],
        compiler_params=pltpu.CompilerParams(
            collective_id=0, has_side_effects=True, vmem_limit_bytes=64 * 1024 * 1024 - 4096
        ),
    )(
        group_id, ctx_len, fut_len, loss_weight,
        tokens.reshape(ROWS, D), context.reshape(2 * CTX, D), out_cot.reshape(ROWS, D),
        norm_gain1, norm_bias1, norm_gain2, norm_bias2, up_bias,
        w_query[0], w_keyval[0], w_out[0], w_up[0], w_down[0],
    )
    outs = pl.pallas_call(
        deliver,
        out_shape=[
            shape((a.shape[0], 1, a.shape[1]) if a.shape[0] == 12 else a.shape, a.dtype) for a in outs
        ],
        in_specs=[vmem] * 12,
        out_specs=[vmem] * 12,
    )(*outs)
    acts, ins, gg1, gb1, gq, gkv, go, gg2, gb2, gup, gub, gdn = outs
    seqs = (1, 2, SEQ, D)
    rows = [g.reshape(1, 12, g.shape[-1]) for g in (gq, gkv, go, gup)]
    return (
        acts.reshape(seqs), ins.reshape(seqs), gg1, gb1, *rows[:3],
        gg2, gb2, rows[3], gub, gdn[None],
    )


def solution(mesh):
    dp, sec = "dp", "section"
    vec, mat = P(sec, None), P(sec, None, None)
    return jax.shard_map(
        on_device,
        mesh=mesh,
        in_specs=(P(dp, None, None),) * 3 + (P(dp),) * 3 + (P(dp, None),)
        + (vec, vec, mat, mat, mat, vec, vec, mat, vec, mat),
        out_specs=(P(sec, dp, None, None),) * 2 + (P(sec, dp),) * 2 + (P(sec, dp, None),) * 3
        + (P(sec, dp),) * 2 + (P(sec, dp, None), P(sec, dp), P(sec, dp, None)),
        check_vma=False,
    )
```

```python
import math

import jax
import jax.numpy as jnp
from jax import lax
from jax.experimental import pallas as pl
from jax.experimental.pallas import tpu as pltpu
from jax.sharding import PartitionSpec as P

MESH = pl.DeviceIdType.MESH
BF = jnp.bfloat16
F32 = jnp.float32
GROUPS = 8
D = 768
FF = 3072
SEQ = 128
ROWS = 256
CTX = 512
PAIRS = 6
T = 256
GELU_C = math.sqrt(2.0 / math.pi)
GELU_A = 0.044715


def mm(a, b):
    return jnp.dot(a, b, preferred_element_type=F32)


def mm_nt(a, b):
    return lax.dot_general(a, b, (((1,), (1,)), ((), ())), preferred_element_type=F32)


def mm_tn(a, b):
    return lax.dot_general(a, b, (((0,), (0,)), ((), ())), preferred_element_type=F32)


def loop(n, body):
    for i in range(n):
        body(i)


def tile(i, size=T):
    if isinstance(i, int):
        return slice(i * size, (i + 1) * size)
    return pl.ds(pl.multiple_of(i * size, size), size)


BUFS = dict(
    wq=((D, D), BF),
    wkv=((D, 2 * D), BF),
    wo=((D, D), BF),
    wu=((D, FF), BF),
    wd=((FF, D), BF),
    xb=((ROWS, D), BF),
    ctx=((2 * CTX, D), BF),
    ctxt=((D, 2 * CTX), BF),
    n1=((ROWS, D), BF),
    q=((ROWS, D), BF),
    kv=((2 * CTX, 2 * D), BF),
    p=((2 * PAIRS, ROWS, CTX), BF),
    inv=((ROWS, D), F32),
    o=((ROWS, D), BF),
    s2t=((2, D, ROWS), BF),
    n2=((ROWS, D), BF),
    n2t=((D, ROWS), BF),
    x2=((ROWS, D), F32),
    xh1=((ROWS, D), F32),
    xh2=((ROWS, D), F32),
    rs1=((ROWS, 1), F32),
    rs2=((ROWS, 1), F32),
    gp=((4, ROWS, D), BF),
    hm=((4, ROWS, D), BF),
    hmt=((FF, ROWS), BF),
    dyb=((ROWS, D), BF),
    dx=((ROWS, D), F32),
    d4=((4, ROWS, 384), BF),
    dkvt=((2 * D, 2 * CTX), BF),
    vec=((8, D), F32),
    rvec=((3, 3, 8, D), F32),
    tot=((8, 128), F32),
    rtot=((3, 3, 8, 128), F32),
    rxh=((D, 4 * ROWS), BF),
    rxy=((4 * ROWS, D), BF),
    rxn=((D, 4 * ROWS), BF),
    rxd=((4 * ROWS, D), BF),
    gd=((4, 4, 48, D), BF),
    rd1=((3, 4, 48, D), BF),
    hd=((4, 48, D), BF),
    rd2=((4, 48, D), BF),
    gu=((4, 4, 48, D), BF),
    ru1=((3, 4, 48, D), BF),
    hu=((4, 4, 16, D), BF),
    ru2=((4, 4, 16, D), BF),
    rxa=((D, 4 * ROWS), BF),
    rxb=((4 * ROWS, 384), BF),
    gq=((4, 192, D), BF),
    rq1=((3, 192, D), BF),
    hq=((4, 4, 16, D), BF),
    rq2=((4, 4, 16, D), BF),
    gk=((2, 4, 4, 48, D), BF),
    rk1=((2, 3, 4, 48, D), BF),
    hk=((2, 4, 4, 16, D), BF),
    rk2=((2, 16, 16, D), BF),
)
KEYS = {}
for _name, _n in dict(
    tot=9, act=1, back=1, a=4, n=4, h=4, y=4, u=4, b=4, a2=4, b2=4,
    d1=4, d2=4, u1=4, u2=16, q1=4, q2=16, k1=8, k2=32, v=9, load=8,
).items():
    KEYS[_name] = sum(KEYS.values()) if not KEYS else _total
    _total = KEYS[_name] + _n
N_SEMS = _total
NAMES = list(BUFS)


def kernel(*refs):
    (gid, clen, flen, lw, tokens, ctx_in, cot_in, g1, b1, g2, b2, bu, wq_in, wkv_in, wo_in, wu_in, wd_in) = refs[:17]
    (acts, ins, og1, ob1, oq, okv, oo, og2, ob2, oup, oub, odn) = refs[17:29]
    b = dict(zip(NAMES, refs[29 : 29 + len(NAMES)]))
    b["do"] = b["n1"]
    b["dn"] = b["x2"]
    b["pad"] = b["x2"].at[pl.ds(0, 208)]
    ssem, rsem = refs[29 + len(NAMES) :]

    sec = lax.axis_index("section")
    dp = lax.axis_index("dp")
    at = {"y": dp // 16, "z": (dp // 4) % 4, "x": dp % 4}
    step = {"y": 16, "z": 4, "x": 1}
    other = 1 - sec

    def peer(axis, r):
        p = lax.rem(at[axis] + r, 4)
        return p, dp + (p - at[axis]) * step[axis]

    def peer2(axis, r, axis2, r2):
        p, to = peer(axis, r)
        p2, to2 = peer(axis2, r2)
        return p, p2, to + to2 - dp

    barrier = pltpu.get_barrier_semaphore()
    pl.semaphore_signal(barrier, inc=1, device_id=(other, dp), device_id_type=MESH)
    near = [peer(axis, r)[1] for axis in "xyz" for r in (1, 2, 3)]
    for axis in "yz":
        near += [peer2(axis, r, "x", r2)[2] for r in (1, 2, 3) for r2 in (1, 2, 3)]
    for to in near:
        for core in (sec, other):
            pl.semaphore_signal(barrier, inc=1, device_id=(core, to), device_id_type=MESH)

    def branch(mine):
        cross = mine == 0
        pending = []

        def send(key, i, src, dst, device):
            k = KEYS[key] + i
            copy = pltpu.make_async_remote_copy(
                src_ref=src, dst_ref=dst, send_sem=ssem.at[k], recv_sem=rsem.at[k],
                device_id=device, device_id_type=MESH,
            )
            copy.start()
            pending.append(copy)

        def recv(key, i, ref):
            k = KEYS[key] + i
            pltpu.make_async_remote_copy(
                src_ref=ref, dst_ref=ref, send_sem=ssem.at[k], recv_sem=rsem.at[k],
                device_id=(other, dp), device_id_type=MESH,
            ).wait_recv()

        def local(key, i, src, dst):
            copy = pltpu.make_async_copy(src, dst, rsem.at[KEYS[key] + i])
            copy.start()
            return copy

        loads = {}

        def load(name, i, src, dst):
            loads[name] = local("load", i, src, dst)

        if cross:
            load("x", 0, tokens, b["xb"])
            load("wq", 3, wq_in, b["wq"])
            load("ctx", 1, ctx_in, b["ctx"])
            load("wkv", 2, wkv_in, b["wkv"])
        else:
            load("cot", 0, cot_in, b["do"])
            load("wq", 3, wq_in, b["wq"])
            load("wkv", 2, wkv_in, b["wkv"])
        load("wo", 4, wo_in, b["wo"])
        load("wu", 5, wu_in, b["wu"])
        load("wd", 6, wd_in, b["wd"])

        lane = lax.broadcasted_iota(jnp.int32, (1, 128), 1)
        first_head = lane < 64
        mask_a = first_head.astype(F32).astype(BF)
        mask_b = 1.0 - mask_a

        def stacked(v):
            return jnp.concatenate([v * mask_a, v * mask_b], axis=0)

        def merged(v):
            return jnp.where(first_head, v[:SEQ], v[SEQ:])

        def norm(src, gain, bias, xh, rs, n, nt):
            def body(i):
                rows = tile(i, 32)
                v = src[rows, :].astype(F32)
                centre = v - jnp.mean(v, axis=-1, keepdims=True)
                spread = jnp.mean(centre * centre, axis=-1, keepdims=True)
                scale = lax.rsqrt(spread + 1e-05)
                hat = centre * scale
                xh[rows, :] = hat
                rs[rows, :] = scale
                n[rows, :] = (hat * gain[...] + bias[...]).astype(BF)

            loop(8, body)
            for j in range(3):
                nt[j * T : (j + 1) * T, :] = n[:, j * T : (j + 1) * T].T

        def norm_back(xh, rs, gain, row, done):
            def body(i, carry):
                sum_g, sum_b = carry
                rows = tile(i, 32)
                grad = b["dn"][rows, :]
                hat = xh[rows, :]
                sum_g = sum_g + (grad * hat).reshape(4, 8, D).sum(0)
                sum_b = sum_b + grad.reshape(4, 8, D).sum(0)
                scaled = grad * gain[...]
                mean = jnp.mean(scaled, axis=-1, keepdims=True)
                along = jnp.mean(scaled * hat, axis=-1, keepdims=True)
                done(rows, b["dx"][rows, :] + rs[rows, :] * (scaled - mean - hat * along))
                return sum_g, sum_b

            sums = (jnp.zeros((8, D), F32),) * 2
            for i in range(8):
                sums = body(i, sums)
            sum_g, sum_b = sums
            b["vec"][row : row + 1, :] = sum_g.sum(0, keepdims=True)
            b["vec"][row + 1 : row + 2, :] = sum_b.sum(0, keepdims=True)

        def gather_to(axis, key, src_of, dst_of, core):
            for r in (1, 3, 2):
                p, to = peer(axis, r)
                send(key, r, src_of(p), dst_of(r), (core, to))
            if core is other:
                send(key, 0, src_of(at[axis]), dst_of(0), (core, dp))
                return None
            return local(key, 0, src_of(at[axis]), dst_of(0))

        def cols(ref):
            return lambda r: ref.at[:, pl.ds(r * ROWS, ROWS)]

        def rows_of(ref):
            return lambda r: ref.at[pl.ds(r * ROWS, ROWS)]

        def scatter(axis, key, src_of, dst_of, base=0, core=sec):
            for r in (1, 3, 2):
                p, to = peer(axis, r)
                send(key, base + r, src_of(p), dst_of(r - 1), (core, to))

        def recv3(key, dst_of, base=0):
            for r in (1, 3, 2):
                recv(key, base + r, dst_of(r - 1))

        if not cross:
            weighted, ids = [], []
            total = jnp.zeros((1, 128), F32)
            for s in range(2):
                w = jnp.where(lane < flen[s], lw[s : s + 1, :].astype(F32), 0.0)
                total = total + jnp.where(lane == gid[s], jnp.sum(w, axis=1, keepdims=True), 0.0)
                weighted.append(w)
            b["tot"][...] = jnp.broadcast_to(total, (8, 128))
        pl.semaphore_wait(barrier, 1 + 2 * len(near))
        if not cross:
            for a, axis in enumerate("xyz"):
                for r in (1, 2, 3):
                    _, to = peer(axis, r)
                    send("tot", 3 * a + r - 1, b["tot"], b["rtot"].at[a, r - 1], (sec, to))
                for r in (1, 2, 3):
                    recv("tot", 3 * a + r - 1, b["rtot"].at[a, r - 1])
                for copy in pending:
                    copy.wait_send()
                pending.clear()
                b["tot"][...] += b["rtot"][a, 0] + b["rtot"][a, 1] + b["rtot"][a, 2]
            totals = b["tot"][0:1, :]
            every = jnp.sum(totals, axis=1, keepdims=True)
            factors = every / (GROUPS * jnp.maximum(totals, 1.0))
            loads["cot"].wait()
            diagonal = lax.broadcasted_iota(jnp.int32, (SEQ, SEQ), 0) == lax.broadcasted_iota(
                jnp.int32, (SEQ, SEQ), 1
            )
            for s in range(2):
                factor = jnp.sum(jnp.where(lane == gid[s], factors, 0.0), axis=1, keepdims=True)
                picked = jnp.where(diagonal, weighted[s], 0.0).astype(BF)
                rows = slice(s * SEQ, (s + 1) * SEQ)
                grad = mm(picked, b["do"][rows, :]) * factor
                b["dx"][rows, :] = grad
                b["dyb"][rows, :] = grad.astype(BF)
            gather_to("y", "y", lambda p: b["dyb"], rows_of(b["rxy"]), other)

        if cross:
            loads["x"].wait()
        else:
            recv("act", 0, b["xb"])
        norm(b["xb"], g1, b1, b["xh1"], b["rs1"], b["n1"], b["s2t"].at[0])

        loads["wq"].wait()

        def query(i):
            b["q"][:, tile(i)] = (mm(b["n1"][...], b["wq"][:, tile(i)]).astype(BF) * 0.125).astype(BF)

        loop(3, query)

        loads["wkv"].wait()
        if cross:
            loads["ctx"].wait()

            def keyval(i):
                for m in range(4):
                    rows = slice(m * T, (m + 1) * T)
                    b["kv"][rows, tile(i)] = mm(b["ctx"][rows, :], b["wkv"][:, tile(i)]).astype(BF)
        else:

            def keyval(i):
                b["kv"][0:ROWS, tile(i)] = mm(b["n1"][...], b["wkv"][:, tile(i)]).astype(BF)

        loop(6, keyval)
        keys = CTX if cross else SEQ

        def blocks(i):
            s, j = i // PAIRS, i % PAIRS
            vcols = slice(D + 128 * j, D + 128 * (j + 1))
            return s, j, tile(s, SEQ), tile(s, keys), tile(j, 128), vcols

        if cross:
            key = lax.broadcasted_iota(jnp.int32, (1, keys), 1)
            masks = [jnp.where(key < clen[s], 0.0, -1e9) for s in range(2)]
        else:
            row = lax.broadcasted_iota(jnp.int32, (SEQ, keys), 0)
            mask = jnp.where(lax.broadcasted_iota(jnp.int32, (SEQ, keys), 1) <= row, 0.0, -1e9)
            masks = [jnp.concatenate([mask, mask], axis=0)] * 2
        ones = jnp.ones((keys, 128), BF)

        def attend(i):
            s, j, rows, krows, kcols, vcols = blocks(i)
            scores = mm_nt(stacked(b["q"][rows, kcols]), b["kv"][krows, kcols]) + masks[s]
            e = jnp.exp(scores - jnp.max(scores, axis=-1, keepdims=True))
            values = b["kv"][krows, vcols]
            if cross:
                e = e.astype(BF)
                b["p"][i] = e
                mixed = mm(e, jnp.concatenate([values, ones], axis=1))
                scale = 1.0 / merged(mixed[:, 128:])
                b["inv"][rows, kcols] = scale
                b["o"][rows, kcols] = (merged(mixed[:, :128]) * scale).astype(BF)
            else:
                probs = (e / jnp.sum(e, axis=-1, keepdims=True)).astype(BF)
                b["p"][i, :, 0:keys] = probs
                b["o"][rows, kcols] = merged(mm(probs, values)).astype(BF)

        loop(2 * PAIRS, attend)
        for j in range(3):
            b["s2t"][1, j * T : (j + 1) * T, :] = b["o"][:, j * T : (j + 1) * T].T
        if cross:
            own_a = gather_to("z", "a", lambda p: b["s2t"].at[p // 2], cols(b["rxa"]), sec)
        else:
            own_a = gather_to("z", "a", lambda p: b["s2t"].at[p // 2], cols(b["rxa"]), sec)
            own_a2 = gather_to("z", "a2", lambda p: b["s2t"].at[0], cols(b["ctxt"]), sec)

        loads["wo"].wait()

        def project(i):
            b["x2"][:, tile(i)] = b["xb"][:, tile(i)].astype(F32) + mm(b["o"][...], b["wo"][:, tile(i)])

        loop(3, project)
        norm(b["x2"], g2, b2, b["xh2"], b["rs2"], b["n2"], b["n2t"])
        gather_to("x", "n", lambda p: b["n2t"], cols(b["rxn"]), other)

        loads["wu"].wait()

        def up(i):
            u = mm(b["n2"][...], b["wu"][:, tile(i)]) + bu[:, tile(i)]
            square = u * u
            th = jnp.tanh(GELU_C * u * (1.0 + GELU_A * square))
            half = 0.5 * (1.0 + th)
            hidden = (u * half).astype(BF)
            slope = half + 0.5 * u * (1.0 - th * th) * (GELU_C * (1.0 + 3.0 * GELU_A * square))
            k, at_cols = i // 3, tile(i % 3)
            b["hm"][k, :, at_cols] = hidden
            b["gp"][k, :, at_cols] = slope.astype(BF)
            b["hmt"][tile(i), :] = hidden.T

        loop(12, up)
        gather_to("y", "h", lambda p: b["hmt"].at[tile(p, D)], cols(b["rxh"]), other)

        loads["wd"].wait()

        def down(i):
            y = b["x2"][:, tile(i)]
            for k in range(4):
                y = y + mm(b["hm"][k], b["wd"][k * D : (k + 1) * D, tile(i)])
            acts[:, tile(i)] = y.astype(BF)

        loop(3, down)
        if cross:
            send("act", 0, acts, b["xb"], (other, dp))

        def add4(own, parts):
            total = own.astype(F32)
            for part in parts:
                total = total + part.astype(F32)
            return total

        def plane(key, axis, src_of, dst, base=0, core=sec):
            for r in (1, 3, 2, 0):
                for r2 in (1, 3, 2, 0):
                    if r or r2 or core is other:
                        p, p2, to = peer2(axis, r, "x", r2)
                        send(key, base + 4 * r + r2, src_of(p, p2), dst(r, r2), (core, to))

        def recv_plane(key, ref, base=0, first=1):
            for i in range(first, 16):
                recv(key, base + i, ref)

        def cut(dst, cols):
            for k in range(4):
                for j in range(4):
                    start = 48 * k + 12 * j
                    dst[k, j, :, cols] = b["pad"][start : start + 16, cols].astype(BF)

        full = slice(0, D)

        def down_a():
            for r in range(4):
                recv("h", r, cols(b["rxh"])(r))
                recv("y", r, rows_of(b["rxy"])(r))
            for i in range(3):
                v = mm(b["rxh"][...], b["rxy"][:, tile(i)]).astype(BF)
                b["gd"][:, :, :, tile(i)] = v.reshape(4, 4, 48, T)
            scatter("x", "d1", lambda p: b["gd"].at[:, p], lambda r: b["rd1"].at[r])

        def down_b():
            recv3("d1", lambda r: b["rd1"].at[r])
            for i in range(4):
                b["hd"][i] = add4(b["gd"][i, at["x"]], [b["rd1"][r, i] for r in range(3)]).astype(BF)
            for r in (1, 3, 2, 0):
                p, to = peer("z", r)
                send("d2", r, b["hd"].at[p], b["rd2"].at[r], (other, to))

        def down_end():
            for r in range(4):
                recv("d2", r, b["rd2"].at[r])
            odn[...] = add4(b["rd2"][0], [b["rd2"][r] for r in (1, 2, 3)])

        def up_axes(layer):
            return ("z", "y") if layer == 1 else ("y", "z")

        def up_a():
            axis = up_axes(1 - mine)[0]
            for r in range(4):
                recv("n", r, cols(b["rxn"])(r))
                recv("u", r, rows_of(b["rxd"])(r))
            for i in range(3):
                v = mm(b["rxn"][...], b["rxd"][:, tile(i)]).astype(BF)
                b["gu"][:, :, :, tile(i)] = v.reshape(4, 4, 48, T)
            pick = (lambda p: b["gu"].at[p]) if axis == "y" else (lambda p: b["gu"].at[:, p])
            scatter(axis, "u1", pick, lambda r: b["ru1"].at[r])

        def up_b():
            axis, rest = up_axes(1 - mine)
            recv3("u1", lambda r: b["ru1"].at[r])
            for i in range(4):
                own = b["gu"][at["y"], i] if axis == "y" else b["gu"][i, at["z"]]
                b["pad"][tile(i, 48), :] = add4(own, [b["ru1"][r, i] for r in range(3)])
            cut(b["hu"], full)
            plane(
                "u2", rest, lambda p, p2: b["hu"].at[p, p2],
                lambda r, r2: b["ru2"].at[r, at["x"]], core=other,
            )

        def up_end():
            recv_plane("u2", b["ru2"].at[0, 0], first=0)
            for k in range(4):
                total = add4(b["ru2"][0, k], [b["ru2"][r, k] for r in (1, 2, 3)])
                oup[:, k * D : (k + 1) * D] = total[:12]

        width = 384 if cross else D
        part = slice(0, width)

        def qo_a():
            own_a.wait()
            own_b.wait()
            for r in range(1, 4):
                recv("a", r, cols(b["rxa"])(r))
                recv("b", r, rows_of(b["rxb"])(r))
            if not cross:
                own_a2.wait()
                own_b2.wait()
                for r in range(1, 4):
                    recv("a2", r, cols(b["ctxt"])(r))
                    recv("b2", r, b["dkvt"].at[pl.ds(r * ROWS, ROWS), pl.ds(0, 384)])
            for i in range(2):
                rows = tile(i, 384)
                v = mm(b["rxa"][rows, :], b["rxb"][...]).astype(BF)
                b["gq"][2 * i : 2 * i + 2, :, 0:384] = v.reshape(2, 192, 384)
                if not cross:
                    v = mm(b["ctxt"][rows, :], b["dkvt"][0:1024, 0:384]).astype(BF)
                    b["gq"][2 * i : 2 * i + 2, :, 384:768] = v.reshape(2, 192, 384)
            scatter("y", "q1", lambda p: b["gq"].at[p, :, pl.ds(0, width)], lambda r: b["rq1"].at[r, :, pl.ds(0, width)])

        def qo_b():
            recv3("q1", lambda r: b["rq1"].at[r, :, pl.ds(0, width)])
            for i in range(4):
                rows = tile(i, 48)
                b["pad"][rows, part] = add4(b["gq"][at["y"], rows, part], [b["rq1"][r, rows, part] for r in range(3)])
            cut(b["hq"], part)
            plane(
                "q2", "z", lambda p, p2: b["hq"].at[p, p2, :, pl.ds(0, width)],
                lambda r, r2: b["rq2"].at[at["z"], r2, :, pl.ds(0, width)],
            )
            b["rq2"][at["z"], 0, :, part] = b["hq"][at["z"], at["x"], :, part]

        def qo_end():
            recv_plane("q2", b["rq2"].at[0, 0, :, pl.ds(0, width)])

            def total(k, at_cols):
                return add4(b["rq2"][k, 0, :, at_cols], [b["rq2"][k, r, :, at_cols] for r in (1, 2, 3)])[:12]

            for k in range(2):
                oq[:, 384 * k : 384 * (k + 1)] = total(k, slice(0, 384))
                oo[:, 384 * k : 384 * (k + 1)] = total(2 + k, slice(0, 384))
            if not cross:
                for k in range(4):
                    okv[:, 384 * k : 384 * (k + 1)] = total(k, slice(384, D))

        def kv_a(h):
            for i in range(3):
                v = mm_nt(b["ctxt"][...], b["dkvt"][tile(3 * h + i), :]).astype(BF)
                b["gk"][h, :, :, :, tile(i)] = v.reshape(4, 4, 48, T)
            pick = (lambda p: b["gk"].at[1, p]) if h else (lambda p: b["gk"].at[0, :, p])
            scatter("y" if h else "z", "k1", pick, lambda r: b["rk1"].at[h, r], 4 * h)

        def kv_b(h):
            recv3("k1", lambda r: b["rk1"].at[h, r], 4 * h)
            for i in range(4):
                own = b["gk"][1, at["y"], i] if h else b["gk"][0, i, at["z"]]
                b["pad"][tile(i, 48), :] = add4(own, [b["rk1"][h, r, i] for r in range(3)])
            cut(b["hk"].at[h], full)
            axis = "z" if h else "y"
            plane(
                "k2", axis, lambda p, p2: b["hk"].at[h, p, p2],
                lambda r, r2: b["rk2"].at[h, 4 * r + r2], 16 * h,
            )
            b["rk2"][h, 0] = b["hk"][h, at[axis], at["x"]]

        def kv_end(h):
            recv_plane("k2", b["rk2"].at[h, 1], 16 * h)
            total = add4(b["rk2"][h, 0], [b["rk2"][h, i] for i in range(1, 16)])
            okv[:, h * D : (h + 1) * D] = total[:12]

        vec_copies = []

        def vec_send(a):
            for r in (1, 2, 3):
                _, to = peer("xyz"[a], r)
                send("v", 3 * a + r - 1, b["vec"], b["rvec"].at[a, r - 1], (sec, to))
                vec_copies.append(pending.pop())

        def vec_add(a):
            for r in (1, 2, 3):
                recv("v", 3 * a + r - 1, b["rvec"].at[a, r - 1])
            for copy in vec_copies:
                copy.wait_send()
            vec_copies.clear()
            b["vec"][...] += b["rvec"][a, 0] + b["rvec"][a, 1] + b["rvec"][a, 2]

        def vec_out():
            shift = lax.rem(D - 12 * dp, D)
            rolled = pltpu.roll(b["vec"][...], shift, axis=1)
            for row, out in enumerate((og1, ob1, og2, ob2)):
                out[...] = rolled[row : row + 1, 0:12]
            bias_row = b["vec"][pl.ds(4 + at["y"], 1), :]
            shift = lax.rem(D - 48 * lax.rem(dp, 16), D)
            rolled = pltpu.roll(jnp.broadcast_to(bias_row, (8, D)), shift, axis=1)
            oub[...] = rolled[0:1, 0:48]

        if cross:
            for j in range(3):
                for m in range(4):
                    rows, at_cols = slice(m * T, (m + 1) * T), slice(j * T, (j + 1) * T)
                    b["ctxt"][at_cols, rows] = b["ctx"][rows, at_cols].T
        if cross:
            recv("back", 0, b["dyb"])
            b["dx"][...] = b["dyb"][...].astype(F32)
            gather_to("y", "y", lambda p: b["dyb"], rows_of(b["rxy"]), other)

        for k in range(4):

            def up_back(i):
                grad = mm_nt(b["dyb"][...], b["wd"][tile(3 * k + i), :])
                du = (b["gp"][k, :, tile(i)].astype(F32) * grad).astype(BF)
                b["hm"][k, :, tile(i)] = du
                b["vec"][4 + k : 5 + k, tile(i)] = jnp.sum(du.astype(F32), axis=0, keepdims=True)

            loop(3, up_back)
        gather_to("x", "u", lambda p: b["hm"].at[p], rows_of(b["rxd"]), other)

        if cross:
            down_a()

        def n2_back(i):
            grad = jnp.zeros((ROWS, T), F32)
            for k in range(4):
                grad = grad + mm_nt(b["hm"][k], b["wu"][tile(i), k * D : (k + 1) * D])
            b["dn"][:, tile(i)] = grad

        loop(3, n2_back)

        def done2(rows, value):
            b["dx"][rows, :] = value
            rounded = value.astype(BF)
            b["d4"][2, rows, :] = rounded[:, 0:384]
            b["d4"][3, rows, :] = rounded[:, 384:768]

        norm_back(b["xh2"], b["rs2"], g2, 2, done2)

        def out_back(i):
            rows = tile(i)
            grad = mm_nt(b["d4"][2], b["wo"][rows, 0:384]) + mm_nt(b["d4"][3], b["wo"][rows, 384:768])
            b["do"][:, tile(i)] = grad.astype(BF)

        loop(3, out_back)

        def attend_back(i):
            s, j, rows, krows, kcols, vcols = blocks(i)
            k2, v2 = b["kv"][krows, kcols], b["kv"][krows, vcols]
            q2 = stacked(b["q"][rows, kcols])
            probs = b["p"][i, :, 0:keys]
            grad = b["do"][rows, kcols].astype(F32)
            if cross:
                grad = grad * b["inv"][rows, kcols]
            along = grad * b["o"][rows, kcols].astype(F32)
            along = jnp.concatenate([jnp.where(first_head, along, 0.0), jnp.where(first_head, 0.0, along)], axis=0)
            along = jnp.sum(along, axis=-1, keepdims=True)
            do2 = stacked(grad.astype(BF))
            ds = (probs.astype(F32) * (mm_nt(do2, v2) - along)).astype(BF)
            half, at_cols = j // 3, tile(j % 3, 128)
            b["d4"][half, rows, at_cols] = (merged(mm(ds, k2)) * 0.125).astype(BF)
            if cross:
                b["dkvt"][tile(j, 128), krows] = mm_tn(q2, ds).astype(BF)
                b["dkvt"][vcols, krows] = mm_tn(do2, probs).astype(BF)
            else:
                b["ctx"][tile(2 * half + s, SEQ), at_cols] = mm_tn(ds, q2).astype(BF)
                b["ctx"][tile(4 + 2 * half + s, SEQ), at_cols] = mm_tn(probs, do2).astype(BF)

        loop(2 * PAIRS, attend_back)
        own_b = gather_to("z", "b", lambda p: b["d4"].at[p], rows_of(b["rxb"]), sec)
        if not cross:

            def kv_quarter(p):
                return b["ctx"].at[tile(p, ROWS), pl.ds(0, 384)]

            own_b2 = gather_to(
                "z", "b2", kv_quarter, lambda r: b["dkvt"].at[pl.ds(r * ROWS, ROWS), pl.ds(0, 384)], sec
            )

        if cross:
            kv_a(0)
            kv_a(1)
            up_a()

        def n1_back(i):
            rows = tile(i)
            grad = mm_nt(b["d4"][0], b["wq"][rows, 0:384]) + mm_nt(b["d4"][1], b["wq"][rows, 384:768])
            if not cross:
                for k in range(4):
                    quarter = b["ctx"][k * ROWS : (k + 1) * ROWS, 0:384]
                    grad = grad + mm_nt(quarter, b["wkv"][rows, 384 * k : 384 * (k + 1)])
            b["dn"][:, tile(i)] = grad

        loop(3, n1_back)

        def done1(rows, value):
            ins[rows, :] = value.astype(BF)

        norm_back(b["xh1"], b["rs1"], g1, 0, done1)
        if not cross:
            send("back", 0, ins, b["dyb"], (other, dp))

        vec_send(0)
        if cross:
            down_b()
            qo_a()
            vec_add(0)
            vec_send(1)
            up_b()
            kv_b(0)
            kv_b(1)
            vec_add(1)
            vec_send(2)
            qo_b()
            vec_add(2)
            vec_out()
            kv_end(0)
            kv_end(1)
        else:
            down_a()
            qo_a()
            vec_add(0)
            vec_send(1)
            up_a()
            qo_b()
            vec_add(1)
            vec_send(2)
            down_b()
            vec_add(2)
            vec_out()
            up_b()
        qo_end()
        down_end()
        up_end()
        for copy in pending:
            copy.wait_send()

    pl.when(sec == 0)(lambda: branch(0))
    pl.when(sec == 1)(lambda: branch(1))


def deliver(*refs):
    for a, out in zip(refs[:12], refs[12:]):
        out[...] = a[...].reshape(out.shape)


def on_device(
    tokens, context, out_cot, group_id, ctx_len, fut_len, loss_weight,
    norm_gain1, norm_bias1, w_query, w_keyval, w_out,
    norm_gain2, norm_bias2, w_up, up_bias, w_down,
):
    smem = pl.BlockSpec(memory_space=pltpu.SMEM)
    vmem = pl.BlockSpec(memory_space=pltpu.VMEM)
    hbm = pl.BlockSpec(memory_space=pl.ANY)
    shape = jax.ShapeDtypeStruct
    outs = pl.pallas_call(
        kernel,
        out_shape=(
            shape((ROWS, D), BF),
            shape((ROWS, D), BF),
            shape((1, 12), F32),
            shape((1, 12), F32),
            shape((12, D), F32),
            shape((12, 2 * D), F32),
            shape((12, D), F32),
            shape((1, 12), F32),
            shape((1, 12), F32),
            shape((12, FF), F32),
            shape((1, 48), F32),
            shape((48, D), F32),
        ),
        in_specs=[smem] * 3 + [vmem] + [hbm] * 3 + [vmem] * 5 + [hbm] * 5,
        out_specs=[vmem] * 12,
        scratch_shapes=[pltpu.VMEM(s, t) for s, t in BUFS.values()]
        + [pltpu.SemaphoreType.DMA((N_SEMS,)), pltpu.SemaphoreType.DMA((N_SEMS,))],
        compiler_params=pltpu.CompilerParams(
            collective_id=0, has_side_effects=True, vmem_limit_bytes=64 * 1024 * 1024 - 4096
        ),
    )(
        group_id, ctx_len, fut_len, loss_weight,
        tokens.reshape(ROWS, D), context.reshape(2 * CTX, D), out_cot.reshape(ROWS, D),
        norm_gain1, norm_bias1, norm_gain2, norm_bias2, up_bias,
        w_query[0], w_keyval[0], w_out[0], w_up[0], w_down[0],
    )
    outs = pl.pallas_call(
        deliver,
        out_shape=[
            shape((a.shape[0], 1, a.shape[1]) if a.shape[0] == 12 else a.shape, a.dtype) for a in outs
        ],
        in_specs=[vmem] * 12,
        out_specs=[vmem] * 12,
    )(*outs)
    acts, ins, gg1, gb1, gq, gkv, go, gg2, gb2, gup, gub, gdn = outs
    seqs = (1, 2, SEQ, D)
    rows = [g.reshape(1, 12, g.shape[-1]) for g in (gq, gkv, go, gup)]
    return (
        acts.reshape(seqs), ins.reshape(seqs), gg1, gb1, *rows[:3],
        gg2, gb2, rows[3], gub, gdn[None],
    )


def solution(mesh):
    dp, sec = "dp", "section"
    vec, mat = P(sec, None), P(sec, None, None)
    return jax.shard_map(
        on_device,
        mesh=mesh,
        in_specs=(P(dp, None, None),) * 3 + (P(dp),) * 3 + (P(dp, None),)
        + (vec, vec, mat, mat, mat, vec, vec, mat, vec, mat),
        out_specs=(P(sec, dp, None, None),) * 2 + (P(sec, dp),) * 2 + (P(sec, dp, None),) * 3
        + (P(sec, dp),) * 2 + (P(sec, dp, None), P(sec, dp), P(sec, dp, None)),
        check_vma=False,
    )
```

```python
import math

import jax
import jax.numpy as jnp
from jax import lax
from jax.experimental import pallas as pl
from jax.experimental.pallas import tpu as pltpu
from jax.sharding import PartitionSpec as P

MESH = pl.DeviceIdType.MESH
BF = jnp.bfloat16
F32 = jnp.float32
GROUPS = 8
D = 768
FF = 3072
SEQ = 128
ROWS = 256
CTX = 512
PAIRS = 6
T = 256
GELU_C = math.sqrt(2.0 / math.pi)
GELU_A = 0.044715


def mm(a, b):
    return jnp.dot(a, b, preferred_element_type=F32)


def mm_nt(a, b):
    return lax.dot_general(a, b, (((1,), (1,)), ((), ())), preferred_element_type=F32)


def mm_tn(a, b):
    return lax.dot_general(a, b, (((0,), (0,)), ((), ())), preferred_element_type=F32)


def loop(n, body):
    for i in range(n):
        body(i)


def rows48(i):
    return pl.ds(pl.multiple_of(i * 48, 16), 48)


def tile(i, size=T):
    if isinstance(i, int):
        return slice(i * size, (i + 1) * size)
    return pl.ds(pl.multiple_of(i * size, size), size)


BUFS = dict(
    wq=((D, D), BF),
    wkv=((D, 2 * D), BF),
    wo=((D, D), BF),
    wu=((D, FF), BF),
    wd=((FF, D), BF),
    xb=((ROWS, D), BF),
    ctx=((2 * CTX, D), BF),
    ctxt=((D, 2 * CTX), BF),
    n1=((ROWS, D), BF),
    q=((ROWS, D), BF),
    kv=((2 * CTX, 2 * D), BF),
    p=((2 * PAIRS, ROWS, CTX), BF),
    inv=((ROWS, D), F32),
    o=((ROWS, D), BF),
    s2t=((2, D, ROWS), BF),
    n2=((ROWS, D), BF),
    x2=((ROWS, D), F32),
    xh1=((ROWS, D), F32),
    xh2=((ROWS, D), F32),
    rs=((ROWS, 2), F32),
    gp=((4, ROWS, D), BF),
    hm=((4, ROWS, D), BF),
    dyb=((ROWS, D), BF),
    dx=((ROWS, D), F32),
    d4=((4, ROWS, 384), BF),
    dkvt=((2 * D, 2 * CTX), BF),
    vec=((8, D), F32),
    rvec=((3, 3, 8, D), F32),
    tot=((8, 128), F32),
    rtot=((3, 3, 8, 128), F32),
    b4=((8, D), F32),
    rb4=((8, D), F32),
    wuq=((D, D), BF),
    wdq=((D, D), BF),
    rn=((4 * ROWS, D), BF),
    rnt=((D, 4 * ROWS), BF),
    ry=((4 * ROWS, D), BF),
    hxt=((D, 4 * ROWS), BF),
    gx=((4 * ROWS, D), BF),
    rd1=((3, 4, 48, D), BF),
    hd=((4, 48, D), BF),
    rd2=((4, 48, D), BF),
    ru1=((3, 192, D), BF),
    hu=((4, 4, 16, D), BF),
    ru2=((4, 4, 16, D), BF),
    rxa=((D, 4 * ROWS), BF),
    rxb=((4 * ROWS, 384), BF),
    gq=((4, 192, D), BF),
    rq1=((3, 192, D), BF),
    hq=((4, 4, 16, D), BF),
    rq2=((4, 4, 16, D), BF),
    rk1=((2, 3, 192, D), BF),
    hk=((2, 4, 4, 16, D), BF),
    rk2=((2, 16, 16, D), BF),
)
KEYS = {}
for _name, _n in dict(
    tot=9, act=1, back=1, a=4, n=4, y=4, w=3, b=4, a2=4, b2=4,
    d1=4, d2=4, u1=16, u2=16, q1=4, q2=16, k1=32, k2=32, v=9, load=8,
).items():
    KEYS[_name] = sum(KEYS.values()) if not KEYS else _total
    _total = KEYS[_name] + _n
N_SEMS = _total
NAMES = list(BUFS)


def kernel(*refs):
    (gid, clen, flen, lw, tokens, ctx_in, cot_in, g1, b1, g2, b2, bu, wq_in, wkv_in, wo_in, wu_in, wd_in) = refs[:17]
    (acts, ins, og1, ob1, oq, okv, oo, og2, ob2, oup, oub, odn) = refs[17:29]
    b = dict(zip(NAMES, refs[29 : 29 + len(NAMES)]))
    b["do"] = b["n1"]
    b["dn"] = b["x2"]
    b["pad"] = b["x2"].at[pl.ds(0, 208)]
    b["gd"] = b["gp"].at[:, pl.ds(0, 192)]
    b["gu"] = b["hm"].at[:, pl.ds(0, 192)]
    ssem, rsem = refs[29 + len(NAMES) :]

    sec = lax.axis_index("section")
    dp = lax.axis_index("dp")
    at = {"y": dp // 16, "z": (dp // 4) % 4, "x": dp % 4}
    step = {"y": 16, "z": 4, "x": 1}
    other = 1 - sec

    def peer(axis, r):
        p = lax.rem(at[axis] + r, 4)
        return p, dp + (p - at[axis]) * step[axis]

    def peer2(axis, r, axis2, r2):
        p, to = peer(axis, r)
        p2, to2 = peer(axis2, r2)
        return p, p2, to + to2 - dp

    barrier = pltpu.get_barrier_semaphore()
    pl.semaphore_signal(barrier, inc=1, device_id=(other, dp), device_id_type=MESH)
    near = [peer(axis, r)[1] for axis in "xyz" for r in (1, 2, 3)]
    for axis, axis2 in ("yx", "zx", "yz"):
        near += [peer2(axis, r, axis2, r2)[2] for r in (1, 2, 3) for r2 in (1, 2, 3)]
    for to in near:
        for core in (sec, other):
            pl.semaphore_signal(barrier, inc=1, device_id=(core, to), device_id_type=MESH)

    def branch(mine):
        cross = mine == 0
        group = {0: "y", 1: "z"}
        group_qo = "z" if cross else "x"
        pending = []

        def send(key, i, src, dst, device, slot=None):
            k = KEYS[key] + i
            copy = pltpu.make_async_remote_copy(
                src_ref=src, dst_ref=dst, send_sem=ssem.at[k],
                recv_sem=rsem.at[k if slot is None else KEYS[key] + slot],
                device_id=device, device_id_type=MESH,
            )
            copy.start()
            pending.append(copy)

        def recv(key, i, ref):
            k = KEYS[key] + i
            pltpu.make_async_remote_copy(
                src_ref=ref, dst_ref=ref, send_sem=ssem.at[k], recv_sem=rsem.at[k],
                device_id=(other, dp), device_id_type=MESH,
            ).wait_recv()

        def local(key, i, src, dst):
            copy = pltpu.make_async_copy(src, dst, rsem.at[KEYS[key] + i])
            copy.start()
            return copy

        loads = {}

        def load(name, i, src, dst):
            loads[name] = local("load", i, src, dst)

        if cross:
            load("x", 0, tokens, b["xb"])
            load("wq", 3, wq_in, b["wq"])
            load("ctx", 1, ctx_in, b["ctx"])
            load("wkv", 2, wkv_in, b["wkv"])
        else:
            load("cot", 0, cot_in, b["do"])
            load("wq", 3, wq_in, b["wq"])
            load("wkv", 2, wkv_in, b["wkv"])
        load("wo", 4, wo_in, b["wo"])
        load("wu", 5, wu_in, b["wu"])
        load("wd", 6, wd_in, b["wd"])

        lane = lax.broadcasted_iota(jnp.int32, (1, 128), 1)
        first_head = lane < 64
        mask_a = first_head.astype(F32).astype(BF)
        mask_b = 1.0 - mask_a

        def stacked(v):
            return jnp.concatenate([v * mask_a, v * mask_b], axis=0)

        def merged(v):
            return jnp.where(first_head, v[:SEQ], v[SEQ:])

        def norm(src, gain, bias, xh, rs, n, nt):
            def body(i):
                rows = tile(i, 32)
                v = src[rows, :].astype(F32)
                centre = v - jnp.mean(v, axis=-1, keepdims=True)
                spread = jnp.mean(centre * centre, axis=-1, keepdims=True)
                scale = lax.rsqrt(spread + 1e-05)
                hat = centre * scale
                xh[rows, :] = hat
                b["rs"][rows, rs : rs + 1] = scale
                n[rows, :] = (hat * gain[...] + bias[...]).astype(BF)

            loop(8, body)
            if nt is not None:
                for j in range(3):
                    nt[j * T : (j + 1) * T, :] = n[:, j * T : (j + 1) * T].T

        def norm_back(xh, rs, gain, row, done):
            def body(i, carry):
                sum_g, sum_b = carry
                rows = tile(i, 32)
                grad = b["dn"][rows, :]
                hat = xh[rows, :]
                sum_g = sum_g + (grad * hat).reshape(4, 8, D).sum(0)
                sum_b = sum_b + grad.reshape(4, 8, D).sum(0)
                scaled = grad * gain[...]
                mean = jnp.mean(scaled, axis=-1, keepdims=True)
                along = jnp.mean(scaled * hat, axis=-1, keepdims=True)
                done(rows, b["dx"][rows, :] + b["rs"][rows, rs : rs + 1] * (scaled - mean - hat * along))
                return sum_g, sum_b

            sums = (jnp.zeros((8, D), F32),) * 2
            for i in range(8):
                sums = body(i, sums)
            sum_g, sum_b = sums
            b["vec"][row : row + 1, :] = sum_g.sum(0, keepdims=True)
            b["vec"][row + 1 : row + 2, :] = sum_b.sum(0, keepdims=True)

        def gather_to(axis, key, src_of, dst_of, core):
            for r in (1, 3, 2):
                p, to = peer(axis, r)
                send(key, r, src_of(p), dst_of(r), (core, to))
            if core is other:
                send(key, 0, src_of(at[axis]), dst_of(0), (core, dp))
                return None
            return local(key, 0, src_of(at[axis]), dst_of(0))

        def cols(ref):
            return lambda r: ref.at[:, pl.ds(r * ROWS, ROWS)]

        def rows_of(ref):
            return lambda r: ref.at[pl.ds(r * ROWS, ROWS)]

        def scatter(axis, key, src_of, dst_of, base=0, core=sec):
            for r in (1, 3, 2):
                p, to = peer(axis, r)
                send(key, base + r, src_of(p), dst_of(r - 1), (core, to))

        def scatter48(axis, key, src_of, dst_of, base=0):
            for r in (1, 3, 2):
                p, to = peer(axis, r)
                for i in range(4):
                    send(key, base + 4 * r + i, src_of(p, i), dst_of(r - 1).at[tile(i, 48)], (sec, to))

        def recv48(key, dst_of, base=0):
            for r in (1, 3, 2):
                for i in range(4):
                    recv(key, base + 4 * r + i, dst_of(r - 1).at[tile(i, 48)])

        def recv3(key, dst_of, base=0):
            for r in (1, 3, 2):
                recv(key, base + r, dst_of(r - 1))

        def send_quarter():
            q = at[group[mine]]
            for k in range(4):
                b["b4"][k : k + 1, :] = bu[:, k * D : (k + 1) * D]
            b["b4"][4:8, :] = jnp.zeros((4, D), F32)
            send("w", 0, b["b4"], b["rb4"], (other, dp))
            loads["wu"].wait()
            send("w", 1, b["wu"].at[:, tile(q, D)], b["wuq"], (other, dp))
            loads["wd"].wait()
            send("w", 2, b["wd"].at[tile(q, D), :], b["wdq"], (other, dp))

        if not cross:
            weighted, ids = [], []
            total = jnp.zeros((1, 128), F32)
            for s in range(2):
                w = jnp.where(lane < flen[s], lw[s : s + 1, :].astype(F32), 0.0)
                total = total + jnp.where(lane == gid[s], jnp.sum(w, axis=1, keepdims=True), 0.0)
                weighted.append(w)
            b["tot"][...] = jnp.broadcast_to(total, (8, 128))
        pl.semaphore_wait(barrier, 1 + 2 * len(near))
        if not cross:
            for a, axis in enumerate("xyz"):
                for r in (1, 2, 3):
                    _, to = peer(axis, r)
                    send("tot", 3 * a + r - 1, b["tot"], b["rtot"].at[a, r - 1], (sec, to))
                for r in (1, 2, 3):
                    recv("tot", 3 * a + r - 1, b["rtot"].at[a, r - 1])
                for copy in pending:
                    copy.wait_send()
                pending.clear()
                b["tot"][...] += b["rtot"][a, 0] + b["rtot"][a, 1] + b["rtot"][a, 2]
            totals = b["tot"][0:1, :]
            every = jnp.sum(totals, axis=1, keepdims=True)
            factors = every / (GROUPS * jnp.maximum(totals, 1.0))
            loads["cot"].wait()
            diagonal = lax.broadcasted_iota(jnp.int32, (SEQ, SEQ), 0) == lax.broadcasted_iota(
                jnp.int32, (SEQ, SEQ), 1
            )
            for s in range(2):
                factor = jnp.sum(jnp.where(lane == gid[s], factors, 0.0), axis=1, keepdims=True)
                picked = jnp.where(diagonal, weighted[s], 0.0).astype(BF)
                rows = slice(s * SEQ, (s + 1) * SEQ)
                grad = mm(picked, b["do"][rows, :]) * factor
                b["dx"][rows, :] = grad
                b["dyb"][rows, :] = grad.astype(BF)
            gather_to(group[1], "y", lambda p: b["dyb"], rows_of(b["ry"]), other)
            send_quarter()

        if cross:
            loads["x"].wait()
        else:
            recv("act", 0, b["xb"])
        norm(b["xb"], g1, b1, b["xh1"], 0, b["n1"], b["s2t"].at[0])

        loads["wq"].wait()

        def query(i):
            b["q"][:, tile(i)] = (mm(b["n1"][...], b["wq"][:, tile(i)]).astype(BF) * 0.125).astype(BF)

        loop(3, query)

        loads["wkv"].wait()
        if cross:
            loads["ctx"].wait()

            def keyval(i):
                for m in range(4):
                    rows = slice(m * T, (m + 1) * T)
                    b["kv"][rows, tile(i)] = mm(b["ctx"][rows, :], b["wkv"][:, tile(i)]).astype(BF)
        else:

            def keyval(i):
                b["kv"][0:ROWS, tile(i)] = mm(b["n1"][...], b["wkv"][:, tile(i)]).astype(BF)

        loop(6, keyval)
        keys = CTX if cross else SEQ

        def blocks(i):
            s, j = i // PAIRS, i % PAIRS
            vcols = slice(D + 128 * j, D + 128 * (j + 1))
            return s, j, tile(s, SEQ), tile(s, keys), tile(j, 128), vcols

        if cross:
            key = lax.broadcasted_iota(jnp.int32, (1, keys), 1)
            masks = [jnp.where(key < clen[s], 0.0, -1e9) for s in range(2)]
        else:
            row = lax.broadcasted_iota(jnp.int32, (SEQ, keys), 0)
            mask = jnp.where(lax.broadcasted_iota(jnp.int32, (SEQ, keys), 1) <= row, 0.0, -1e9)
            masks = [jnp.concatenate([mask, mask], axis=0)] * 2
        ones = jnp.ones((keys, 128), BF)

        def attend(i):
            s, j, rows, krows, kcols, vcols = blocks(i)
            scores = mm_nt(stacked(b["q"][rows, kcols]), b["kv"][krows, kcols]) + masks[s]
            e = jnp.exp(scores - jnp.max(scores, axis=-1, keepdims=True))
            values = b["kv"][krows, vcols]
            if cross:
                e = e.astype(BF)
                b["p"][i] = e
                mixed = mm(e, jnp.concatenate([values, ones], axis=1))
                scale = 1.0 / merged(mixed[:, 128:])
                b["inv"][rows, kcols] = scale
                b["o"][rows, kcols] = (merged(mixed[:, :128]) * scale).astype(BF)
            else:
                probs = (e / jnp.sum(e, axis=-1, keepdims=True)).astype(BF)
                b["p"][i, :, 0:keys] = probs
                b["o"][rows, kcols] = merged(mm(probs, values)).astype(BF)

        loop(2 * PAIRS, attend)
        for j in range(3):
            b["s2t"][1, j * T : (j + 1) * T, :] = b["o"][:, j * T : (j + 1) * T].T
        own_a = gather_to(group_qo, "a", lambda p: b["s2t"].at[p // 2], cols(b["rxa"]), sec)
        if not cross:
            own_a2 = gather_to(group_qo, "a2", lambda p: b["s2t"].at[0], cols(b["ctxt"]), sec)

        loads["wo"].wait()

        def project(i):
            b["x2"][:, tile(i)] = b["xb"][:, tile(i)].astype(F32) + mm(b["o"][...], b["wo"][:, tile(i)])

        loop(3, project)
        norm(b["x2"], g2, b2, b["xh2"], 1, b["n2"], None)
        gather_to(group[mine], "n", lambda p: b["n2"], rows_of(b["rn"]), other)
        if cross:
            send_quarter()

        def gelu(u):
            square = u * u
            th = jnp.tanh(u * (GELU_C + (GELU_C * GELU_A) * square))
            half = 0.5 + 0.5 * th
            slope = half + (u * (0.5 - 0.5 * th * th)) * (GELU_C + (3.0 * GELU_A * GELU_C) * square)
            return (u * half).astype(BF), slope.astype(BF)

        def up(i):
            u = mm(b["n2"][...], b["wu"][:, tile(i)]) + bu[:, tile(i)]
            k, at_cols = i // 3, tile(i % 3)
            b["hm"][k, :, at_cols], b["gp"][k, :, at_cols] = gelu(u)

        loop(12, up)

        def down(i):
            y = b["x2"][:, tile(i)]
            for k in range(4):
                y = y + mm(b["hm"][k], b["wd"][k * D : (k + 1) * D, tile(i)])
            acts[:, tile(i)] = y.astype(BF)

        loop(3, down)
        if cross:
            send("act", 0, acts, b["xb"], (other, dp))

        def add4(own, parts):
            total = own.astype(F32)
            for part in parts:
                total = total + part.astype(F32)
            return total

        def plane(key, axis, src_of, dst, base=0, core=sec):
            for r in (1, 3, 2, 0):
                for r2 in (1, 3, 2, 0):
                    if r or r2 or core is other:
                        p, p2, to = peer2(axis, r, "x", r2)
                        send(key, base + 4 * r + r2, src_of(p, p2), dst(r, r2), (core, to))

        def recv_plane(key, ref, base=0, first=1):
            for i in range(first, 16):
                recv(key, base + i, ref)

        def cut(dst, cols):
            for k in range(4):
                for j in range(4):
                    start = 48 * k + 12 * j
                    dst[k, j, :, cols] = b["pad"][start : start + 16, cols].astype(BF)

        full = slice(0, D)

        theirs = 1 - mine

        def ffn_forward():
            for i, name in enumerate(("rb4", "wuq", "wdq")):
                recv("w", i, b[name])
            for r in range(4):
                recv("n", r, rows_of(b["rn"])(r))
            bias = b["rb4"][pl.ds(at[group[theirs]], 1), :]
            for m in range(4):
                for i in range(3):
                    u = mm(b["rn"][tile(m), :], b["wuq"][:, tile(i)]) + bias[:, tile(i)]
                    hidden, b["gx"][tile(m), tile(i)] = gelu(u)
                    b["hxt"][tile(i), tile(m)] = hidden.T
                    b["rnt"][tile(i), tile(m)] = b["rn"][tile(m), tile(i)].T

        def down_a():
            for r in range(4):
                recv("y", r, rows_of(b["ry"])(r))
            for i in range(3):
                v = mm(b["hxt"][...], b["ry"][:, tile(i)]).astype(BF)
                b["gd"][:, :, tile(i)] = v.reshape(4, 192, T)
            scatter("x", "d1", lambda p: b["gd"].at[:, rows48(p)], lambda r: b["rd1"].at[r])

        def down_b():
            recv3("d1", lambda r: b["rd1"].at[r])
            for i in range(4):
                b["hd"][i] = add4(b["gd"][i, rows48(at["x"])], [b["rd1"][r, i] for r in range(3)]).astype(BF)
            if theirs == 0:
                for r in (1, 3, 2, 0):
                    p, to = peer("z", r)
                    send("d2", r, b["hd"].at[p], b["rd2"].at[r], (other, to))
            else:
                to = dp + (at["z"] - at["y"]) * step["y"]
                for r in (1, 3, 2, 0):
                    p, there = peer("z", r)
                    send("d2", r, b["hd"].at[p], b["rd2"].at[at["y"]], (other, to + there - dp), at["y"])

        def down_end():
            for r in range(4):
                recv("d2", r, b["rd2"].at[r])
            odn[...] = add4(b["rd2"][0], [b["rd2"][r] for r in (1, 2, 3)])

        def up_axes(layer):
            return ("y", "z") if layer == 1 else ("z", "y")

        def up_a():
            axis = up_axes(theirs)[0]
            for m in range(4):
                for i in range(3):
                    grad = mm_nt(b["ry"][tile(m), :], b["wdq"][tile(i), :])
                    b["gx"][tile(m), tile(i)] = (b["gx"][tile(m), tile(i)].astype(F32) * grad).astype(BF)
            for i in range(3):
                v = mm(b["rnt"][...], b["gx"][:, tile(i)]).astype(BF)
                b["gu"][:, :, tile(i)] = v.reshape(4, 192, T)
            if axis == "y":
                scatter(axis, "u1", lambda p: b["gu"].at[p], lambda r: b["ru1"].at[r])
            else:
                scatter48(axis, "u1", lambda p, i: b["gu"].at[i, rows48(p)], lambda r: b["ru1"].at[r])

        def up_b():
            axis, rest = up_axes(theirs)
            (recv3 if axis == "y" else recv48)("u1", lambda r: b["ru1"].at[r])
            for i in range(4):
                if axis == "y":
                    own, parts = b["gu"][at["y"], tile(i, 48)], [b["ru1"][r, tile(i, 48)] for r in range(3)]
                else:
                    own, parts = b["gu"][i, rows48(at["z"])], [b["ru1"][r, tile(i, 48)] for r in range(3)]
                b["pad"][tile(i, 48), :] = add4(own, parts)
            cut(b["hu"], full)
            plane(
                "u2", rest, lambda p, p2: b["hu"].at[p, p2],
                lambda r, r2: b["ru2"].at[at[rest], r2], core=other,
            )

        def up_end():
            recv_plane("u2", b["ru2"].at[0, 0], first=0)
            for k in range(4):
                total = add4(b["ru2"][k, 0], [b["ru2"][k, r] for r in (1, 2, 3)])
                oup[:, k * D : (k + 1) * D] = total[:12]

        width = 384 if cross else D
        part = slice(0, width)

        def qo_a():
            own_a.wait()
            own_b.wait()
            for r in range(1, 4):
                recv("a", r, cols(b["rxa"])(r))
                recv("b", r, rows_of(b["rxb"])(r))
            if not cross:
                own_a2.wait()
                own_b2.wait()
                for r in range(1, 4):
                    recv("a2", r, cols(b["ctxt"])(r))
                    recv("b2", r, b["dkvt"].at[pl.ds(r * ROWS, ROWS), pl.ds(0, 384)])
            for i in range(2):
                rows = tile(i, 384)
                v = mm(b["rxa"][rows, :], b["rxb"][...]).astype(BF)
                b["gq"][2 * i : 2 * i + 2, :, 0:384] = v.reshape(2, 192, 384)
                if not cross:
                    v = mm(b["ctxt"][rows, :], b["dkvt"][0:1024, 0:384]).astype(BF)
                    b["gq"][2 * i : 2 * i + 2, :, 384:768] = v.reshape(2, 192, 384)
            scatter("y", "q1", lambda p: b["gq"].at[p, :, pl.ds(0, width)], lambda r: b["rq1"].at[r, :, pl.ds(0, width)])

        def qo_b():
            recv3("q1", lambda r: b["rq1"].at[r, :, pl.ds(0, width)])
            for i in range(4):
                rows = tile(i, 48)
                b["pad"][rows, part] = add4(b["gq"][at["y"], rows, part], [b["rq1"][r, rows, part] for r in range(3)])
            cut(b["hq"], part)
            if cross:
                slot = lambda r, r2: b["rq2"].at[at["z"], r2, :, pl.ds(0, width)]
            else:
                slot = lambda r, r2: b["rq2"].at[at["x"], r, :, pl.ds(0, width)]
            plane("q2", "z", lambda p, p2: b["hq"].at[p, p2, :, pl.ds(0, width)], slot)
            b["rq2"][at[group_qo], 0, :, part] = b["hq"][at["z"], at["x"], :, part]

        def qo_end():
            recv_plane("q2", b["rq2"].at[0, 0, :, pl.ds(0, width)])

            def total(k, at_cols):
                return add4(b["rq2"][k, 0, :, at_cols], [b["rq2"][k, r, :, at_cols] for r in (1, 2, 3)])[:12]

            for k in range(2):
                oq[:, 384 * k : 384 * (k + 1)] = total(k, slice(0, 384))
                oo[:, 384 * k : 384 * (k + 1)] = total(2 + k, slice(0, 384))
            if not cross:
                for k in range(4):
                    okv[:, 384 * k : 384 * (k + 1)] = total(k, slice(384, D))

        def kv_a(h):
            for i in range(3):
                v = mm_nt(b["ctxt"][...], b["dkvt"][tile(3 * h + i), :]).astype(BF)
                b["kv"][0:D, tile(3 * h + i)] = v
            if h:
                scatter("y", "k1", lambda p: b["kv"].at[tile(p, 192), D:], lambda r: b["rk1"].at[1, r])
            else:
                scatter48("z", "k1", lambda p, i: b["kv"].at[rows48(4 * i + p), 0:D], lambda r: b["rk1"].at[0, r], 16)

        def kv_b(h):
            if h:
                recv3("k1", lambda r: b["rk1"].at[1, r])
            else:
                recv48("k1", lambda r: b["rk1"].at[0, r], 16)
            for i in range(4):
                m = 4 * at["y"] + i if h else 4 * i + at["z"]
                own = b["kv"][rows48(m), h * D : (h + 1) * D]
                b["pad"][tile(i, 48), :] = add4(own, [b["rk1"][h, r, tile(i, 48)] for r in range(3)])
            cut(b["hk"].at[h], full)
            axis = "z" if h else "y"
            plane(
                "k2", axis, lambda p, p2: b["hk"].at[h, p, p2],
                lambda r, r2: b["rk2"].at[h, 4 * r + r2], 16 * h,
            )
            b["rk2"][h, 0] = b["hk"][h, at[axis], at["x"]]

        def kv_end(h):
            recv_plane("k2", b["rk2"].at[h, 1], 16 * h)
            total = add4(b["rk2"][h, 0], [b["rk2"][h, i] for i in range(1, 16)])
            okv[:, h * D : (h + 1) * D] = total[:12]

        vec_copies = []

        def vec_send(a):
            for r in (1, 2, 3):
                _, to = peer("xyz"[a], r)
                send("v", 3 * a + r - 1, b["vec"], b["rvec"].at[a, r - 1], (sec, to))
                vec_copies.append(pending.pop())

        def vec_add(a):
            for r in (1, 2, 3):
                recv("v", 3 * a + r - 1, b["rvec"].at[a, r - 1])
            for copy in vec_copies:
                copy.wait_send()
            vec_copies.clear()
            b["vec"][...] += b["rvec"][a, 0] + b["rvec"][a, 1] + b["rvec"][a, 2]

        def vec_out():
            shift = lax.rem(D - 12 * dp, D)
            rolled = pltpu.roll(b["vec"][...], shift, axis=1)
            for row, out in enumerate((og1, ob1, og2, ob2)):
                out[...] = rolled[row : row + 1, 0:12]
            bias_row = b["vec"][pl.ds(4 + at["y"], 1), :]
            shift = lax.rem(D - 48 * lax.rem(dp, 16), D)
            rolled = pltpu.roll(jnp.broadcast_to(bias_row, (8, D)), shift, axis=1)
            oub[...] = rolled[0:1, 0:48]

        if cross:
            for j in range(3):
                for m in range(4):
                    rows, at_cols = slice(m * T, (m + 1) * T), slice(j * T, (j + 1) * T)
                    b["ctxt"][at_cols, rows] = b["ctx"][rows, at_cols].T
        if cross:
            recv("back", 0, b["dyb"])
            b["dx"][...] = b["dyb"][...].astype(F32)
            gather_to(group[0], "y", lambda p: b["dyb"], rows_of(b["ry"]), other)

        for k in range(4):

            def up_back(i):
                grad = mm_nt(b["dyb"][...], b["wd"][tile(3 * k + i), :])
                du = (b["gp"][k, :, tile(i)].astype(F32) * grad).astype(BF)
                b["gp"][k, :, tile(i)] = du
                b["vec"][4 + k : 5 + k, tile(i)] = jnp.sum(du.astype(F32), axis=0, keepdims=True)

            loop(3, up_back)

        def n2_back(i):
            grad = jnp.zeros((ROWS, T), F32)
            for k in range(4):
                grad = grad + mm_nt(b["gp"][k], b["wu"][tile(i), k * D : (k + 1) * D])
            b["dn"][:, tile(i)] = grad

        loop(3, n2_back)

        def done2(rows, value):
            b["dx"][rows, :] = value
            rounded = value.astype(BF)
            b["d4"][2, rows, :] = rounded[:, 0:384]
            b["d4"][3, rows, :] = rounded[:, 384:768]

        norm_back(b["xh2"], 1, g2, 2, done2)

        def out_back(i):
            rows = tile(i)
            grad = mm_nt(b["d4"][2], b["wo"][rows, 0:384]) + mm_nt(b["d4"][3], b["wo"][rows, 384:768])
            b["do"][:, tile(i)] = grad.astype(BF)

        loop(3, out_back)

        def attend_back(i):
            s, j, rows, krows, kcols, vcols = blocks(i)
            k2, v2 = b["kv"][krows, kcols], b["kv"][krows, vcols]
            q2 = stacked(b["q"][rows, kcols])
            probs = b["p"][i, :, 0:keys]
            grad = b["do"][rows, kcols].astype(F32)
            if cross:
                grad = grad * b["inv"][rows, kcols]
            along = grad * b["o"][rows, kcols].astype(F32)
            along = jnp.concatenate([jnp.where(first_head, along, 0.0), jnp.where(first_head, 0.0, along)], axis=0)
            along = jnp.sum(along, axis=-1, keepdims=True)
            do2 = stacked(grad.astype(BF))
            ds = (probs.astype(F32) * (mm_nt(do2, v2) - along)).astype(BF)
            half, at_cols = j // 3, tile(j % 3, 128)
            b["d4"][half, rows, at_cols] = (merged(mm(ds, k2)) * 0.125).astype(BF)
            if cross:
                b["dkvt"][tile(j, 128), krows] = mm_tn(q2, ds).astype(BF)
                b["dkvt"][vcols, krows] = mm_tn(do2, probs).astype(BF)
            else:
                b["ctx"][tile(2 * half + s, SEQ), at_cols] = mm_tn(ds, q2).astype(BF)
                b["ctx"][tile(4 + 2 * half + s, SEQ), at_cols] = mm_tn(probs, do2).astype(BF)

        loop(2 * PAIRS, attend_back)
        own_b = gather_to(group_qo, "b", lambda p: b["d4"].at[p], rows_of(b["rxb"]), sec)
        if not cross:

            def kv_quarter(p):
                return b["ctx"].at[tile(p, ROWS), pl.ds(0, 384)]

            own_b2 = gather_to(
                group_qo, "b2", kv_quarter, lambda r: b["dkvt"].at[pl.ds(r * ROWS, ROWS), pl.ds(0, 384)], sec
            )

        if cross:
            kv_a(0)
            kv_a(1)

        def n1_back(i):
            rows = tile(i)
            grad = mm_nt(b["d4"][0], b["wq"][rows, 0:384]) + mm_nt(b["d4"][1], b["wq"][rows, 384:768])
            if not cross:
                for k in range(4):
                    quarter = b["ctx"][k * ROWS : (k + 1) * ROWS, 0:384]
                    grad = grad + mm_nt(quarter, b["wkv"][rows, 384 * k : 384 * (k + 1)])
            b["dn"][:, tile(i)] = grad

        loop(3, n1_back)

        def done1(rows, value):
            ins[rows, :] = value.astype(BF)

        norm_back(b["xh1"], 0, g1, 0, done1)
        if not cross:
            send("back", 0, ins, b["dyb"], (other, dp))

        vec_send(0)
        if cross:
            ffn_forward()
            down_a()
            up_a()
            vec_add(0)
            vec_send(1)
            qo_a()
            kv_b(0)
            kv_b(1)
            vec_add(1)
            vec_send(2)
            down_b()
            up_b()
            qo_b()
            vec_add(2)
            vec_out()
            kv_end(0)
            kv_end(1)
        else:
            ffn_forward()
            qo_a()
            vec_add(0)
            vec_send(1)
            down_a()
            up_a()
            vec_add(1)
            vec_send(2)
            qo_b()
            down_b()
            up_b()
            vec_add(2)
            vec_out()
        qo_end()
        down_end()
        up_end()
        for copy in pending:
            copy.wait_send()

    pl.when(sec == 0)(lambda: branch(0))
    pl.when(sec == 1)(lambda: branch(1))


def deliver(*refs):
    for a, out in zip(refs[:12], refs[12:]):
        out[...] = a[...].reshape(out.shape)


def on_device(
    tokens, context, out_cot, group_id, ctx_len, fut_len, loss_weight,
    norm_gain1, norm_bias1, w_query, w_keyval, w_out,
    norm_gain2, norm_bias2, w_up, up_bias, w_down,
):
    smem = pl.BlockSpec(memory_space=pltpu.SMEM)
    vmem = pl.BlockSpec(memory_space=pltpu.VMEM)
    hbm = pl.BlockSpec(memory_space=pl.ANY)
    shape = jax.ShapeDtypeStruct
    outs = pl.pallas_call(
        kernel,
        out_shape=(
            shape((ROWS, D), BF),
            shape((ROWS, D), BF),
            shape((1, 12), F32),
            shape((1, 12), F32),
            shape((12, D), F32),
            shape((12, 2 * D), F32),
            shape((12, D), F32),
            shape((1, 12), F32),
            shape((1, 12), F32),
            shape((12, FF), F32),
            shape((1, 48), F32),
            shape((48, D), F32),
        ),
        in_specs=[smem] * 3 + [vmem] + [hbm] * 3 + [vmem] * 5 + [hbm] * 5,
        out_specs=[vmem] * 12,
        scratch_shapes=[pltpu.VMEM(s, t) for s, t in BUFS.values()]
        + [pltpu.SemaphoreType.DMA((N_SEMS,)), pltpu.SemaphoreType.DMA((N_SEMS,))],
        compiler_params=pltpu.CompilerParams(
            collective_id=0, has_side_effects=True, vmem_limit_bytes=64 * 1024 * 1024 - 4096
        ),
    )(
        group_id, ctx_len, fut_len, loss_weight,
        tokens.reshape(ROWS, D), context.reshape(2 * CTX, D), out_cot.reshape(ROWS, D),
        norm_gain1, norm_bias1, norm_gain2, norm_bias2, up_bias,
        w_query[0], w_keyval[0], w_out[0], w_up[0], w_down[0],
    )
    outs = pl.pallas_call(
        deliver,
        out_shape=[
            shape((a.shape[0], 1, a.shape[1]) if a.shape[0] == 12 else a.shape, a.dtype) for a in outs
        ],
        in_specs=[vmem] * 12,
        out_specs=[vmem] * 12,
    )(*outs)
    acts, ins, gg1, gb1, gq, gkv, go, gg2, gb2, gup, gub, gdn = outs
    seqs = (1, 2, SEQ, D)
    rows = [g.reshape(1, 12, g.shape[-1]) for g in (gq, gkv, go, gup)]
    return (
        acts.reshape(seqs), ins.reshape(seqs), gg1, gb1, *rows[:3],
        gg2, gb2, rows[3], gub, gdn[None],
    )


def solution(mesh):
    dp, sec = "dp", "section"
    vec, mat = P(sec, None), P(sec, None, None)
    return jax.shard_map(
        on_device,
        mesh=mesh,
        in_specs=(P(dp, None, None),) * 3 + (P(dp),) * 3 + (P(dp, None),)
        + (vec, vec, mat, mat, mat, vec, vec, mat, vec, mat),
        out_specs=(P(sec, dp, None, None),) * 2 + (P(sec, dp),) * 2 + (P(sec, dp, None),) * 3
        + (P(sec, dp),) * 2 + (P(sec, dp, None), P(sec, dp), P(sec, dp, None)),
        check_vma=False,
    )
```

```python
import math

import jax
import jax.numpy as jnp
from jax import lax
from jax.experimental import pallas as pl
from jax.experimental.pallas import tpu as pltpu
from jax.sharding import PartitionSpec as P

MESH = pl.DeviceIdType.MESH
BF = jnp.bfloat16
F32 = jnp.float32
GROUPS = 8
D = 768
FF = 3072
SEQ = 128
ROWS = 256
CTX = 512
PAIRS = 6
T = 256
GELU_C = math.sqrt(2.0 / math.pi)
GELU_A = 0.044715


def mm(a, b):
    return jnp.dot(a, b, preferred_element_type=F32)


def mm_nt(a, b):
    return lax.dot_general(a, b, (((1,), (1,)), ((), ())), preferred_element_type=F32)


def mm_tn(a, b):
    return lax.dot_general(a, b, (((0,), (0,)), ((), ())), preferred_element_type=F32)


def loop(n, body):
    for i in range(n):
        body(i)


def rows48(i):
    return pl.ds(pl.multiple_of(i * 48, 16), 48)


def tile(i, size=T):
    if isinstance(i, int):
        return slice(i * size, (i + 1) * size)
    return pl.ds(pl.multiple_of(i * size, size), size)


BUFS = dict(
    wq=((D, D), BF),
    wkv=((D, 2 * D), BF),
    wo=((D, D), BF),
    wu=((D, FF), BF),
    wd=((FF, D), BF),
    xb=((ROWS, D), BF),
    ctx=((2 * CTX, D), BF),
    ctxt=((D, 2 * CTX), BF),
    n1=((ROWS, D), BF),
    q=((ROWS, D), BF),
    kv=((2 * CTX, 2 * D), BF),
    p=((2 * PAIRS, ROWS, CTX), BF),
    inv=((ROWS, D), F32),
    o=((ROWS, D), BF),
    s2t=((2, D, ROWS), BF),
    n2=((ROWS, D), BF),
    x2=((ROWS, D), F32),
    xh1=((ROWS, D), F32),
    xh2=((ROWS, D), F32),
    rs=((ROWS, 2), F32),
    gp=((4, ROWS, D), BF),
    hm=((4, ROWS, D), BF),
    dyb=((ROWS, D), BF),
    dx=((ROWS, D), F32),
    d4=((4, ROWS, 384), BF),
    dkvt=((2 * D, 2 * CTX), BF),
    vec=((8, D), F32),
    rvec=((3, 3, 8, D), F32),
    tot=((8, 128), F32),
    rtot=((3, 3, 8, 128), F32),
    b4=((8, D), F32),
    rb4=((8, D), F32),
    wuq=((D, D), BF),
    wdq=((D, D), BF),
    rn=((4 * ROWS, D), BF),
    rnt=((D, 4 * ROWS), BF),
    ry=((4 * ROWS, D), BF),
    hxt=((D, 4 * ROWS), BF),
    gx=((4 * ROWS, D), BF),
    rd1=((3, 4, 48, D), BF),
    hd=((4, 48, D), BF),
    rd2=((4, 48, D), BF),
    ru1=((3, 192, D), BF),
    hu=((4, 4, 16, D), BF),
    ru2=((4, 4, 16, D), BF),
    rxa=((D, 4 * ROWS), BF),
    rxb=((4 * ROWS, 384), BF),
    gq=((4, 192, D), BF),
    rq1=((3, 192, D), BF),
    hq=((4, 4, 16, D), BF),
    rq2=((4, 4, 16, D), BF),
    rk1=((2, 3, 192, D), BF),
    hk=((2, 4, 4, 16, D), BF),
    rk2=((2, 16, 16, D), BF),
)
KEYS = {}
for _name, _n in dict(
    tot=9, act=1, back=1, a=4, n=4, y=4, w=3, b=4, a2=4, b2=4,
    d1=4, d2=4, u1=16, u2=16, q1=4, q2=16, k1=32, k2=32, v=9, load=8,
).items():
    KEYS[_name] = sum(KEYS.values()) if not KEYS else _total
    _total = KEYS[_name] + _n
N_SEMS = _total
NAMES = list(BUFS)


def kernel(*refs):
    (gid, clen, flen, lw, tokens, ctx_in, cot_in, g1, b1, g2, b2, bu, wq_in, wkv_in, wo_in, wu_in, wd_in) = refs[:17]
    (acts, ins, og1, ob1, oq, okv, oo, og2, ob2, oup, oub, odn) = refs[17:29]
    b = dict(zip(NAMES, refs[29 : 29 + len(NAMES)]))
    b["do"] = b["n1"]
    b["dn"] = b["x2"]
    b["pad"] = b["x2"].at[pl.ds(0, 208)]
    b["gd"] = b["gp"].at[:, pl.ds(0, 192)]
    b["gu"] = b["hm"].at[:, pl.ds(0, 192)]
    ssem, rsem = refs[29 + len(NAMES) :]

    sec = lax.axis_index("section")
    dp = lax.axis_index("dp")
    at = {"y": dp // 16, "z": (dp // 4) % 4, "x": dp % 4}
    step = {"y": 16, "z": 4, "x": 1}
    other = 1 - sec

    def peer(axis, r):
        p = lax.rem(at[axis] + r, 4)
        return p, dp + (p - at[axis]) * step[axis]

    def peer2(axis, r, axis2, r2):
        p, to = peer(axis, r)
        p2, to2 = peer(axis2, r2)
        return p, p2, to + to2 - dp

    barrier = pltpu.get_barrier_semaphore()
    pl.semaphore_signal(barrier, inc=1, device_id=(other, dp), device_id_type=MESH)
    near = [peer(axis, r)[1] for axis in "xyz" for r in (1, 2, 3)]
    for axis, axis2 in ("yx", "zx", "yz"):
        near += [peer2(axis, r, axis2, r2)[2] for r in (1, 2, 3) for r2 in (1, 2, 3)]
    for to in near:
        for core in (sec, other):
            pl.semaphore_signal(barrier, inc=1, device_id=(core, to), device_id_type=MESH)

    def branch(mine):
        cross = mine == 0
        group = {0: "y", 1: "z"}
        group_qo = "z" if cross else "x"
        pending = []

        def send(key, i, src, dst, device, slot=None, when=None):
            k = KEYS[key] + i
            copy = pltpu.make_async_remote_copy(
                src_ref=src, dst_ref=dst, send_sem=ssem.at[k],
                recv_sem=rsem.at[k if slot is None else KEYS[key] + slot],
                device_id=device, device_id_type=MESH,
            )
            if when is None:
                copy.start()
                pending.append(copy.wait_send)
            else:
                pl.when(when)(copy.start)
                pending.append(lambda: pl.when(when)(copy.wait_send))

        def recv(key, i, ref):
            k = KEYS[key] + i
            pltpu.make_async_remote_copy(
                src_ref=ref, dst_ref=ref, send_sem=ssem.at[k], recv_sem=rsem.at[k],
                device_id=(other, dp), device_id_type=MESH,
            ).wait_recv()

        def local(key, i, src, dst):
            copy = pltpu.make_async_copy(src, dst, rsem.at[KEYS[key] + i])
            copy.start()
            return copy

        loads = {}

        def load(name, i, src, dst):
            loads[name] = local("load", i, src, dst)

        if cross:
            load("x", 0, tokens, b["xb"])
            load("wq", 3, wq_in, b["wq"])
            load("ctx", 1, ctx_in, b["ctx"])
            load("wkv", 2, wkv_in, b["wkv"])
        else:
            load("cot", 0, cot_in, b["do"])
            load("wq", 3, wq_in, b["wq"])
            load("wkv", 2, wkv_in, b["wkv"])
        load("wo", 4, wo_in, b["wo"])
        load("wu", 5, wu_in, b["wu"])
        load("wd", 6, wd_in, b["wd"])

        lane = lax.broadcasted_iota(jnp.int32, (1, 128), 1)
        first_head = lane < 64
        mask_a = first_head.astype(F32).astype(BF)
        mask_b = 1.0 - mask_a

        def stacked(v):
            return jnp.concatenate([v * mask_a, v * mask_b], axis=0)

        def merged(v):
            return jnp.where(first_head, v[:SEQ], v[SEQ:])

        def norm(src, gain, bias, xh, rs, n, nt):
            def body(i):
                rows = tile(i, 32)
                v = src[rows, :].astype(F32)
                centre = v - jnp.mean(v, axis=-1, keepdims=True)
                spread = jnp.mean(centre * centre, axis=-1, keepdims=True)
                scale = lax.rsqrt(spread + 1e-05)
                hat = centre * scale
                xh[rows, :] = hat
                b["rs"][rows, rs : rs + 1] = scale
                n[rows, :] = (hat * gain[...] + bias[...]).astype(BF)

            loop(8, body)
            if nt is not None:
                for j in range(3):
                    nt[j * T : (j + 1) * T, :] = n[:, j * T : (j + 1) * T].T

        def norm_back(xh, rs, gain, row, done):
            def body(i, carry):
                sum_g, sum_b = carry
                rows = tile(i, 32)
                grad = b["dn"][rows, :]
                hat = xh[rows, :]
                sum_g = sum_g + (grad * hat).reshape(4, 8, D).sum(0)
                sum_b = sum_b + grad.reshape(4, 8, D).sum(0)
                scaled = grad * gain[...]
                mean = jnp.mean(scaled, axis=-1, keepdims=True)
                along = jnp.mean(scaled * hat, axis=-1, keepdims=True)
                done(rows, b["dx"][rows, :] + b["rs"][rows, rs : rs + 1] * (scaled - mean - hat * along))
                return sum_g, sum_b

            sums = (jnp.zeros((8, D), F32),) * 2
            for i in range(8):
                sums = body(i, sums)
            sum_g, sum_b = sums
            b["vec"][row : row + 1, :] = sum_g.sum(0, keepdims=True)
            b["vec"][row + 1 : row + 2, :] = sum_b.sum(0, keepdims=True)

        def gather_to(axis, key, src_of, dst_of, core):
            for r in (1, 3, 2):
                p, to = peer(axis, r)
                send(key, r, src_of(p), dst_of(r), (core, to))
            if core is other:
                send(key, 0, src_of(at[axis]), dst_of(0), (core, dp))
                return None
            return local(key, 0, src_of(at[axis]), dst_of(0))

        def gather_some(axis, key, src, dst_of, chosen):
            for r in (1, 3, 2):
                p, to = peer(axis, r)
                send(key, r, src, dst_of(r), (sec, to), when=chosen(p))

        def cols(ref):
            return lambda r: ref.at[:, pl.ds(r * ROWS, ROWS)]

        def rows_of(ref):
            return lambda r: ref.at[pl.ds(r * ROWS, ROWS)]

        def scatter(axis, key, src_of, dst_of, base=0, core=sec):
            for r in (1, 3, 2):
                p, to = peer(axis, r)
                send(key, base + r, src_of(p), dst_of(r - 1), (core, to))

        def scatter48(axis, key, src_of, dst_of, base=0):
            for r in (1, 3, 2):
                p, to = peer(axis, r)
                for i in range(4):
                    send(key, base + 4 * r + i, src_of(p, i), dst_of(r - 1).at[tile(i, 48)], (sec, to))

        def recv48(key, dst_of, base=0):
            for r in (1, 3, 2):
                for i in range(4):
                    recv(key, base + 4 * r + i, dst_of(r - 1).at[tile(i, 48)])

        def recv3(key, dst_of, base=0):
            for r in (1, 3, 2):
                recv(key, base + r, dst_of(r - 1))

        def send_quarter():
            q = at[group[mine]]
            for k in range(4):
                b["b4"][k : k + 1, :] = bu[:, k * D : (k + 1) * D]
            b["b4"][4:8, :] = jnp.zeros((4, D), F32)
            send("w", 0, b["b4"], b["rb4"], (other, dp))
            loads["wu"].wait()
            send("w", 1, b["wu"].at[:, tile(q, D)], b["wuq"], (other, dp))
            loads["wd"].wait()
            send("w", 2, b["wd"].at[tile(q, D), :], b["wdq"], (other, dp))

        if not cross:
            weighted, ids = [], []
            total = jnp.zeros((1, 128), F32)
            for s in range(2):
                w = jnp.where(lane < flen[s], lw[s : s + 1, :].astype(F32), 0.0)
                total = total + jnp.where(lane == gid[s], jnp.sum(w, axis=1, keepdims=True), 0.0)
                weighted.append(w)
            b["tot"][...] = jnp.broadcast_to(total, (8, 128))
        if not cross:
            pl.semaphore_wait(barrier, 1 + 2 * len(near))
            for a, axis in enumerate("xyz"):
                for r in (1, 2, 3):
                    _, to = peer(axis, r)
                    send("tot", 3 * a + r - 1, b["tot"], b["rtot"].at[a, r - 1], (sec, to))
                for r in (1, 2, 3):
                    recv("tot", 3 * a + r - 1, b["rtot"].at[a, r - 1])
                for wait in pending:
                    wait()
                pending.clear()
                b["tot"][...] += b["rtot"][a, 0] + b["rtot"][a, 1] + b["rtot"][a, 2]
            totals = b["tot"][0:1, :]
            every = jnp.sum(totals, axis=1, keepdims=True)
            factors = every / (GROUPS * jnp.maximum(totals, 1.0))
            loads["cot"].wait()
            diagonal = lax.broadcasted_iota(jnp.int32, (SEQ, SEQ), 0) == lax.broadcasted_iota(
                jnp.int32, (SEQ, SEQ), 1
            )
            for s in range(2):
                factor = jnp.sum(jnp.where(lane == gid[s], factors, 0.0), axis=1, keepdims=True)
                picked = jnp.where(diagonal, weighted[s], 0.0).astype(BF)
                rows = slice(s * SEQ, (s + 1) * SEQ)
                grad = mm(picked, b["do"][rows, :]) * factor
                b["dx"][rows, :] = grad
                b["dyb"][rows, :] = grad.astype(BF)
            gather_to(group[1], "y", lambda p: b["dyb"], rows_of(b["ry"]), other)
            send_quarter()

        if cross:
            loads["x"].wait()
        else:
            recv("act", 0, b["xb"])
        norm(b["xb"], g1, b1, b["xh1"], 0, b["n1"], b["s2t"].at[0])

        if not cross:
            own_a2 = gather_to(group_qo, "a2", lambda p: b["s2t"].at[0], cols(b["ctxt"]), sec)
        loads["wq"].wait()

        def query(i):
            b["q"][:, tile(i)] = (mm(b["n1"][...], b["wq"][:, tile(i)]).astype(BF) * 0.125).astype(BF)

        loop(3, query)

        loads["wkv"].wait()
        if cross:
            loads["ctx"].wait()

            def keyval(i):
                for m in range(4):
                    rows = slice(m * T, (m + 1) * T)
                    b["kv"][rows, tile(i)] = mm(b["ctx"][rows, :], b["wkv"][:, tile(i)]).astype(BF)
        else:

            def keyval(i):
                b["kv"][0:ROWS, tile(i)] = mm(b["n1"][...], b["wkv"][:, tile(i)]).astype(BF)

        loop(6, keyval)
        keys = CTX if cross else SEQ
        if cross:
            pl.semaphore_wait(barrier, 1 + 2 * len(near))
            gather_some(group_qo, "a", b["s2t"].at[0], cols(b["rxa"]), lambda p: p < 2)

        def blocks(i):
            s, j = i // PAIRS, i % PAIRS
            vcols = slice(D + 128 * j, D + 128 * (j + 1))
            return s, j, tile(s, SEQ), tile(s, keys), tile(j, 128), vcols

        if cross:
            key = lax.broadcasted_iota(jnp.int32, (1, keys), 1)
            masks = [jnp.where(key < clen[s], 0.0, -1e9) for s in range(2)]
        else:
            row = lax.broadcasted_iota(jnp.int32, (SEQ, keys), 0)
            mask = jnp.where(lax.broadcasted_iota(jnp.int32, (SEQ, keys), 1) <= row, 0.0, -1e9)
            masks = [jnp.concatenate([mask, mask], axis=0)] * 2
        ones = jnp.ones((keys, 128), BF)

        def attend(i):
            s, j, rows, krows, kcols, vcols = blocks(i)
            scores = mm_nt(stacked(b["q"][rows, kcols]), b["kv"][krows, kcols]) + masks[s]
            e = jnp.exp(scores - jnp.max(scores, axis=-1, keepdims=True))
            values = b["kv"][krows, vcols]
            if cross:
                e = e.astype(BF)
                b["p"][i] = e
                mixed = mm(e, jnp.concatenate([values, ones], axis=1))
                scale = 1.0 / merged(mixed[:, 128:])
                b["inv"][rows, kcols] = scale
                b["o"][rows, kcols] = (merged(mixed[:, :128]) * scale).astype(BF)
            else:
                probs = (e / jnp.sum(e, axis=-1, keepdims=True)).astype(BF)
                b["p"][i, :, 0:keys] = probs
                b["o"][rows, kcols] = merged(mm(probs, values)).astype(BF)

        loop(2 * PAIRS, attend)
        for j in range(3):
            b["s2t"][1, j * T : (j + 1) * T, :] = b["o"][:, j * T : (j + 1) * T].T
        gather_some(group_qo, "a", b["s2t"].at[1], cols(b["rxa"]), lambda p: p >= 2)
        own_a = local("a", 0, b["s2t"].at[at[group_qo] // 2], cols(b["rxa"])(0))

        loads["wo"].wait()

        def project(i):
            b["x2"][:, tile(i)] = b["xb"][:, tile(i)].astype(F32) + mm(b["o"][...], b["wo"][:, tile(i)])

        loop(3, project)
        norm(b["x2"], g2, b2, b["xh2"], 1, b["n2"], None)
        gather_to(group[mine], "n", lambda p: b["n2"], rows_of(b["rn"]), other)
        if cross:
            send_quarter()

        def gelu(u):
            square = u * u
            th = jnp.tanh(u * (GELU_C + (GELU_C * GELU_A) * square))
            half = 0.5 + 0.5 * th
            slope = half + (u * (0.5 - 0.5 * th * th)) * (GELU_C + (3.0 * GELU_A * GELU_C) * square)
            return (u * half).astype(BF), slope.astype(BF)

        def up(i):
            u = mm(b["n2"][...], b["wu"][:, tile(i)]) + bu[:, tile(i)]
            k, at_cols = i // 3, tile(i % 3)
            b["hm"][k, :, at_cols], b["gp"][k, :, at_cols] = gelu(u)

        loop(12, up)

        def down(i):
            y = b["x2"][:, tile(i)]
            for k in range(4):
                y = y + mm(b["hm"][k], b["wd"][k * D : (k + 1) * D, tile(i)])
            acts[:, tile(i)] = y.astype(BF)

        loop(3, down)
        if cross:
            send("act", 0, acts, b["xb"], (other, dp))

        def add4(own, parts):
            total = own.astype(F32)
            for part in parts:
                total = total + part.astype(F32)
            return total

        def plane(key, axis, src_of, dst, base=0, core=sec):
            for r in (1, 3, 2, 0):
                for r2 in (1, 3, 2, 0):
                    if r or r2 or core is other:
                        p, p2, to = peer2(axis, r, "x", r2)
                        send(key, base + 4 * r + r2, src_of(p, p2), dst(r, r2), (core, to))

        def recv_plane(key, ref, base=0, first=1):
            for i in range(first, 16):
                recv(key, base + i, ref)

        def cut(dst, cols):
            for k in range(4):
                for j in range(4):
                    start = 48 * k + 12 * j
                    dst[k, j, :, cols] = b["pad"][start : start + 16, cols].astype(BF)

        full = slice(0, D)

        theirs = 1 - mine

        def ffn_forward():
            for i, name in enumerate(("rb4", "wuq", "wdq")):
                recv("w", i, b[name])
            for r in range(4):
                recv("n", r, rows_of(b["rn"])(r))
            bias = b["rb4"][pl.ds(at[group[theirs]], 1), :]
            for m in range(4):
                for i in range(3):
                    u = mm(b["rn"][tile(m), :], b["wuq"][:, tile(i)]) + bias[:, tile(i)]
                    hidden, b["gx"][tile(m), tile(i)] = gelu(u)
                    b["hxt"][tile(i), tile(m)] = hidden.T
                    b["rnt"][tile(i), tile(m)] = b["rn"][tile(m), tile(i)].T

        def down_a():
            for r in range(4):
                recv("y", r, rows_of(b["ry"])(r))
            for i in range(3):
                v = mm(b["hxt"][...], b["ry"][:, tile(i)]).astype(BF)
                b["gd"][:, :, tile(i)] = v.reshape(4, 192, T)
            scatter("x", "d1", lambda p: b["gd"].at[:, rows48(p)], lambda r: b["rd1"].at[r])

        def down_b():
            recv3("d1", lambda r: b["rd1"].at[r])
            for i in range(4):
                b["hd"][i] = add4(b["gd"][i, rows48(at["x"])], [b["rd1"][r, i] for r in range(3)]).astype(BF)
            if theirs == 0:
                for r in (1, 3, 2, 0):
                    p, to = peer("z", r)
                    send("d2", r, b["hd"].at[p], b["rd2"].at[r], (other, to))
            else:
                to = dp + (at["z"] - at["y"]) * step["y"]
                for r in (1, 3, 2, 0):
                    p, there = peer("z", r)
                    send("d2", r, b["hd"].at[p], b["rd2"].at[at["y"]], (other, to + there - dp), at["y"])

        def down_end():
            for r in range(4):
                recv("d2", r, b["rd2"].at[r])
            odn[...] = add4(b["rd2"][0], [b["rd2"][r] for r in (1, 2, 3)])

        def up_axes(layer):
            return ("y", "z") if layer == 1 else ("z", "y")

        def up_a():
            axis = up_axes(theirs)[0]
            for m in range(4):
                for i in range(3):
                    grad = mm_nt(b["ry"][tile(m), :], b["wdq"][tile(i), :])
                    b["gx"][tile(m), tile(i)] = (b["gx"][tile(m), tile(i)].astype(F32) * grad).astype(BF)
            for i in range(3):
                v = mm(b["rnt"][...], b["gx"][:, tile(i)]).astype(BF)
                b["gu"][:, :, tile(i)] = v.reshape(4, 192, T)
            if axis == "y":
                scatter(axis, "u1", lambda p: b["gu"].at[p], lambda r: b["ru1"].at[r])
            else:
                scatter48(axis, "u1", lambda p, i: b["gu"].at[i, rows48(p)], lambda r: b["ru1"].at[r])

        def up_b():
            axis, rest = up_axes(theirs)
            (recv3 if axis == "y" else recv48)("u1", lambda r: b["ru1"].at[r])
            for i in range(4):
                if axis == "y":
                    own, parts = b["gu"][at["y"], tile(i, 48)], [b["ru1"][r, tile(i, 48)] for r in range(3)]
                else:
                    own, parts = b["gu"][i, rows48(at["z"])], [b["ru1"][r, tile(i, 48)] for r in range(3)]
                b["pad"][tile(i, 48), :] = add4(own, parts)
            cut(b["hu"], full)
            plane(
                "u2", rest, lambda p, p2: b["hu"].at[p, p2],
                lambda r, r2: b["ru2"].at[at[rest], r2], core=other,
            )

        def up_end():
            recv_plane("u2", b["ru2"].at[0, 0], first=0)
            for k in range(4):
                total = add4(b["ru2"][k, 0], [b["ru2"][k, r] for r in (1, 2, 3)])
                oup[:, k * D : (k + 1) * D] = total[:12]

        width = 384 if cross else D
        part = slice(0, width)

        def qo_a():
            own_a.wait()
            own_b.wait()
            makes_out = at[group_qo] >= 2

            def recv_a():
                for r in range(1, 4):
                    recv("a", r, cols(b["rxa"])(r))

            if cross:
                recv_a()
            else:
                pl.when(makes_out)(recv_a)
            for r in range(1, 4):
                recv("b", r, rows_of(b["rxb"])(r))
            if not cross:
                own_a2.wait()
                own_b2.wait()
                for r in range(1, 4):
                    recv("a2", r, cols(b["ctxt"])(r))
                    recv("b2", r, b["dkvt"].at[pl.ds(r * ROWS, ROWS), pl.ds(0, 384)])

            def make(from_ref):
                for i in range(2):
                    v = mm(from_ref[tile(i, 384), :], b["rxb"][...]).astype(BF)
                    b["gq"][2 * i : 2 * i + 2, :, 0:384] = v.reshape(2, 192, 384)

            if cross:
                make(b["rxa"])
            else:
                pl.when(makes_out)(lambda: make(b["rxa"]))
                pl.when(jnp.logical_not(makes_out))(lambda: make(b["ctxt"]))
                for i in range(2):
                    v = mm(b["ctxt"][tile(i, 384), :], b["dkvt"][0:1024, 0:384]).astype(BF)
                    b["gq"][2 * i : 2 * i + 2, :, 384:768] = v.reshape(2, 192, 384)
            scatter("y", "q1", lambda p: b["gq"].at[p, :, pl.ds(0, width)], lambda r: b["rq1"].at[r, :, pl.ds(0, width)])

        def qo_b():
            recv3("q1", lambda r: b["rq1"].at[r, :, pl.ds(0, width)])
            for i in range(4):
                rows = tile(i, 48)
                b["pad"][rows, part] = add4(b["gq"][at["y"], rows, part], [b["rq1"][r, rows, part] for r in range(3)])
            cut(b["hq"], part)
            if cross:
                slot = lambda r, r2: b["rq2"].at[at["z"], r2, :, pl.ds(0, width)]
            else:
                slot = lambda r, r2: b["rq2"].at[at["x"], r, :, pl.ds(0, width)]
            plane("q2", "z", lambda p, p2: b["hq"].at[p, p2, :, pl.ds(0, width)], slot)
            b["rq2"][at[group_qo], 0, :, part] = b["hq"][at["z"], at["x"], :, part]

        def qo_end():
            recv_plane("q2", b["rq2"].at[0, 0, :, pl.ds(0, width)])

            def total(k, at_cols):
                return add4(b["rq2"][k, 0, :, at_cols], [b["rq2"][k, r, :, at_cols] for r in (1, 2, 3)])[:12]

            for k in range(2):
                oq[:, 384 * k : 384 * (k + 1)] = total(k, slice(0, 384))
                oo[:, 384 * k : 384 * (k + 1)] = total(2 + k, slice(0, 384))
            if not cross:
                for k in range(4):
                    okv[:, 384 * k : 384 * (k + 1)] = total(k, slice(384, D))

        def kv_a(h):
            for i in range(3):
                v = mm_nt(b["ctxt"][...], b["dkvt"][tile(3 * h + i), :]).astype(BF)
                b["kv"][0:D, tile(3 * h + i)] = v
            if h:
                scatter("y", "k1", lambda p: b["kv"].at[tile(p, 192), D:], lambda r: b["rk1"].at[1, r])
            else:
                scatter48("z", "k1", lambda p, i: b["kv"].at[rows48(4 * i + p), 0:D], lambda r: b["rk1"].at[0, r], 16)

        def kv_b(h):
            if h:
                recv3("k1", lambda r: b["rk1"].at[1, r])
            else:
                recv48("k1", lambda r: b["rk1"].at[0, r], 16)
            for i in range(4):
                m = 4 * at["y"] + i if h else 4 * i + at["z"]
                own = b["kv"][rows48(m), h * D : (h + 1) * D]
                b["pad"][tile(i, 48), :] = add4(own, [b["rk1"][h, r, tile(i, 48)] for r in range(3)])
            cut(b["hk"].at[h], full)
            axis = "z" if h else "y"
            plane(
                "k2", axis, lambda p, p2: b["hk"].at[h, p, p2],
                lambda r, r2: b["rk2"].at[h, 4 * r + r2], 16 * h,
            )
            b["rk2"][h, 0] = b["hk"][h, at[axis], at["x"]]

        def kv_end(h):
            recv_plane("k2", b["rk2"].at[h, 1], 16 * h)
            total = add4(b["rk2"][h, 0], [b["rk2"][h, i] for i in range(1, 16)])
            okv[:, h * D : (h + 1) * D] = total[:12]

        vec_copies = []

        def vec_send(a):
            for r in (1, 2, 3):
                _, to = peer("xyz"[a], r)
                send("v", 3 * a + r - 1, b["vec"], b["rvec"].at[a, r - 1], (sec, to))
                vec_copies.append(pending.pop())

        def vec_add(a):
            for r in (1, 2, 3):
                recv("v", 3 * a + r - 1, b["rvec"].at[a, r - 1])
            for wait in vec_copies:
                wait()
            vec_copies.clear()
            b["vec"][...] += b["rvec"][a, 0] + b["rvec"][a, 1] + b["rvec"][a, 2]

        def vec_out():
            shift = lax.rem(D - 12 * dp, D)
            rolled = pltpu.roll(b["vec"][...], shift, axis=1)
            for row, out in enumerate((og1, ob1, og2, ob2)):
                out[...] = rolled[row : row + 1, 0:12]
            bias_row = b["vec"][pl.ds(4 + at["y"], 1), :]
            shift = lax.rem(D - 48 * lax.rem(dp, 16), D)
            rolled = pltpu.roll(jnp.broadcast_to(bias_row, (8, D)), shift, axis=1)
            oub[...] = rolled[0:1, 0:48]

        if cross:
            for j in range(3):
                for m in range(4):
                    rows, at_cols = slice(m * T, (m + 1) * T), slice(j * T, (j + 1) * T)
                    b["ctxt"][at_cols, rows] = b["ctx"][rows, at_cols].T
        if cross:
            ffn_forward()
            recv("back", 0, b["dyb"])
            b["dx"][...] = b["dyb"][...].astype(F32)
            gather_to(group[0], "y", lambda p: b["dyb"], rows_of(b["ry"]), other)

        for k in range(4):

            def up_back(i):
                grad = mm_nt(b["dyb"][...], b["wd"][tile(3 * k + i), :])
                du = (b["gp"][k, :, tile(i)].astype(F32) * grad).astype(BF)
                b["gp"][k, :, tile(i)] = du
                b["vec"][4 + k : 5 + k, tile(i)] = jnp.sum(du.astype(F32), axis=0, keepdims=True)

            loop(3, up_back)

        def n2_back(i):
            grad = jnp.zeros((ROWS, T), F32)
            for k in range(4):
                grad = grad + mm_nt(b["gp"][k], b["wu"][tile(i), k * D : (k + 1) * D])
            b["dn"][:, tile(i)] = grad

        loop(3, n2_back)

        def done2(rows, value):
            b["dx"][rows, :] = value
            rounded = value.astype(BF)
            b["d4"][2, rows, :] = rounded[:, 0:384]
            b["d4"][3, rows, :] = rounded[:, 384:768]

        norm_back(b["xh2"], 1, g2, 2, done2)

        def out_back(i):
            rows = tile(i)
            grad = mm_nt(b["d4"][2], b["wo"][rows, 0:384]) + mm_nt(b["d4"][3], b["wo"][rows, 384:768])
            b["do"][:, tile(i)] = grad.astype(BF)

        loop(3, out_back)

        def attend_back(i):
            s, j, rows, krows, kcols, vcols = blocks(i)
            k2, v2 = b["kv"][krows, kcols], b["kv"][krows, vcols]
            q2 = stacked(b["q"][rows, kcols])
            probs = b["p"][i, :, 0:keys]
            grad = b["do"][rows, kcols].astype(F32)
            if cross:
                grad = grad * b["inv"][rows, kcols]
            along = grad * b["o"][rows, kcols].astype(F32)
            along = jnp.concatenate([jnp.where(first_head, along, 0.0), jnp.where(first_head, 0.0, along)], axis=0)
            along = jnp.sum(along, axis=-1, keepdims=True)
            do2 = stacked(grad.astype(BF))
            ds = (probs.astype(F32) * (mm_nt(do2, v2) - along)).astype(BF)
            half, at_cols = j // 3, tile(j % 3, 128)
            b["d4"][half, rows, at_cols] = (merged(mm(ds, k2)) * 0.125).astype(BF)
            if cross:
                b["dkvt"][tile(j, 128), krows] = mm_tn(q2, ds).astype(BF)
                b["dkvt"][vcols, krows] = mm_tn(do2, probs).astype(BF)
            else:
                b["ctx"][tile(2 * half + s, SEQ), at_cols] = mm_tn(ds, q2).astype(BF)
                b["ctx"][tile(4 + 2 * half + s, SEQ), at_cols] = mm_tn(probs, do2).astype(BF)

        loop(2 * PAIRS, attend_back)
        own_b = gather_to(group_qo, "b", lambda p: b["d4"].at[p], rows_of(b["rxb"]), sec)
        if not cross:

            def kv_quarter(p):
                return b["ctx"].at[tile(p, ROWS), pl.ds(0, 384)]

            own_b2 = gather_to(
                group_qo, "b2", kv_quarter, lambda r: b["dkvt"].at[pl.ds(r * ROWS, ROWS), pl.ds(0, 384)], sec
            )

        if cross:
            kv_a(1)
            kv_a(0)

        def n1_back(i):
            rows = tile(i)
            grad = mm_nt(b["d4"][0], b["wq"][rows, 0:384]) + mm_nt(b["d4"][1], b["wq"][rows, 384:768])
            if not cross:
                for k in range(4):
                    quarter = b["ctx"][k * ROWS : (k + 1) * ROWS, 0:384]
                    grad = grad + mm_nt(quarter, b["wkv"][rows, 384 * k : 384 * (k + 1)])
            b["dn"][:, tile(i)] = grad

        loop(3, n1_back)

        def done1(rows, value):
            ins[rows, :] = value.astype(BF)

        norm_back(b["xh1"], 0, g1, 0, done1)
        if not cross:
            send("back", 0, ins, b["dyb"], (other, dp))

        if cross:
            vec_send(0)
            down_a()
            up_a()
            qo_a()
            kv_b(1)
            kv_b(0)
            vec_add(0)
            vec_send(1)
            down_b()
            up_b()
            qo_b()
            vec_add(1)
            vec_send(2)
            vec_add(2)
            vec_out()
            kv_end(0)
            kv_end(1)
        else:
            vec_send(0)
            ffn_forward()
            vec_add(0)
            vec_send(1)
            down_a()
            up_a()
            vec_add(1)
            vec_send(2)
            qo_a()
            down_b()
            up_b()
            qo_b()
            vec_add(2)
            vec_out()
        qo_end()
        down_end()
        up_end()
        for wait in pending:
            wait()

    pl.when(sec == 0)(lambda: branch(0))
    pl.when(sec == 1)(lambda: branch(1))


def deliver(*refs):
    for a, out in zip(refs[:12], refs[12:]):
        out[...] = a[...].reshape(out.shape)


def on_device(
    tokens, context, out_cot, group_id, ctx_len, fut_len, loss_weight,
    norm_gain1, norm_bias1, w_query, w_keyval, w_out,
    norm_gain2, norm_bias2, w_up, up_bias, w_down,
):
    smem = pl.BlockSpec(memory_space=pltpu.SMEM)
    vmem = pl.BlockSpec(memory_space=pltpu.VMEM)
    hbm = pl.BlockSpec(memory_space=pl.ANY)
    shape = jax.ShapeDtypeStruct
    outs = pl.pallas_call(
        kernel,
        out_shape=(
            shape((ROWS, D), BF),
            shape((ROWS, D), BF),
            shape((1, 12), F32),
            shape((1, 12), F32),
            shape((12, D), F32),
            shape((12, 2 * D), F32),
            shape((12, D), F32),
            shape((1, 12), F32),
            shape((1, 12), F32),
            shape((12, FF), F32),
            shape((1, 48), F32),
            shape((48, D), F32),
        ),
        in_specs=[smem] * 3 + [vmem] + [hbm] * 3 + [vmem] * 5 + [hbm] * 5,
        out_specs=[vmem] * 12,
        scratch_shapes=[pltpu.VMEM(s, t) for s, t in BUFS.values()]
        + [pltpu.SemaphoreType.DMA((N_SEMS,)), pltpu.SemaphoreType.DMA((N_SEMS,))],
        compiler_params=pltpu.CompilerParams(
            collective_id=0, has_side_effects=True, vmem_limit_bytes=64 * 1024 * 1024 - 4096
        ),
    )(
        group_id, ctx_len, fut_len, loss_weight,
        tokens.reshape(ROWS, D), context.reshape(2 * CTX, D), out_cot.reshape(ROWS, D),
        norm_gain1, norm_bias1, norm_gain2, norm_bias2, up_bias,
        w_query[0], w_keyval[0], w_out[0], w_up[0], w_down[0],
    )
    outs = pl.pallas_call(
        deliver,
        out_shape=[
            shape((a.shape[0], 1, a.shape[1]) if a.shape[0] == 12 else a.shape, a.dtype) for a in outs
        ],
        in_specs=[vmem] * 12,
        out_specs=[vmem] * 12,
    )(*outs)
    acts, ins, gg1, gb1, gq, gkv, go, gg2, gb2, gup, gub, gdn = outs
    seqs = (1, 2, SEQ, D)
    rows = [g.reshape(1, 12, g.shape[-1]) for g in (gq, gkv, go, gup)]
    return (
        acts.reshape(seqs), ins.reshape(seqs), gg1, gb1, *rows[:3],
        gg2, gb2, rows[3], gub, gdn[None],
    )


def solution(mesh):
    dp, sec = "dp", "section"
    vec, mat = P(sec, None), P(sec, None, None)
    return jax.shard_map(
        on_device,
        mesh=mesh,
        in_specs=(P(dp, None, None),) * 3 + (P(dp),) * 3 + (P(dp, None),)
        + (vec, vec, mat, mat, mat, vec, vec, mat, vec, mat),
        out_specs=(P(sec, dp, None, None),) * 2 + (P(sec, dp),) * 2 + (P(sec, dp, None),) * 3
        + (P(sec, dp),) * 2 + (P(sec, dp, None), P(sec, dp), P(sec, dp, None)),
        check_vma=False,
    )
```

```python
import math

import jax
import jax.numpy as jnp
from jax import lax
from jax.experimental import pallas as pl
from jax.experimental.pallas import tpu as pltpu
from jax.sharding import PartitionSpec as P

MESH = pl.DeviceIdType.MESH
BF = jnp.bfloat16
F32 = jnp.float32
GROUPS = 8
D = 768
FF = 3072
SEQ = 128
ROWS = 256
CTX = 512
PAIRS = 6
T = 256
GELU_C = math.sqrt(2.0 / math.pi)
GELU_A = 0.044715


def mm(a, b):
    return jnp.dot(a, b, preferred_element_type=F32)


def mm_nt(a, b):
    return lax.dot_general(a, b, (((1,), (1,)), ((), ())), preferred_element_type=F32)


def mm_tn(a, b):
    return lax.dot_general(a, b, (((0,), (0,)), ((), ())), preferred_element_type=F32)


def loop(n, body):
    for i in range(n):
        body(i)


def rows48(i):
    return pl.ds(pl.multiple_of(i * 48, 16), 48)


def tile(i, size=T):
    if isinstance(i, int):
        return slice(i * size, (i + 1) * size)
    return pl.ds(pl.multiple_of(i * size, size), size)


BUFS = dict(
    wq=((D, D), BF),
    wkv=((D, 2 * D), BF),
    wo=((D, D), BF),
    wu=((D, FF), BF),
    wd=((FF, D), BF),
    xb=((ROWS, D), BF),
    ctx=((2 * CTX, D), BF),
    ctxt=((D, 2 * CTX), BF),
    n1=((ROWS, D), BF),
    q=((ROWS, D), BF),
    kv=((2 * CTX, 2 * D), BF),
    p=((2 * PAIRS, ROWS, CTX), BF),
    inv=((ROWS, D), F32),
    o=((ROWS, D), BF),
    s2t=((2, D, ROWS), BF),
    n2=((ROWS, D), BF),
    x2=((ROWS, D), F32),
    xh1=((ROWS, D), F32),
    xh2=((ROWS, D), F32),
    rs=((ROWS, 2), F32),
    gp=((4, ROWS, D), BF),
    hm=((4, ROWS, D), BF),
    dyb=((ROWS, D), BF),
    dx=((ROWS, D), F32),
    d4=((4, ROWS, 384), BF),
    dkvt=((2 * D, 2 * CTX), BF),
    vec=((8, D), F32),
    rvec=((3, 3, 8, D), F32),
    tot=((8, 128), F32),
    rtot=((3, 3, 8, 128), F32),
    b4=((8, D), F32),
    rb4=((8, D), F32),
    wuq=((D, D), BF),
    wdq=((D, D), BF),
    rn=((4 * ROWS, D), BF),
    rnt=((D, 4 * ROWS), BF),
    ry=((4 * ROWS, D), BF),
    hxt=((D, 4 * ROWS), BF),
    gx=((4 * ROWS, D), BF),
    rd1=((3, 4, 48, D), BF),
    hd=((4, 48, D), BF),
    rd2=((4, 48, D), BF),
    ru1=((3, 192, D), BF),
    hu=((4, 4, 16, D), BF),
    ru2=((4, 4, 16, D), BF),
    rxa=((D, 4 * ROWS), BF),
    rxb=((4 * ROWS, 384), BF),
    gq=((4, 192, D), BF),
    rq1=((3, 192, D), BF),
    hq=((4, 4, 16, D), BF),
    rq2=((4, 4, 16, D), BF),
    rk1=((2, 3, 192, D), BF),
    hk=((2, 4, 4, 16, D), BF),
    rk2=((2, 16, 16, D), BF),
)
KEYS = {}
for _name, _n in dict(
    tot=9, act=1, back=1, a=4, n=4, y=4, w=3, b=4, a2=4, b2=4,
    d1=4, d2=4, u1=16, u2=16, q1=4, q2=16, k1=32, k2=32, v=9, load=8,
).items():
    KEYS[_name] = sum(KEYS.values()) if not KEYS else _total
    _total = KEYS[_name] + _n
N_SEMS = _total
NAMES = list(BUFS)


def kernel(*refs):
    (gid, clen, flen, lw, tokens, ctx_in, cot_in, g1, b1, g2, b2, bu, wq_in, wkv_in, wo_in, wu_in, wd_in) = refs[:17]
    (acts, ins, og1, ob1, oq, okv, oo, og2, ob2, oup, oub, odn) = refs[17:29]
    b = dict(zip(NAMES, refs[29 : 29 + len(NAMES)]))
    b["do"] = b["n1"]
    b["dn"] = b["x2"]
    b["pad"] = b["x2"].at[pl.ds(0, 208)]
    b["gd"] = b["gp"].at[:, pl.ds(0, 192)]
    b["gu"] = b["hm"].at[:, pl.ds(0, 192)]
    ssem, rsem, done_sem = refs[29 + len(NAMES) :]

    sec = lax.axis_index("section")
    dp = lax.axis_index("dp")
    at = {"y": dp // 16, "z": (dp // 4) % 4, "x": dp % 4}
    step = {"y": 16, "z": 4, "x": 1}
    other = 1 - sec

    def peer(axis, r):
        p = lax.rem(at[axis] + r, 4)
        return p, dp + (p - at[axis]) * step[axis]

    def peer2(axis, r, axis2, r2):
        p, to = peer(axis, r)
        p2, to2 = peer(axis2, r2)
        return p, p2, to + to2 - dp

    barrier = pltpu.get_barrier_semaphore()
    pl.semaphore_signal(barrier, inc=1, device_id=(other, dp), device_id_type=MESH)
    near = [peer(axis, r)[1] for axis in "xyz" for r in (1, 2, 3)]
    for axis, axis2 in ("yx", "zx", "yz"):
        near += [peer2(axis, r, axis2, r2)[2] for r in (1, 2, 3) for r2 in (1, 2, 3)]
    for to in near:
        for core in (sec, other):
            pl.semaphore_signal(barrier, inc=1, device_id=(core, to), device_id_type=MESH)

    def branch(mine):
        cross = mine == 0
        group = {0: "y", 1: "z"}
        group_qo = "z" if cross else "x"
        pending = []

        def send(key, i, src, dst, device, slot=None):
            k = KEYS[key] + i
            copy = pltpu.make_async_remote_copy(
                src_ref=src, dst_ref=dst, send_sem=ssem.at[k],
                recv_sem=rsem.at[k if slot is None else KEYS[key] + slot],
                device_id=device, device_id_type=MESH,
            )
            copy.start()
            pending.append(copy)

        def recv(key, i, ref):
            k = KEYS[key] + i
            pltpu.make_async_remote_copy(
                src_ref=ref, dst_ref=ref, send_sem=ssem.at[k], recv_sem=rsem.at[k],
                device_id=(other, dp), device_id_type=MESH,
            ).wait_recv()

        def local(key, i, src, dst):
            copy = pltpu.make_async_copy(src, dst, rsem.at[KEYS[key] + i])
            copy.start()
            return copy

        loads = {}

        def load(name, i, src, dst):
            loads[name] = local("load", i, src, dst)

        if cross:
            load("x", 0, tokens, b["xb"])
            load("wq", 3, wq_in, b["wq"])
            load("ctx", 1, ctx_in, b["ctx"])
            load("wkv", 2, wkv_in, b["wkv"])
        else:
            load("cot", 0, cot_in, b["do"])
            load("wq", 3, wq_in, b["wq"])
            load("wkv", 2, wkv_in, b["wkv"])
        load("wo", 4, wo_in, b["wo"])
        load("wu", 5, wu_in, b["wu"])
        load("wd", 6, wd_in, b["wd"])

        lane = lax.broadcasted_iota(jnp.int32, (1, 128), 1)
        first_head = lane < 64
        mask_a = first_head.astype(F32).astype(BF)
        mask_b = 1.0 - mask_a

        def stacked(v):
            return jnp.concatenate([v * mask_a, v * mask_b], axis=0)

        def merged(v):
            return jnp.where(first_head, v[:SEQ], v[SEQ:])

        def norm(src, gain, bias, xh, rs, n, nt):
            def body(i):
                rows = tile(i, 32)
                v = src[rows, :].astype(F32)
                centre = v - jnp.mean(v, axis=-1, keepdims=True)
                spread = jnp.mean(centre * centre, axis=-1, keepdims=True)
                scale = lax.rsqrt(spread + 1e-05)
                hat = centre * scale
                xh[rows, :] = hat
                b["rs"][rows, rs : rs + 1] = scale
                n[rows, :] = (hat * gain[...] + bias[...]).astype(BF)

            loop(8, body)
            if nt is not None:
                for j in range(3):
                    nt[j * T : (j + 1) * T, :] = n[:, j * T : (j + 1) * T].T

        def norm_back(xh, rs, gain, row, done):
            def body(i, carry):
                sum_g, sum_b = carry
                rows = tile(i, 32)
                grad = b["dn"][rows, :]
                hat = xh[rows, :]
                sum_g = sum_g + (grad * hat).reshape(4, 8, D).sum(0)
                sum_b = sum_b + grad.reshape(4, 8, D).sum(0)
                scaled = grad * gain[...]
                mean = jnp.mean(scaled, axis=-1, keepdims=True)
                along = jnp.mean(scaled * hat, axis=-1, keepdims=True)
                done(rows, b["dx"][rows, :] + b["rs"][rows, rs : rs + 1] * (scaled - mean - hat * along))
                return sum_g, sum_b

            sums = (jnp.zeros((8, D), F32),) * 2
            for i in range(8):
                sums = body(i, sums)
            sum_g, sum_b = sums
            b["vec"][row : row + 1, :] = sum_g.sum(0, keepdims=True)
            b["vec"][row + 1 : row + 2, :] = sum_b.sum(0, keepdims=True)

        def gather_to(axis, key, src_of, dst_of, core):
            for r in (1, 3, 2):
                p, to = peer(axis, r)
                send(key, r, src_of(p), dst_of(r), (core, to))
            if core is other:
                send(key, 0, src_of(at[axis]), dst_of(0), (core, dp))
                return None
            return local(key, 0, src_of(at[axis]), dst_of(0))

        def cols(ref):
            return lambda r: ref.at[:, pl.ds(r * ROWS, ROWS)]

        def rows_of(ref):
            return lambda r: ref.at[pl.ds(r * ROWS, ROWS)]

        def scatter(axis, key, src_of, dst_of, base=0, core=sec):
            for r in (1, 3, 2):
                p, to = peer(axis, r)
                send(key, base + r, src_of(p), dst_of(r - 1), (core, to))

        def scatter48(axis, key, src_of, dst_of, base=0):
            for r in (1, 3, 2):
                p, to = peer(axis, r)
                for i in range(4):
                    send(key, base + 4 * r + i, src_of(p, i), dst_of(r - 1).at[tile(i, 48)], (sec, to))

        def recv48(key, dst_of, base=0):
            for r in (1, 3, 2):
                for i in range(4):
                    recv(key, base + 4 * r + i, dst_of(r - 1).at[tile(i, 48)])

        def recv3(key, dst_of, base=0):
            for r in (1, 3, 2):
                recv(key, base + r, dst_of(r - 1))

        def send_quarter():
            q = at[group[mine]]
            for k in range(4):
                b["b4"][k : k + 1, :] = bu[:, k * D : (k + 1) * D]
            b["b4"][4:8, :] = jnp.zeros((4, D), F32)
            send("w", 0, b["b4"], b["rb4"], (other, dp))
            loads["wu"].wait()
            send("w", 1, b["wu"].at[:, tile(q, D)], b["wuq"], (other, dp))
            loads["wd"].wait()
            send("w", 2, b["wd"].at[tile(q, D), :], b["wdq"], (other, dp))

        if not cross:
            weighted, ids = [], []
            total = jnp.zeros((1, 128), F32)
            for s in range(2):
                w = jnp.where(lane < flen[s], lw[s : s + 1, :].astype(F32), 0.0)
                total = total + jnp.where(lane == gid[s], jnp.sum(w, axis=1, keepdims=True), 0.0)
                weighted.append(w)
            b["tot"][...] = jnp.broadcast_to(total, (8, 128))
        pl.semaphore_wait(barrier, 1 + 2 * len(near))
        if not cross:
            for a, axis in enumerate("xyz"):
                for r in (1, 2, 3):
                    _, to = peer(axis, r)
                    send("tot", 3 * a + r - 1, b["tot"], b["rtot"].at[a, r - 1], (sec, to))
                for r in (1, 2, 3):
                    recv("tot", 3 * a + r - 1, b["rtot"].at[a, r - 1])
                for copy in pending:
                    copy.wait_send()
                pending.clear()
                b["tot"][...] += b["rtot"][a, 0] + b["rtot"][a, 1] + b["rtot"][a, 2]
            totals = b["tot"][0:1, :]
            every = jnp.sum(totals, axis=1, keepdims=True)
            factors = every / (GROUPS * jnp.maximum(totals, 1.0))
            loads["cot"].wait()
            diagonal = lax.broadcasted_iota(jnp.int32, (SEQ, SEQ), 0) == lax.broadcasted_iota(
                jnp.int32, (SEQ, SEQ), 1
            )
            for s in range(2):
                factor = jnp.sum(jnp.where(lane == gid[s], factors, 0.0), axis=1, keepdims=True)
                picked = jnp.where(diagonal, weighted[s], 0.0).astype(BF)
                rows = slice(s * SEQ, (s + 1) * SEQ)
                grad = mm(picked, b["do"][rows, :]) * factor
                b["dx"][rows, :] = grad
                b["dyb"][rows, :] = grad.astype(BF)
            gather_to(group[1], "y", lambda p: b["dyb"], rows_of(b["ry"]), other)
            send_quarter()

        if cross:
            loads["x"].wait()
        else:
            recv("act", 0, b["xb"])
        norm(b["xb"], g1, b1, b["xh1"], 0, b["n1"], b["s2t"].at[0])

        loads["wq"].wait()

        def query(i):
            b["q"][:, tile(i)] = (mm(b["n1"][...], b["wq"][:, tile(i)]).astype(BF) * 0.125).astype(BF)

        loop(3, query)

        loads["wkv"].wait()
        if cross:
            loads["ctx"].wait()

            def keyval(i):
                for m in range(4):
                    rows = slice(m * T, (m + 1) * T)
                    b["kv"][rows, tile(i)] = mm(b["ctx"][rows, :], b["wkv"][:, tile(i)]).astype(BF)
        else:

            def keyval(i):
                b["kv"][0:ROWS, tile(i)] = mm(b["n1"][...], b["wkv"][:, tile(i)]).astype(BF)

        loop(6, keyval)
        keys = CTX if cross else SEQ

        def blocks(i):
            s, j = i // PAIRS, i % PAIRS
            vcols = slice(D + 128 * j, D + 128 * (j + 1))
            return s, j, tile(s, SEQ), tile(s, keys), tile(j, 128), vcols

        if cross:
            key = lax.broadcasted_iota(jnp.int32, (1, keys), 1)
            masks = [jnp.where(key < clen[s], 0.0, -1e9) for s in range(2)]
        else:
            row = lax.broadcasted_iota(jnp.int32, (SEQ, keys), 0)
            mask = jnp.where(lax.broadcasted_iota(jnp.int32, (SEQ, keys), 1) <= row, 0.0, -1e9)
            masks = [jnp.concatenate([mask, mask], axis=0)] * 2
        ones = jnp.ones((keys, 128), BF)

        def attend(i):
            s, j, rows, krows, kcols, vcols = blocks(i)
            scores = mm_nt(stacked(b["q"][rows, kcols]), b["kv"][krows, kcols]) + masks[s]
            e = jnp.exp(scores - jnp.max(scores, axis=-1, keepdims=True))
            values = b["kv"][krows, vcols]
            if cross:
                e = e.astype(BF)
                b["p"][i] = e
                mixed = mm(e, jnp.concatenate([values, ones], axis=1))
                scale = 1.0 / merged(mixed[:, 128:])
                b["inv"][rows, kcols] = scale
                b["o"][rows, kcols] = (merged(mixed[:, :128]) * scale).astype(BF)
            else:
                probs = (e / jnp.sum(e, axis=-1, keepdims=True)).astype(BF)
                b["p"][i, :, 0:keys] = probs
                b["o"][rows, kcols] = merged(mm(probs, values)).astype(BF)

        loop(2 * PAIRS, attend)
        for j in range(3):
            b["s2t"][1, j * T : (j + 1) * T, :] = b["o"][:, j * T : (j + 1) * T].T
        own_a = gather_to(group_qo, "a", lambda p: b["s2t"].at[p // 2], cols(b["rxa"]), sec)
        if not cross:
            own_a2 = gather_to(group_qo, "a2", lambda p: b["s2t"].at[0], cols(b["ctxt"]), sec)

        loads["wo"].wait()

        def project(i):
            b["x2"][:, tile(i)] = b["xb"][:, tile(i)].astype(F32) + mm(b["o"][...], b["wo"][:, tile(i)])

        loop(3, project)
        norm(b["x2"], g2, b2, b["xh2"], 1, b["n2"], None)
        gather_to(group[mine], "n", lambda p: b["n2"], rows_of(b["rn"]), other)
        if cross:
            send_quarter()

        def gelu(u):
            square = u * u
            th = jnp.tanh(u * (GELU_C + (GELU_C * GELU_A) * square))
            half = 0.5 + 0.5 * th
            slope = half + (u * (0.5 - 0.5 * th * th)) * (GELU_C + (3.0 * GELU_A * GELU_C) * square)
            return (u * half).astype(BF), slope.astype(BF)

        def up(i):
            u = mm(b["n2"][...], b["wu"][:, tile(i)]) + bu[:, tile(i)]
            k, at_cols = i // 3, tile(i % 3)
            b["hm"][k, :, at_cols], b["gp"][k, :, at_cols] = gelu(u)

        loop(12, up)

        def down(i):
            y = b["x2"][:, tile(i)]
            for k in range(4):
                y = y + mm(b["hm"][k], b["wd"][k * D : (k + 1) * D, tile(i)])
            acts[:, tile(i)] = y.astype(BF)

        loop(3, down)
        if cross:
            send("act", 0, acts, b["xb"], (other, dp))

        def add4(own, parts):
            total = own.astype(F32)
            for part in parts:
                total = total + part.astype(F32)
            return total

        def plane(key, axis, src_of, dst, base=0, core=sec):
            for r in (1, 3, 2, 0):
                for r2 in (1, 3, 2, 0):
                    if r or r2 or core is other:
                        p, p2, to = peer2(axis, r, "x", r2)
                        send(key, base + 4 * r + r2, src_of(p, p2), dst(r, r2), (core, to))

        def recv_plane(key, ref, base=0, first=1):
            for i in range(first, 16):
                recv(key, base + i, ref)

        def cut(dst, cols):
            for k in range(4):
                for j in range(4):
                    start = 48 * k + 12 * j
                    dst[k, j, :, cols] = b["pad"][start : start + 16, cols].astype(BF)

        full = slice(0, D)

        theirs = 1 - mine

        def ffn_forward():
            for i, name in enumerate(("rb4", "wuq", "wdq")):
                recv("w", i, b[name])
            for r in range(4):
                recv("n", r, rows_of(b["rn"])(r))
            bias = b["rb4"][pl.ds(at[group[theirs]], 1), :]
            for m in range(4):
                for i in range(3):
                    u = mm(b["rn"][tile(m), :], b["wuq"][:, tile(i)]) + bias[:, tile(i)]
                    hidden, b["gx"][tile(m), tile(i)] = gelu(u)
                    b["hxt"][tile(i), tile(m)] = hidden.T
                    b["rnt"][tile(i), tile(m)] = b["rn"][tile(m), tile(i)].T

        def down_a():
            for r in range(4):
                recv("y", r, rows_of(b["ry"])(r))
            for i in range(3):
                v = mm(b["hxt"][...], b["ry"][:, tile(i)]).astype(BF)
                b["gd"][:, :, tile(i)] = v.reshape(4, 192, T)
            scatter("x", "d1", lambda p: b["gd"].at[:, rows48(p)], lambda r: b["rd1"].at[r])

        def down_b():
            recv3("d1", lambda r: b["rd1"].at[r])
            for i in range(4):
                b["hd"][i] = add4(b["gd"][i, rows48(at["x"])], [b["rd1"][r, i] for r in range(3)]).astype(BF)
            if theirs == 0:
                for r in (1, 3, 2, 0):
                    p, to = peer("z", r)
                    send("d2", r, b["hd"].at[p], b["rd2"].at[r], (other, to))
            else:
                to = dp + (at["z"] - at["y"]) * step["y"]
                for r in (1, 3, 2, 0):
                    p, there = peer("z", r)
                    send("d2", r, b["hd"].at[p], b["rd2"].at[at["y"]], (other, to + there - dp), at["y"])

        def down_end():
            for r in range(4):
                recv("d2", r, b["rd2"].at[r])
            odn[...] = add4(b["rd2"][0], [b["rd2"][r] for r in (1, 2, 3)])

        def up_axes(layer):
            return ("y", "z") if layer == 1 else ("z", "y")

        def up_a():
            axis = up_axes(theirs)[0]
            for m in range(4):
                for i in range(3):
                    grad = mm_nt(b["ry"][tile(m), :], b["wdq"][tile(i), :])
                    b["gx"][tile(m), tile(i)] = (b["gx"][tile(m), tile(i)].astype(F32) * grad).astype(BF)
            for i in range(3):
                v = mm(b["rnt"][...], b["gx"][:, tile(i)]).astype(BF)
                b["gu"][:, :, tile(i)] = v.reshape(4, 192, T)
            if axis == "y":
                scatter(axis, "u1", lambda p: b["gu"].at[p], lambda r: b["ru1"].at[r])
            else:
                scatter48(axis, "u1", lambda p, i: b["gu"].at[i, rows48(p)], lambda r: b["ru1"].at[r])

        def up_b():
            axis, rest = up_axes(theirs)
            (recv3 if axis == "y" else recv48)("u1", lambda r: b["ru1"].at[r])
            for i in range(4):
                if axis == "y":
                    own, parts = b["gu"][at["y"], tile(i, 48)], [b["ru1"][r, tile(i, 48)] for r in range(3)]
                else:
                    own, parts = b["gu"][i, rows48(at["z"])], [b["ru1"][r, tile(i, 48)] for r in range(3)]
                b["pad"][tile(i, 48), :] = add4(own, parts)
            cut(b["hu"], full)
            plane(
                "u2", rest, lambda p, p2: b["hu"].at[p, p2],
                lambda r, r2: b["ru2"].at[at[rest], r2], core=other,
            )

        def up_end():
            recv_plane("u2", b["ru2"].at[0, 0], first=0)
            for k in range(4):
                total = add4(b["ru2"][k, 0], [b["ru2"][k, r] for r in (1, 2, 3)])
                oup[:, k * D : (k + 1) * D] = total[:12]

        width = 384 if cross else D
        part = slice(0, width)

        def qo_a():
            own_a.wait()
            own_b.wait()
            for r in range(1, 4):
                recv("a", r, cols(b["rxa"])(r))
                recv("b", r, rows_of(b["rxb"])(r))
            if not cross:
                own_a2.wait()
                own_b2.wait()
                for r in range(1, 4):
                    recv("a2", r, cols(b["ctxt"])(r))
                    recv("b2", r, b["dkvt"].at[pl.ds(r * ROWS, ROWS), pl.ds(0, 384)])
            for i in range(2):
                rows = tile(i, 384)
                v = mm(b["rxa"][rows, :], b["rxb"][...]).astype(BF)
                b["gq"][2 * i : 2 * i + 2, :, 0:384] = v.reshape(2, 192, 384)
                if not cross:
                    v = mm(b["ctxt"][rows, :], b["dkvt"][0:1024, 0:384]).astype(BF)
                    b["gq"][2 * i : 2 * i + 2, :, 384:768] = v.reshape(2, 192, 384)
            scatter("y", "q1", lambda p: b["gq"].at[p, :, pl.ds(0, width)], lambda r: b["rq1"].at[r, :, pl.ds(0, width)])

        def qo_b():
            recv3("q1", lambda r: b["rq1"].at[r, :, pl.ds(0, width)])
            for i in range(4):
                rows = tile(i, 48)
                b["pad"][rows, part] = add4(b["gq"][at["y"], rows, part], [b["rq1"][r, rows, part] for r in range(3)])
            cut(b["hq"], part)
            if cross:
                slot = lambda r, r2: b["rq2"].at[at["z"], r2, :, pl.ds(0, width)]
            else:
                slot = lambda r, r2: b["rq2"].at[at["x"], r, :, pl.ds(0, width)]
            plane("q2", "z", lambda p, p2: b["hq"].at[p, p2, :, pl.ds(0, width)], slot)
            b["rq2"][at[group_qo], 0, :, part] = b["hq"][at["z"], at["x"], :, part]

        def qo_end():
            recv_plane("q2", b["rq2"].at[0, 0, :, pl.ds(0, width)])

            def total(k, at_cols):
                return add4(b["rq2"][k, 0, :, at_cols], [b["rq2"][k, r, :, at_cols] for r in (1, 2, 3)])[:12]

            for k in range(2):
                oq[:, 384 * k : 384 * (k + 1)] = total(k, slice(0, 384))
                oo[:, 384 * k : 384 * (k + 1)] = total(2 + k, slice(0, 384))
            if not cross:
                for k in range(4):
                    okv[:, 384 * k : 384 * (k + 1)] = total(k, slice(384, D))

        def kv_a(h):
            for i in range(3):
                v = mm_nt(b["ctxt"][...], b["dkvt"][tile(3 * h + i), :]).astype(BF)
                b["kv"][0:D, tile(3 * h + i)] = v
            if h:
                scatter("y", "k1", lambda p: b["kv"].at[tile(p, 192), D:], lambda r: b["rk1"].at[1, r])
            else:
                scatter48("z", "k1", lambda p, i: b["kv"].at[rows48(4 * i + p), 0:D], lambda r: b["rk1"].at[0, r], 16)

        def kv_b(h):
            if h:
                recv3("k1", lambda r: b["rk1"].at[1, r])
            else:
                recv48("k1", lambda r: b["rk1"].at[0, r], 16)
            for i in range(4):
                m = 4 * at["y"] + i if h else 4 * i + at["z"]
                own = b["kv"][rows48(m), h * D : (h + 1) * D]
                b["pad"][tile(i, 48), :] = add4(own, [b["rk1"][h, r, tile(i, 48)] for r in range(3)])
            cut(b["hk"].at[h], full)
            axis = "z" if h else "y"
            plane(
                "k2", axis, lambda p, p2: b["hk"].at[h, p, p2],
                lambda r, r2: b["rk2"].at[h, 4 * r + r2], 16 * h,
            )
            b["rk2"][h, 0] = b["hk"][h, at[axis], at["x"]]

        def kv_end(h):
            recv_plane("k2", b["rk2"].at[h, 1], 16 * h)
            total = add4(b["rk2"][h, 0], [b["rk2"][h, i] for i in range(1, 16)])
            okv[:, h * D : (h + 1) * D] = total[:12]

        vec_copies = []

        def vec_send(a):
            for r in (1, 2, 3):
                _, to = peer("xyz"[a], r)
                send("v", 3 * a + r - 1, b["vec"], b["rvec"].at[a, r - 1], (sec, to))
                vec_copies.append(pending.pop())

        def vec_add(a):
            for r in (1, 2, 3):
                recv("v", 3 * a + r - 1, b["rvec"].at[a, r - 1])
            for copy in vec_copies:
                copy.wait_send()
            vec_copies.clear()
            b["vec"][...] += b["rvec"][a, 0] + b["rvec"][a, 1] + b["rvec"][a, 2]

        def vec_out():
            shift = lax.rem(D - 12 * dp, D)
            rolled = pltpu.roll(b["vec"][...], shift, axis=1)
            for row, out in enumerate((og1, ob1, og2, ob2)):
                out[...] = rolled[row : row + 1, 0:12]
            bias_row = b["vec"][pl.ds(4 + at["y"], 1), :]
            shift = lax.rem(D - 48 * lax.rem(dp, 16), D)
            rolled = pltpu.roll(jnp.broadcast_to(bias_row, (8, D)), shift, axis=1)
            oub[...] = rolled[0:1, 0:48]

        if cross:
            for j in range(3):
                for m in range(4):
                    rows, at_cols = slice(m * T, (m + 1) * T), slice(j * T, (j + 1) * T)
                    b["ctxt"][at_cols, rows] = b["ctx"][rows, at_cols].T
        if cross:
            recv("back", 0, b["dyb"])
            b["dx"][...] = b["dyb"][...].astype(F32)
            gather_to(group[0], "y", lambda p: b["dyb"], rows_of(b["ry"]), other)

        for k in range(4):

            def up_back(i):
                grad = mm_nt(b["dyb"][...], b["wd"][tile(3 * k + i), :])
                du = (b["gp"][k, :, tile(i)].astype(F32) * grad).astype(BF)
                b["gp"][k, :, tile(i)] = du
                b["vec"][4 + k : 5 + k, tile(i)] = jnp.sum(du.astype(F32), axis=0, keepdims=True)

            loop(3, up_back)

        def n2_back(i):
            grad = jnp.zeros((ROWS, T), F32)
            for k in range(4):
                grad = grad + mm_nt(b["gp"][k], b["wu"][tile(i), k * D : (k + 1) * D])
            b["dn"][:, tile(i)] = grad

        loop(3, n2_back)

        def done2(rows, value):
            b["dx"][rows, :] = value
            rounded = value.astype(BF)
            b["d4"][2, rows, :] = rounded[:, 0:384]
            b["d4"][3, rows, :] = rounded[:, 384:768]

        norm_back(b["xh2"], 1, g2, 2, done2)

        def out_back(i):
            rows = tile(i)
            grad = mm_nt(b["d4"][2], b["wo"][rows, 0:384]) + mm_nt(b["d4"][3], b["wo"][rows, 384:768])
            b["do"][:, tile(i)] = grad.astype(BF)

        loop(3, out_back)

        def attend_back(i):
            s, j, rows, krows, kcols, vcols = blocks(i)
            k2, v2 = b["kv"][krows, kcols], b["kv"][krows, vcols]
            q2 = stacked(b["q"][rows, kcols])
            probs = b["p"][i, :, 0:keys]
            grad = b["do"][rows, kcols].astype(F32)
            if cross:
                grad = grad * b["inv"][rows, kcols]
            along = grad * b["o"][rows, kcols].astype(F32)
            along = jnp.concatenate([jnp.where(first_head, along, 0.0), jnp.where(first_head, 0.0, along)], axis=0)
            along = jnp.sum(along, axis=-1, keepdims=True)
            do2 = stacked(grad.astype(BF))
            ds = (probs.astype(F32) * (mm_nt(do2, v2) - along)).astype(BF)
            half, at_cols = j // 3, tile(j % 3, 128)
            b["d4"][half, rows, at_cols] = (merged(mm(ds, k2)) * 0.125).astype(BF)
            if cross:
                b["dkvt"][tile(j, 128), krows] = mm_tn(q2, ds).astype(BF)
                b["dkvt"][vcols, krows] = mm_tn(do2, probs).astype(BF)
            else:
                b["ctx"][tile(2 * half + s, SEQ), at_cols] = mm_tn(ds, q2).astype(BF)
                b["ctx"][tile(4 + 2 * half + s, SEQ), at_cols] = mm_tn(probs, do2).astype(BF)

        loop(2 * PAIRS, attend_back)
        own_b = gather_to(group_qo, "b", lambda p: b["d4"].at[p], rows_of(b["rxb"]), sec)
        if not cross:

            def kv_quarter(p):
                return b["ctx"].at[tile(p, ROWS), pl.ds(0, 384)]

            own_b2 = gather_to(
                group_qo, "b2", kv_quarter, lambda r: b["dkvt"].at[pl.ds(r * ROWS, ROWS), pl.ds(0, 384)], sec
            )

        if cross:
            kv_a(0)
            kv_a(1)

        def n1_back(i):
            rows = tile(i)
            grad = mm_nt(b["d4"][0], b["wq"][rows, 0:384]) + mm_nt(b["d4"][1], b["wq"][rows, 384:768])
            if not cross:
                for k in range(4):
                    quarter = b["ctx"][k * ROWS : (k + 1) * ROWS, 0:384]
                    grad = grad + mm_nt(quarter, b["wkv"][rows, 384 * k : 384 * (k + 1)])
            b["dn"][:, tile(i)] = grad

        loop(3, n1_back)

        def done1(rows, value):
            ins[rows, :] = value.astype(BF)

        norm_back(b["xh1"], 0, g1, 0, done1)
        if not cross:
            send("back", 0, ins, b["dyb"], (other, dp))

        vec_send(0)
        if cross:
            ffn_forward()
            down_a()
            up_a()
            vec_add(0)
            vec_send(1)
            qo_a()
            kv_b(0)
            kv_b(1)
            vec_add(1)
            vec_send(2)
            down_b()
            up_b()
            qo_b()
            vec_add(2)
            vec_out()
            kv_end(0)
            kv_end(1)
        else:
            ffn_forward()
            qo_a()
            vec_add(0)
            vec_send(1)
            down_a()
            up_a()
            vec_add(1)
            vec_send(2)
            qo_b()
            down_b()
            up_b()
            vec_add(2)
            vec_out()
        qo_end()
        down_end()
        up_end()
        for copy in pending:
            copy.wait_send()
        pl.semaphore_signal(done_sem, inc=1, device_id=(other, dp), device_id_type=MESH)
        pl.semaphore_wait(done_sem, 1)

    pl.when(sec == 0)(lambda: branch(0))
    pl.when(sec == 1)(lambda: branch(1))


def deliver(*refs):
    for a, out in zip(refs[:12], refs[12:]):
        out[...] = a[...].reshape(out.shape)


def on_device(
    tokens, context, out_cot, group_id, ctx_len, fut_len, loss_weight,
    norm_gain1, norm_bias1, w_query, w_keyval, w_out,
    norm_gain2, norm_bias2, w_up, up_bias, w_down,
):
    smem = pl.BlockSpec(memory_space=pltpu.SMEM)
    vmem = pl.BlockSpec(memory_space=pltpu.VMEM)
    hbm = pl.BlockSpec(memory_space=pl.ANY)
    shape = jax.ShapeDtypeStruct
    outs = pl.pallas_call(
        kernel,
        out_shape=(
            shape((ROWS, D), BF),
            shape((ROWS, D), BF),
            shape((1, 12), F32),
            shape((1, 12), F32),
            shape((12, D), F32),
            shape((12, 2 * D), F32),
            shape((12, D), F32),
            shape((1, 12), F32),
            shape((1, 12), F32),
            shape((12, FF), F32),
            shape((1, 48), F32),
            shape((48, D), F32),
        ),
        in_specs=[smem] * 3 + [vmem] + [hbm] * 3 + [vmem] * 5 + [hbm] * 5,
        out_specs=[vmem] * 12,
        scratch_shapes=[pltpu.VMEM(s, t) for s, t in BUFS.values()]
        + [pltpu.SemaphoreType.DMA((N_SEMS,)), pltpu.SemaphoreType.DMA((N_SEMS,)), pltpu.SemaphoreType.REGULAR],
        compiler_params=pltpu.CompilerParams(
            collective_id=0, has_side_effects=True, vmem_limit_bytes=64 * 1024 * 1024 - 4096
        ),
    )(
        group_id, ctx_len, fut_len, loss_weight,
        tokens.reshape(ROWS, D), context.reshape(2 * CTX, D), out_cot.reshape(ROWS, D),
        norm_gain1, norm_bias1, norm_gain2, norm_bias2, up_bias,
        w_query[0], w_keyval[0], w_out[0], w_up[0], w_down[0],
    )
    outs = pl.pallas_call(
        deliver,
        out_shape=[
            shape((a.shape[0], 1, a.shape[1]) if a.shape[0] == 12 else a.shape, a.dtype) for a in outs
        ],
        in_specs=[vmem] * 12,
        out_specs=[vmem] * 12,
    )(*outs)
    acts, ins, gg1, gb1, gq, gkv, go, gg2, gb2, gup, gub, gdn = outs
    seqs = (1, 2, SEQ, D)
    rows = [g.reshape(1, 12, g.shape[-1]) for g in (gq, gkv, go, gup)]
    return (
        acts.reshape(seqs), ins.reshape(seqs), gg1, gb1, *rows[:3],
        gg2, gb2, rows[3], gub, gdn[None],
    )


def solution(mesh):
    dp, sec = "dp", "section"
    vec, mat = P(sec, None), P(sec, None, None)
    return jax.shard_map(
        on_device,
        mesh=mesh,
        in_specs=(P(dp, None, None),) * 3 + (P(dp),) * 3 + (P(dp, None),)
        + (vec, vec, mat, mat, mat, vec, vec, mat, vec, mat),
        out_specs=(P(sec, dp, None, None),) * 2 + (P(sec, dp),) * 2 + (P(sec, dp, None),) * 3
        + (P(sec, dp),) * 2 + (P(sec, dp, None), P(sec, dp), P(sec, dp, None)),
        check_vma=False,
    )
```

```python
import math

import jax
import jax.numpy as jnp
from jax import lax
from jax.experimental import pallas as pl
from jax.experimental.pallas import tpu as pltpu
from jax.sharding import PartitionSpec as P

MESH = pl.DeviceIdType.MESH
BF = jnp.bfloat16
F32 = jnp.float32
GROUPS = 8
D = 768
FF = 3072
SEQ = 128
ROWS = 256
CTX = 512
PAIRS = 6
T = 256
GELU_C = math.sqrt(2.0 / math.pi)
GELU_A = 0.044715


def mm(a, b):
    return jnp.dot(a, b, preferred_element_type=F32)


def mm_nt(a, b):
    return lax.dot_general(a, b, (((1,), (1,)), ((), ())), preferred_element_type=F32)


def mm_tn(a, b):
    return lax.dot_general(a, b, (((0,), (0,)), ((), ())), preferred_element_type=F32)


def loop(n, body):
    for i in range(n):
        body(i)


def rows48(i):
    return pl.ds(pl.multiple_of(i * 48, 16), 48)


def tile(i, size=T):
    if isinstance(i, int):
        return slice(i * size, (i + 1) * size)
    return pl.ds(pl.multiple_of(i * size, size), size)


BUFS = dict(
    wq=((D, D), BF),
    wkv=((D, 2 * D), BF),
    wo=((D, D), BF),
    wu=((D, FF), BF),
    wd=((FF, D), BF),
    xb=((ROWS, D), BF),
    ctx=((2 * CTX, D), BF),
    ctxt=((D, 2 * CTX), BF),
    n1=((ROWS, D), BF),
    q=((ROWS, D), BF),
    kv=((2 * CTX, 2 * D), BF),
    p=((2 * PAIRS, ROWS, CTX), BF),
    inv=((ROWS, D), F32),
    o=((ROWS, D), BF),
    s2t=((2, D, ROWS), BF),
    n2=((ROWS, D), BF),
    x2=((ROWS, D), F32),
    xh1=((ROWS, D), F32),
    xh2=((ROWS, D), F32),
    rs=((ROWS, 2), F32),
    gp=((4, ROWS, D), BF),
    hm=((4, ROWS, D), BF),
    dyb=((ROWS, D), BF),
    dx=((ROWS, D), F32),
    d4=((4, ROWS, 384), BF),
    dkvt=((2 * D, 2 * CTX), BF),
    vec=((8, D), F32),
    rvec=((3, 3, 8, D), F32),
    tot=((8, 128), F32),
    rtot=((3, 3, 8, 128), F32),
    b4=((8, D), F32),
    rb4=((8, D), F32),
    wuq=((D, D), BF),
    wdq=((D, D), BF),
    rn=((4 * ROWS, D), BF),
    rnt=((D, 4 * ROWS), BF),
    ry=((4 * ROWS, D), BF),
    hxt=((D, 4 * ROWS), BF),
    gx=((4 * ROWS, D), BF),
    rd1=((3, 4, 48, D), BF),
    hd=((4, 48, D), BF),
    rd2=((4, 48, D), BF),
    ru1=((3, 192, D), BF),
    hu=((4, 4, 16, D), BF),
    ru2=((4, 4, 16, D), BF),
    rxa=((D, 4 * ROWS), BF),
    rxb=((4 * ROWS, 384), BF),
    gq=((4, 192, D), BF),
    rq1=((3, 192, D), BF),
    hq=((4, 4, 16, D), BF),
    rq2=((4, 4, 16, D), BF),
    rk1=((2, 3, 192, D), BF),
    hk=((2, 4, 4, 16, D), BF),
    rk2=((2, 16, 16, D), BF),
)
KEYS = {}
for _name, _n in dict(
    tot=9, act=1, back=1, a=4, n=4, y=4, w=3, b=4, a2=4, b2=4,
    d1=4, d2=4, u1=16, u2=16, q1=4, q2=16, k1=32, k2=32, v=9, load=8,
).items():
    KEYS[_name] = sum(KEYS.values()) if not KEYS else _total
    _total = KEYS[_name] + _n
N_SEMS = _total
NAMES = list(BUFS)


def kernel(*refs):
    (gid, clen, flen, lw, tokens, ctx_in, cot_in, g1, b1, g2, b2, bu, wq_in, wkv_in, wo_in, wu_in, wd_in) = refs[:17]
    (acts, ins, og1, ob1, oq, okv, oo, og2, ob2, oup, oub, odn) = refs[17:29]
    b = dict(zip(NAMES, refs[29 : 29 + len(NAMES)]))
    b["do"] = b["n1"]
    b["dn"] = b["x2"]
    b["pad"] = b["x2"].at[pl.ds(0, 208)]
    b["gd"] = b["gp"].at[:, pl.ds(0, 192)]
    b["gu"] = b["hm"].at[:, pl.ds(0, 192)]
    ssem, rsem = refs[29 + len(NAMES) :]

    sec = lax.axis_index("section")
    dp = lax.axis_index("dp")
    at = {"y": dp // 16, "z": (dp // 4) % 4, "x": dp % 4}
    step = {"y": 16, "z": 4, "x": 1}
    other = 1 - sec

    def peer(axis, r):
        p = lax.rem(at[axis] + r, 4)
        return p, dp + (p - at[axis]) * step[axis]

    def peer2(axis, r, axis2, r2):
        p, to = peer(axis, r)
        p2, to2 = peer(axis2, r2)
        return p, p2, to + to2 - dp

    barrier = pltpu.get_barrier_semaphore()
    pl.semaphore_signal(barrier, inc=1, device_id=(other, dp), device_id_type=MESH)
    near = [peer(axis, r)[1] for axis in "xyz" for r in (1, 2, 3)]
    for axis, axis2 in ("yx", "zx", "yz"):
        near += [peer2(axis, r, axis2, r2)[2] for r in (1, 2, 3) for r2 in (1, 2, 3)]
    for to in near:
        for core in (sec, other):
            pl.semaphore_signal(barrier, inc=1, device_id=(core, to), device_id_type=MESH)

    def branch(mine):
        cross = mine == 0
        group = {0: "y", 1: "z"}
        group_qo = "z" if cross else "x"
        pending = []

        def send(key, i, src, dst, device, slot=None, when=None):
            k = KEYS[key] + i
            copy = pltpu.make_async_remote_copy(
                src_ref=src, dst_ref=dst, send_sem=ssem.at[k],
                recv_sem=rsem.at[k if slot is None else KEYS[key] + slot],
                device_id=device, device_id_type=MESH,
            )
            if when is None:
                copy.start()
                pending.append(copy.wait_send)
            else:
                pl.when(when)(copy.start)
                pending.append(lambda: pl.when(when)(copy.wait_send))

        def recv(key, i, ref):
            k = KEYS[key] + i
            pltpu.make_async_remote_copy(
                src_ref=ref, dst_ref=ref, send_sem=ssem.at[k], recv_sem=rsem.at[k],
                device_id=(other, dp), device_id_type=MESH,
            ).wait_recv()

        def local(key, i, src, dst):
            copy = pltpu.make_async_copy(src, dst, rsem.at[KEYS[key] + i])
            copy.start()
            return copy

        loads = {}

        def load(name, i, src, dst):
            loads[name] = local("load", i, src, dst)

        if cross:
            load("x", 0, tokens, b["xb"])
            load("wq", 3, wq_in, b["wq"])
            load("ctx", 1, ctx_in, b["ctx"])
            load("wkv", 2, wkv_in, b["wkv"])
        else:
            load("cot", 0, cot_in, b["do"])
            load("wq", 3, wq_in, b["wq"])
            load("wkv", 2, wkv_in, b["wkv"])
        load("wo", 4, wo_in, b["wo"])
        load("wu", 5, wu_in, b["wu"])
        load("wd", 6, wd_in, b["wd"])

        lane = lax.broadcasted_iota(jnp.int32, (1, 128), 1)
        first_head = lane < 64
        mask_a = first_head.astype(F32).astype(BF)
        mask_b = 1.0 - mask_a

        def stacked(v):
            return jnp.concatenate([v * mask_a, v * mask_b], axis=0)

        def merged(v):
            return jnp.where(first_head, v[:SEQ], v[SEQ:])

        def norm(src, gain, bias, xh, rs, n, nt):
            def body(i):
                rows = tile(i, 32)
                v = src[rows, :].astype(F32)
                centre = v - jnp.mean(v, axis=-1, keepdims=True)
                spread = jnp.mean(centre * centre, axis=-1, keepdims=True)
                scale = lax.rsqrt(spread + 1e-05)
                hat = centre * scale
                xh[rows, :] = hat
                b["rs"][rows, rs : rs + 1] = scale
                n[rows, :] = (hat * gain[...] + bias[...]).astype(BF)

            loop(8, body)
            if nt is not None:
                for j in range(3):
                    nt[j * T : (j + 1) * T, :] = n[:, j * T : (j + 1) * T].T

        def norm_back(xh, rs, gain, row, done):
            def body(i, carry):
                sum_g, sum_b = carry
                rows = tile(i, 32)
                grad = b["dn"][rows, :]
                hat = xh[rows, :]
                sum_g = sum_g + (grad * hat).reshape(4, 8, D).sum(0)
                sum_b = sum_b + grad.reshape(4, 8, D).sum(0)
                scaled = grad * gain[...]
                mean = jnp.mean(scaled, axis=-1, keepdims=True)
                along = jnp.mean(scaled * hat, axis=-1, keepdims=True)
                done(rows, b["dx"][rows, :] + b["rs"][rows, rs : rs + 1] * (scaled - mean - hat * along))
                return sum_g, sum_b

            sums = (jnp.zeros((8, D), F32),) * 2
            for i in range(8):
                sums = body(i, sums)
            sum_g, sum_b = sums
            b["vec"][row : row + 1, :] = sum_g.sum(0, keepdims=True)
            b["vec"][row + 1 : row + 2, :] = sum_b.sum(0, keepdims=True)

        def gather_to(axis, key, src_of, dst_of, core):
            for r in (1, 3, 2):
                p, to = peer(axis, r)
                send(key, r, src_of(p), dst_of(r), (core, to))
            if core is other:
                send(key, 0, src_of(at[axis]), dst_of(0), (core, dp))
                return None
            return local(key, 0, src_of(at[axis]), dst_of(0))

        def gather_some(axis, key, src, dst_of, chosen):
            for r in (1, 3, 2):
                p, to = peer(axis, r)
                send(key, r, src, dst_of(r), (sec, to), when=chosen(p))

        def cols(ref):
            return lambda r: ref.at[:, pl.ds(r * ROWS, ROWS)]

        def rows_of(ref):
            return lambda r: ref.at[pl.ds(r * ROWS, ROWS)]

        def scatter(axis, key, src_of, dst_of, base=0, core=sec):
            for r in (1, 3, 2):
                p, to = peer(axis, r)
                send(key, base + r, src_of(p), dst_of(r - 1), (core, to))

        def scatter48(axis, key, src_of, dst_of, base=0):
            for r in (1, 3, 2):
                p, to = peer(axis, r)
                for i in range(4):
                    send(key, base + 4 * r + i, src_of(p, i), dst_of(r - 1).at[tile(i, 48)], (sec, to))

        def recv48(key, dst_of, base=0):
            for r in (1, 3, 2):
                for i in range(4):
                    recv(key, base + 4 * r + i, dst_of(r - 1).at[tile(i, 48)])

        def recv3(key, dst_of, base=0):
            for r in (1, 3, 2):
                recv(key, base + r, dst_of(r - 1))

        def send_quarter():
            q = at[group[mine]]
            for k in range(4):
                b["b4"][k : k + 1, :] = bu[:, k * D : (k + 1) * D]
            b["b4"][4:8, :] = jnp.zeros((4, D), F32)
            send("w", 0, b["b4"], b["rb4"], (other, dp))
            loads["wu"].wait()
            send("w", 1, b["wu"].at[:, tile(q, D)], b["wuq"], (other, dp))
            loads["wd"].wait()
            send("w", 2, b["wd"].at[tile(q, D), :], b["wdq"], (other, dp))

        if not cross:
            weighted, ids = [], []
            total = jnp.zeros((1, 128), F32)
            for s in range(2):
                w = jnp.where(lane < flen[s], lw[s : s + 1, :].astype(F32), 0.0)
                total = total + jnp.where(lane == gid[s], jnp.sum(w, axis=1, keepdims=True), 0.0)
                weighted.append(w)
            b["tot"][...] = jnp.broadcast_to(total, (8, 128))
        if not cross:
            pl.semaphore_wait(barrier, 1 + 2 * len(near))
            for a, axis in enumerate("xyz"):
                for r in (1, 2, 3):
                    _, to = peer(axis, r)
                    send("tot", 3 * a + r - 1, b["tot"], b["rtot"].at[a, r - 1], (sec, to))
                for r in (1, 2, 3):
                    recv("tot", 3 * a + r - 1, b["rtot"].at[a, r - 1])
                for wait in pending:
                    wait()
                pending.clear()
                b["tot"][...] += b["rtot"][a, 0] + b["rtot"][a, 1] + b["rtot"][a, 2]
            totals = b["tot"][0:1, :]
            every = jnp.sum(totals, axis=1, keepdims=True)
            factors = every / (GROUPS * jnp.maximum(totals, 1.0))
            loads["cot"].wait()
            diagonal = lax.broadcasted_iota(jnp.int32, (SEQ, SEQ), 0) == lax.broadcasted_iota(
                jnp.int32, (SEQ, SEQ), 1
            )
            for s in range(2):
                factor = jnp.sum(jnp.where(lane == gid[s], factors, 0.0), axis=1, keepdims=True)
                picked = jnp.where(diagonal, weighted[s], 0.0).astype(BF)
                rows = slice(s * SEQ, (s + 1) * SEQ)
                grad = mm(picked, b["do"][rows, :]) * factor
                b["dx"][rows, :] = grad
                b["dyb"][rows, :] = grad.astype(BF)
            gather_to(group[1], "y", lambda p: b["dyb"], rows_of(b["ry"]), other)
            send_quarter()

        if cross:
            loads["x"].wait()
        else:
            recv("act", 0, b["xb"])
        norm(b["xb"], g1, b1, b["xh1"], 0, b["n1"], b["s2t"].at[0])

        if not cross:
            own_a2 = gather_to(group_qo, "a2", lambda p: b["s2t"].at[0], cols(b["ctxt"]), sec)
        loads["wq"].wait()

        def query(i):
            b["q"][:, tile(i)] = (mm(b["n1"][...], b["wq"][:, tile(i)]).astype(BF) * 0.125).astype(BF)

        loop(3, query)

        loads["wkv"].wait()
        if cross:
            loads["ctx"].wait()

            def keyval(i):
                for m in range(4):
                    rows = slice(m * T, (m + 1) * T)
                    b["kv"][rows, tile(i)] = mm(b["ctx"][rows, :], b["wkv"][:, tile(i)]).astype(BF)
        else:

            def keyval(i):
                b["kv"][0:ROWS, tile(i)] = mm(b["n1"][...], b["wkv"][:, tile(i)]).astype(BF)

        loop(6, keyval)
        keys = CTX if cross else SEQ
        if cross:
            pl.semaphore_wait(barrier, 1 + 2 * len(near))
            gather_some(group_qo, "a", b["s2t"].at[0], cols(b["rxa"]), lambda p: p < 2)

        def blocks(i):
            s, j = i // PAIRS, i % PAIRS
            vcols = slice(D + 128 * j, D + 128 * (j + 1))
            return s, j, tile(s, SEQ), tile(s, keys), tile(j, 128), vcols

        if cross:
            key = lax.broadcasted_iota(jnp.int32, (1, keys), 1)
            masks = [jnp.where(key < clen[s], 0.0, -1e9) for s in range(2)]
        else:
            row = lax.broadcasted_iota(jnp.int32, (SEQ, keys), 0)
            mask = jnp.where(lax.broadcasted_iota(jnp.int32, (SEQ, keys), 1) <= row, 0.0, -1e9)
            masks = [jnp.concatenate([mask, mask], axis=0)] * 2
        ones = jnp.ones((keys, 128), BF)

        def attend(i):
            s, j, rows, krows, kcols, vcols = blocks(i)
            scores = mm_nt(stacked(b["q"][rows, kcols]), b["kv"][krows, kcols]) + masks[s]
            e = jnp.exp(scores - jnp.max(scores, axis=-1, keepdims=True))
            values = b["kv"][krows, vcols]
            if cross:
                e = e.astype(BF)
                b["p"][i] = e
                mixed = mm(e, jnp.concatenate([values, ones], axis=1))
                scale = 1.0 / merged(mixed[:, 128:])
                b["inv"][rows, kcols] = scale
                b["o"][rows, kcols] = (merged(mixed[:, :128]) * scale).astype(BF)
            else:
                probs = (e / jnp.sum(e, axis=-1, keepdims=True)).astype(BF)
                b["p"][i, :, 0:keys] = probs
                b["o"][rows, kcols] = merged(mm(probs, values)).astype(BF)

        loop(2 * PAIRS, attend)
        for j in range(3):
            b["s2t"][1, j * T : (j + 1) * T, :] = b["o"][:, j * T : (j + 1) * T].T
        gather_some(group_qo, "a", b["s2t"].at[1], cols(b["rxa"]), lambda p: p >= 2)
        own_a = local("a", 0, b["s2t"].at[at[group_qo] // 2], cols(b["rxa"])(0))

        loads["wo"].wait()

        def project(i):
            b["x2"][:, tile(i)] = b["xb"][:, tile(i)].astype(F32) + mm(b["o"][...], b["wo"][:, tile(i)])

        loop(3, project)
        norm(b["x2"], g2, b2, b["xh2"], 1, b["n2"], None)
        gather_to(group[mine], "n", lambda p: b["n2"], rows_of(b["rn"]), other)
        if cross:
            send_quarter()

        def gelu(u):
            square = u * u
            th = jnp.tanh(u * (GELU_C + (GELU_C * GELU_A) * square))
            half = 0.5 + 0.5 * th
            slope = half + (u * (0.5 - 0.5 * th * th)) * (GELU_C + (3.0 * GELU_A * GELU_C) * square)
            return (u * half).astype(BF), slope.astype(BF)

        def up(i):
            u = mm(b["n2"][...], b["wu"][:, tile(i)]) + bu[:, tile(i)]
            k, at_cols = i // 3, tile(i % 3)
            b["hm"][k, :, at_cols], b["gp"][k, :, at_cols] = gelu(u)

        loop(12, up)

        def down(i):
            y = b["x2"][:, tile(i)]
            for k in range(4):
                y = y + mm(b["hm"][k], b["wd"][k * D : (k + 1) * D, tile(i)])
            acts[:, tile(i)] = y.astype(BF)

        loop(3, down)
        if cross:
            send("act", 0, acts, b["xb"], (other, dp))

        def add4(own, parts):
            total = own.astype(F32)
            for part in parts:
                total = total + part.astype(F32)
            return total

        def plane(key, axis, src_of, dst, base=0, core=sec):
            for r in (1, 3, 2, 0):
                for r2 in (1, 3, 2, 0):
                    if r or r2 or core is other:
                        p, p2, to = peer2(axis, r, "x", r2)
                        send(key, base + 4 * r + r2, src_of(p, p2), dst(r, r2), (core, to))

        def recv_plane(key, ref, base=0, first=1):
            for i in range(first, 16):
                recv(key, base + i, ref)

        def cut(dst, cols):
            for k in range(4):
                for j in range(4):
                    start = 48 * k + 12 * j
                    dst[k, j, :, cols] = b["pad"][start : start + 16, cols].astype(BF)

        full = slice(0, D)

        theirs = 1 - mine

        def ffn_forward():
            for i, name in enumerate(("rb4", "wuq", "wdq")):
                recv("w", i, b[name])
            for r in range(4):
                recv("n", r, rows_of(b["rn"])(r))
            bias = b["rb4"][pl.ds(at[group[theirs]], 1), :]
            for m in range(4):
                for i in range(3):
                    u = mm(b["rn"][tile(m), :], b["wuq"][:, tile(i)]) + bias[:, tile(i)]
                    hidden, b["gx"][tile(m), tile(i)] = gelu(u)
                    b["hxt"][tile(i), tile(m)] = hidden.T
                    b["rnt"][tile(i), tile(m)] = b["rn"][tile(m), tile(i)].T

        def down_a():
            for r in range(4):
                recv("y", r, rows_of(b["ry"])(r))
            for i in range(3):
                v = mm(b["hxt"][...], b["ry"][:, tile(i)]).astype(BF)
                b["gd"][:, :, tile(i)] = v.reshape(4, 192, T)
            scatter("x", "d1", lambda p: b["gd"].at[:, rows48(p)], lambda r: b["rd1"].at[r])

        def down_b():
            recv3("d1", lambda r: b["rd1"].at[r])
            for i in range(4):
                b["hd"][i] = add4(b["gd"][i, rows48(at["x"])], [b["rd1"][r, i] for r in range(3)]).astype(BF)
            if theirs == 0:
                for r in (1, 3, 2, 0):
                    p, to = peer("z", r)
                    send("d2", r, b["hd"].at[p], b["rd2"].at[r], (other, to))
            else:
                to = dp + (at["z"] - at["y"]) * step["y"]
                for r in (1, 3, 2, 0):
                    p, there = peer("z", r)
                    send("d2", r, b["hd"].at[p], b["rd2"].at[at["y"]], (other, to + there - dp), at["y"])

        def down_end():
            for r in range(4):
                recv("d2", r, b["rd2"].at[r])
            odn[...] = add4(b["rd2"][0], [b["rd2"][r] for r in (1, 2, 3)])

        def up_axes(layer):
            return ("y", "z") if layer == 1 else ("z", "y")

        def up_a():
            axis = up_axes(theirs)[0]
            for m in range(4):
                for i in range(3):
                    grad = mm_nt(b["ry"][tile(m), :], b["wdq"][tile(i), :])
                    b["gx"][tile(m), tile(i)] = (b["gx"][tile(m), tile(i)].astype(F32) * grad).astype(BF)
            for i in range(3):
                v = mm(b["rnt"][...], b["gx"][:, tile(i)]).astype(BF)
                b["gu"][:, :, tile(i)] = v.reshape(4, 192, T)
            if axis == "y":
                scatter(axis, "u1", lambda p: b["gu"].at[p], lambda r: b["ru1"].at[r])
            else:
                scatter48(axis, "u1", lambda p, i: b["gu"].at[i, rows48(p)], lambda r: b["ru1"].at[r])

        def up_b():
            axis, rest = up_axes(theirs)
            (recv3 if axis == "y" else recv48)("u1", lambda r: b["ru1"].at[r])
            for i in range(4):
                if axis == "y":
                    own, parts = b["gu"][at["y"], tile(i, 48)], [b["ru1"][r, tile(i, 48)] for r in range(3)]
                else:
                    own, parts = b["gu"][i, rows48(at["z"])], [b["ru1"][r, tile(i, 48)] for r in range(3)]
                b["pad"][tile(i, 48), :] = add4(own, parts)
            cut(b["hu"], full)
            plane(
                "u2", rest, lambda p, p2: b["hu"].at[p, p2],
                lambda r, r2: b["ru2"].at[at[rest], r2], core=other,
            )

        def up_end():
            recv_plane("u2", b["ru2"].at[0, 0], first=0)
            for k in range(4):
                total = add4(b["ru2"][k, 0], [b["ru2"][k, r] for r in (1, 2, 3)])
                oup[:, k * D : (k + 1) * D] = total[:12]

        width = 384 if cross else D
        part = slice(0, width)

        def qo_a():
            own_a.wait()
            own_b.wait()
            makes_out = at[group_qo] >= 2

            def recv_a():
                for r in range(1, 4):
                    recv("a", r, cols(b["rxa"])(r))

            if cross:
                recv_a()
            else:
                pl.when(makes_out)(recv_a)
            for r in range(1, 4):
                recv("b", r, rows_of(b["rxb"])(r))
            if not cross:
                own_a2.wait()
                own_b2.wait()
                for r in range(1, 4):
                    recv("a2", r, cols(b["ctxt"])(r))
                    recv("b2", r, b["dkvt"].at[pl.ds(r * ROWS, ROWS), pl.ds(0, 384)])

            def make(from_ref):
                for i in range(2):
                    v = mm(from_ref[tile(i, 384), :], b["rxb"][...]).astype(BF)
                    b["gq"][2 * i : 2 * i + 2, :, 0:384] = v.reshape(2, 192, 384)

            if cross:
                make(b["rxa"])
            else:
                pl.when(makes_out)(lambda: make(b["rxa"]))
                pl.when(jnp.logical_not(makes_out))(lambda: make(b["ctxt"]))
                for i in range(2):
                    v = mm(b["ctxt"][tile(i, 384), :], b["dkvt"][0:1024, 0:384]).astype(BF)
                    b["gq"][2 * i : 2 * i + 2, :, 384:768] = v.reshape(2, 192, 384)
            scatter("y", "q1", lambda p: b["gq"].at[p, :, pl.ds(0, width)], lambda r: b["rq1"].at[r, :, pl.ds(0, width)])

        def qo_b():
            recv3("q1", lambda r: b["rq1"].at[r, :, pl.ds(0, width)])
            for i in range(4):
                rows = tile(i, 48)
                b["pad"][rows, part] = add4(b["gq"][at["y"], rows, part], [b["rq1"][r, rows, part] for r in range(3)])
            cut(b["hq"], part)
            if cross:
                slot = lambda r, r2: b["rq2"].at[at["z"], r2, :, pl.ds(0, width)]
            else:
                slot = lambda r, r2: b["rq2"].at[at["x"], r, :, pl.ds(0, width)]
            plane("q2", "z", lambda p, p2: b["hq"].at[p, p2, :, pl.ds(0, width)], slot)
            b["rq2"][at[group_qo], 0, :, part] = b["hq"][at["z"], at["x"], :, part]

        def qo_end():
            recv_plane("q2", b["rq2"].at[0, 0, :, pl.ds(0, width)])

            def total(k, at_cols):
                return add4(b["rq2"][k, 0, :, at_cols], [b["rq2"][k, r, :, at_cols] for r in (1, 2, 3)])[:12]

            for k in range(2):
                oq[:, 384 * k : 384 * (k + 1)] = total(k, slice(0, 384))
                oo[:, 384 * k : 384 * (k + 1)] = total(2 + k, slice(0, 384))
            if not cross:
                for k in range(4):
                    okv[:, 384 * k : 384 * (k + 1)] = total(k, slice(384, D))

        def kv_a(h):
            for i in range(3):
                v = mm_nt(b["ctxt"][...], b["dkvt"][tile(3 * h + i), :]).astype(BF)
                b["kv"][0:D, tile(3 * h + i)] = v
            if h:
                scatter("y", "k1", lambda p: b["kv"].at[tile(p, 192), D:], lambda r: b["rk1"].at[1, r])
            else:
                scatter48("z", "k1", lambda p, i: b["kv"].at[rows48(4 * i + p), 0:D], lambda r: b["rk1"].at[0, r], 16)

        def kv_b(h):
            if h:
                recv3("k1", lambda r: b["rk1"].at[1, r])
            else:
                recv48("k1", lambda r: b["rk1"].at[0, r], 16)
            for i in range(4):
                m = 4 * at["y"] + i if h else 4 * i + at["z"]
                own = b["kv"][rows48(m), h * D : (h + 1) * D]
                b["pad"][tile(i, 48), :] = add4(own, [b["rk1"][h, r, tile(i, 48)] for r in range(3)])
            cut(b["hk"].at[h], full)
            axis = "z" if h else "y"
            plane(
                "k2", axis, lambda p, p2: b["hk"].at[h, p, p2],
                lambda r, r2: b["rk2"].at[h, 4 * r + r2], 16 * h,
            )
            b["rk2"][h, 0] = b["hk"][h, at[axis], at["x"]]

        def kv_end(h):
            recv_plane("k2", b["rk2"].at[h, 1], 16 * h)
            total = add4(b["rk2"][h, 0], [b["rk2"][h, i] for i in range(1, 16)])
            okv[:, h * D : (h + 1) * D] = total[:12]

        vec_copies = []

        def vec_send(a):
            for r in (1, 2, 3):
                _, to = peer("xyz"[a], r)
                send("v", 3 * a + r - 1, b["vec"], b["rvec"].at[a, r - 1], (sec, to))
                vec_copies.append(pending.pop())

        def vec_add(a):
            for r in (1, 2, 3):
                recv("v", 3 * a + r - 1, b["rvec"].at[a, r - 1])
            for wait in vec_copies:
                wait()
            vec_copies.clear()
            b["vec"][...] += b["rvec"][a, 0] + b["rvec"][a, 1] + b["rvec"][a, 2]

        def vec_out():
            shift = lax.rem(D - 12 * dp, D)
            rolled = pltpu.roll(b["vec"][...], shift, axis=1)
            for row, out in enumerate((og1, ob1, og2, ob2)):
                out[...] = rolled[row : row + 1, 0:12]
            bias_row = b["vec"][pl.ds(4 + at["y"], 1), :]
            shift = lax.rem(D - 48 * lax.rem(dp, 16), D)
            rolled = pltpu.roll(jnp.broadcast_to(bias_row, (8, D)), shift, axis=1)
            oub[...] = rolled[0:1, 0:48]

        if cross:
            for j in range(3):
                for m in range(4):
                    rows, at_cols = slice(m * T, (m + 1) * T), slice(j * T, (j + 1) * T)
                    b["ctxt"][at_cols, rows] = b["ctx"][rows, at_cols].T
        if cross:
            recv("back", 0, b["dyb"])
            b["dx"][...] = b["dyb"][...].astype(F32)
            gather_to(group[0], "y", lambda p: b["dyb"], rows_of(b["ry"]), other)

        for k in range(4):

            def up_back(i):
                grad = mm_nt(b["dyb"][...], b["wd"][tile(3 * k + i), :])
                du = (b["gp"][k, :, tile(i)].astype(F32) * grad).astype(BF)
                b["gp"][k, :, tile(i)] = du
                b["vec"][4 + k : 5 + k, tile(i)] = jnp.sum(du.astype(F32), axis=0, keepdims=True)

            loop(3, up_back)

        def n2_back(i):
            grad = jnp.zeros((ROWS, T), F32)
            for k in range(4):
                grad = grad + mm_nt(b["gp"][k], b["wu"][tile(i), k * D : (k + 1) * D])
            b["dn"][:, tile(i)] = grad

        loop(3, n2_back)

        def done2(rows, value):
            b["dx"][rows, :] = value
            rounded = value.astype(BF)
            b["d4"][2, rows, :] = rounded[:, 0:384]
            b["d4"][3, rows, :] = rounded[:, 384:768]

        norm_back(b["xh2"], 1, g2, 2, done2)

        def out_back(i):
            rows = tile(i)
            grad = mm_nt(b["d4"][2], b["wo"][rows, 0:384]) + mm_nt(b["d4"][3], b["wo"][rows, 384:768])
            b["do"][:, tile(i)] = grad.astype(BF)

        loop(3, out_back)

        def attend_back(i):
            s, j, rows, krows, kcols, vcols = blocks(i)
            k2, v2 = b["kv"][krows, kcols], b["kv"][krows, vcols]
            q2 = stacked(b["q"][rows, kcols])
            probs = b["p"][i, :, 0:keys]
            grad = b["do"][rows, kcols].astype(F32)
            if cross:
                grad = grad * b["inv"][rows, kcols]
            along = grad * b["o"][rows, kcols].astype(F32)
            along = jnp.concatenate([jnp.where(first_head, along, 0.0), jnp.where(first_head, 0.0, along)], axis=0)
            along = jnp.sum(along, axis=-1, keepdims=True)
            do2 = stacked(grad.astype(BF))
            ds = (probs.astype(F32) * (mm_nt(do2, v2) - along)).astype(BF)
            half, at_cols = j // 3, tile(j % 3, 128)
            b["d4"][half, rows, at_cols] = (merged(mm(ds, k2)) * 0.125).astype(BF)
            if cross:
                b["dkvt"][tile(j, 128), krows] = mm_tn(q2, ds).astype(BF)
                b["dkvt"][vcols, krows] = mm_tn(do2, probs).astype(BF)
            else:
                b["ctx"][tile(2 * half + s, SEQ), at_cols] = mm_tn(ds, q2).astype(BF)
                b["ctx"][tile(4 + 2 * half + s, SEQ), at_cols] = mm_tn(probs, do2).astype(BF)

        loop(2 * PAIRS, attend_back)
        own_b = gather_to(group_qo, "b", lambda p: b["d4"].at[p], rows_of(b["rxb"]), sec)
        if not cross:

            def kv_quarter(p):
                return b["ctx"].at[tile(p, ROWS), pl.ds(0, 384)]

            own_b2 = gather_to(
                group_qo, "b2", kv_quarter, lambda r: b["dkvt"].at[pl.ds(r * ROWS, ROWS), pl.ds(0, 384)], sec
            )

        if cross:
            kv_a(1)
            kv_a(0)

        def n1_back(i):
            rows = tile(i)
            grad = mm_nt(b["d4"][0], b["wq"][rows, 0:384]) + mm_nt(b["d4"][1], b["wq"][rows, 384:768])
            if not cross:
                for k in range(4):
                    quarter = b["ctx"][k * ROWS : (k + 1) * ROWS, 0:384]
                    grad = grad + mm_nt(quarter, b["wkv"][rows, 384 * k : 384 * (k + 1)])
            b["dn"][:, tile(i)] = grad

        loop(3, n1_back)

        def done1(rows, value):
            ins[rows, :] = value.astype(BF)

        norm_back(b["xh1"], 0, g1, 0, done1)
        if not cross:
            send("back", 0, ins, b["dyb"], (other, dp))

        if cross:
            vec_send(0)
            ffn_forward()
            down_a()
            up_a()
            vec_add(0)
            vec_send(1)
            qo_a()
            kv_b(1)
            kv_b(0)
            vec_add(1)
            vec_send(2)
            qo_b()
            down_b()
            up_b()
            vec_add(2)
            vec_out()
            kv_end(0)
            kv_end(1)
        else:
            vec_send(0)
            ffn_forward()
            vec_add(0)
            vec_send(1)
            down_a()
            up_a()
            vec_add(1)
            vec_send(2)
            qo_a()
            down_b()
            up_b()
            qo_b()
            vec_add(2)
            vec_out()
        qo_end()
        down_end()
        up_end()
        for wait in pending:
            wait()

    pl.when(sec == 0)(lambda: branch(0))
    pl.when(sec == 1)(lambda: branch(1))


def deliver(*refs):
    for a, out in zip(refs[:12], refs[12:]):
        out[...] = a[...].reshape(out.shape)


def on_device(
    tokens, context, out_cot, group_id, ctx_len, fut_len, loss_weight,
    norm_gain1, norm_bias1, w_query, w_keyval, w_out,
    norm_gain2, norm_bias2, w_up, up_bias, w_down,
):
    smem = pl.BlockSpec(memory_space=pltpu.SMEM)
    vmem = pl.BlockSpec(memory_space=pltpu.VMEM)
    hbm = pl.BlockSpec(memory_space=pl.ANY)
    shape = jax.ShapeDtypeStruct
    outs = pl.pallas_call(
        kernel,
        out_shape=(
            shape((ROWS, D), BF),
            shape((ROWS, D), BF),
            shape((1, 12), F32),
            shape((1, 12), F32),
            shape((12, D), F32),
            shape((12, 2 * D), F32),
            shape((12, D), F32),
            shape((1, 12), F32),
            shape((1, 12), F32),
            shape((12, FF), F32),
            shape((1, 48), F32),
            shape((48, D), F32),
        ),
        in_specs=[smem] * 3 + [vmem] + [hbm] * 3 + [vmem] * 5 + [hbm] * 5,
        out_specs=[vmem] * 12,
        scratch_shapes=[pltpu.VMEM(s, t) for s, t in BUFS.values()]
        + [pltpu.SemaphoreType.DMA((N_SEMS,)), pltpu.SemaphoreType.DMA((N_SEMS,))],
        compiler_params=pltpu.CompilerParams(
            collective_id=0, has_side_effects=True, vmem_limit_bytes=64 * 1024 * 1024 - 4096
        ),
    )(
        group_id, ctx_len, fut_len, loss_weight,
        tokens.reshape(ROWS, D), context.reshape(2 * CTX, D), out_cot.reshape(ROWS, D),
        norm_gain1, norm_bias1, norm_gain2, norm_bias2, up_bias,
        w_query[0], w_keyval[0], w_out[0], w_up[0], w_down[0],
    )
    outs = pl.pallas_call(
        deliver,
        out_shape=[
            shape((a.shape[0], 1, a.shape[1]) if a.shape[0] == 12 else a.shape, a.dtype) for a in outs
        ],
        in_specs=[vmem] * 12,
        out_specs=[vmem] * 12,
    )(*outs)
    acts, ins, gg1, gb1, gq, gkv, go, gg2, gb2, gup, gub, gdn = outs
    seqs = (1, 2, SEQ, D)
    rows = [g.reshape(1, 12, g.shape[-1]) for g in (gq, gkv, go, gup)]
    return (
        acts.reshape(seqs), ins.reshape(seqs), gg1, gb1, *rows[:3],
        gg2, gb2, rows[3], gub, gdn[None],
    )


def solution(mesh):
    dp, sec = "dp", "section"
    vec, mat = P(sec, None), P(sec, None, None)
    return jax.shard_map(
        on_device,
        mesh=mesh,
        in_specs=(P(dp, None, None),) * 3 + (P(dp),) * 3 + (P(dp, None),)
        + (vec, vec, mat, mat, mat, vec, vec, mat, vec, mat),
        out_specs=(P(sec, dp, None, None),) * 2 + (P(sec, dp),) * 2 + (P(sec, dp, None),) * 3
        + (P(sec, dp),) * 2 + (P(sec, dp, None), P(sec, dp), P(sec, dp, None)),
        check_vma=False,
    )
```

```python
import math

import jax
import jax.numpy as jnp
from jax import lax
from jax.experimental import pallas as pl
from jax.experimental.pallas import tpu as pltpu
from jax.sharding import PartitionSpec as P

MESH = pl.DeviceIdType.MESH
BF = jnp.bfloat16
F32 = jnp.float32
GROUPS = 8
D = 768
FF = 3072
SEQ = 128
ROWS = 256
CTX = 512
PAIRS = 6
T = 256
GELU_C = math.sqrt(2.0 / math.pi)
GELU_A = 0.044715


def mm(a, b):
    return jnp.dot(a, b, preferred_element_type=F32)


def mm_nt(a, b):
    return lax.dot_general(a, b, (((1,), (1,)), ((), ())), preferred_element_type=F32)


def mm_tn(a, b):
    return lax.dot_general(a, b, (((0,), (0,)), ((), ())), preferred_element_type=F32)


def loop(n, body):
    for i in range(n):
        body(i)


def rows48(i):
    return pl.ds(pl.multiple_of(i * 48, 16), 48)


def tile(i, size=T):
    if isinstance(i, int):
        return slice(i * size, (i + 1) * size)
    return pl.ds(pl.multiple_of(i * size, size), size)


BUFS = dict(
    wq=((D, D), BF),
    wkv=((D, 2 * D), BF),
    wo=((D, D), BF),
    wu=((D, FF), BF),
    wd=((FF, D), BF),
    xb=((ROWS, D), BF),
    ctx=((2 * CTX, D), BF),
    ctxt=((D, 2 * CTX), BF),
    n1=((ROWS, D), BF),
    q=((ROWS, D), BF),
    kv=((2 * CTX, 2 * D), BF),
    p=((2 * PAIRS, ROWS, CTX), BF),
    inv=((ROWS, D), F32),
    o=((ROWS, D), BF),
    s2t=((2, D, ROWS), BF),
    n2=((ROWS, D), BF),
    x2=((ROWS, D), F32),
    xh1=((ROWS, D), F32),
    xh2=((ROWS, D), F32),
    rs=((ROWS, 2), F32),
    gp=((4, ROWS, D), BF),
    hm=((4, ROWS, D), BF),
    dyb=((ROWS, D), BF),
    dx=((ROWS, D), F32),
    d4=((4, ROWS, 384), BF),
    dkvt=((2 * D, 2 * CTX), BF),
    vec=((8, D), F32),
    rvec=((3, 3, 8, D), F32),
    tot=((8, 128), F32),
    rtot=((3, 3, 8, 128), F32),
    b4=((8, D), F32),
    rb4=((8, D), F32),
    wuq=((D, D), BF),
    wdq=((D, D), BF),
    rn=((4 * ROWS, D), BF),
    rnt=((D, 4 * ROWS), BF),
    ry=((4 * ROWS, D), BF),
    hxt=((D, 4 * ROWS), BF),
    gx=((4 * ROWS, D), BF),
    rd1=((3, 4, 48, D), BF),
    hd=((4, 48, D), BF),
    rd2=((4, 48, D), BF),
    ru1=((3, 192, D), BF),
    hu=((4, 4, 16, D), BF),
    ru2=((4, 4, 16, D), BF),
    rxa=((D, 4 * ROWS), BF),
    rxb=((4 * ROWS, 384), BF),
    gq=((4, 192, D), BF),
    rq1=((3, 192, D), BF),
    hq=((4, 4, 16, D), BF),
    rq2=((4, 4, 16, D), BF),
    rk1=((2, 3, 192, D), BF),
    hk=((2, 4, 4, 16, D), BF),
    rk2=((2, 16, 16, D), BF),
)
KEYS = {}
for _name, _n in dict(
    tot=9, act=1, back=1, a=4, n=4, y=4, w=3, b=4, a2=4, b2=4,
    d1=4, d2=4, u1=16, u2=16, q1=4, q2=16, k1=32, k2=32, v=9, load=8,
).items():
    KEYS[_name] = sum(KEYS.values()) if not KEYS else _total
    _total = KEYS[_name] + _n
N_SEMS = _total
NAMES = list(BUFS)


def kernel(*refs):
    (gid, clen, flen, lw, tokens, ctx_in, cot_in, g1, b1, g2, b2, bu, wq_in, wkv_in, wo_in, wu_in, wd_in) = refs[:17]
    (acts, ins, og1, ob1, oq, okv, oo, og2, ob2, oup, oub, odn) = refs[17:29]
    b = dict(zip(NAMES, refs[29 : 29 + len(NAMES)]))
    b["do"] = b["n1"]
    b["dn"] = b["x2"]
    b["pad"] = b["x2"].at[pl.ds(0, 208)]
    b["gd"] = b["gp"].at[:, pl.ds(0, 192)]
    b["gu"] = b["hm"].at[:, pl.ds(0, 192)]
    ssem, rsem = refs[29 + len(NAMES) :]

    sec = lax.axis_index("section")
    dp = lax.axis_index("dp")
    at = {"y": dp // 16, "z": (dp // 4) % 4, "x": dp % 4}
    step = {"y": 16, "z": 4, "x": 1}
    other = 1 - sec

    def peer(axis, r):
        p = lax.rem(at[axis] + r, 4)
        return p, dp + (p - at[axis]) * step[axis]

    def peer2(axis, r, axis2, r2):
        p, to = peer(axis, r)
        p2, to2 = peer(axis2, r2)
        return p, p2, to + to2 - dp

    barrier = pltpu.get_barrier_semaphore()
    pl.semaphore_signal(barrier, inc=1, device_id=(other, dp), device_id_type=MESH)
    near = [peer(axis, r)[1] for axis in "xyz" for r in (1, 2, 3)]
    for axis, axis2 in ("yx", "zx", "yz"):
        near += [peer2(axis, r, axis2, r2)[2] for r in (1, 2, 3) for r2 in (1, 2, 3)]
    for to in near:
        for core in (sec, other):
            pl.semaphore_signal(barrier, inc=1, device_id=(core, to), device_id_type=MESH)

    def branch(mine):
        cross = mine == 0
        group = {0: "y", 1: "z"}
        group_qo = "z" if cross else "x"
        pending = []

        def send(key, i, src, dst, device, slot=None, when=None):
            k = KEYS[key] + i
            copy = pltpu.make_async_remote_copy(
                src_ref=src, dst_ref=dst, send_sem=ssem.at[k],
                recv_sem=rsem.at[k if slot is None else KEYS[key] + slot],
                device_id=device, device_id_type=MESH,
            )
            if when is None:
                copy.start()
                pending.append(copy.wait_send)
            else:
                pl.when(when)(copy.start)
                pending.append(lambda: pl.when(when)(copy.wait_send))

        def recv(key, i, ref):
            k = KEYS[key] + i
            pltpu.make_async_remote_copy(
                src_ref=ref, dst_ref=ref, send_sem=ssem.at[k], recv_sem=rsem.at[k],
                device_id=(other, dp), device_id_type=MESH,
            ).wait_recv()

        def local(key, i, src, dst):
            copy = pltpu.make_async_copy(src, dst, rsem.at[KEYS[key] + i])
            copy.start()
            return copy

        loads = {}

        def load(name, i, src, dst):
            loads[name] = local("load", i, src, dst)

        if cross:
            load("x", 0, tokens, b["xb"])
            load("wq", 3, wq_in, b["wq"])
            load("ctx", 1, ctx_in, b["ctx"])
            load("wkv", 2, wkv_in, b["wkv"])
        else:
            load("cot", 0, cot_in, b["do"])
            load("wq", 3, wq_in, b["wq"])
            load("wkv", 2, wkv_in, b["wkv"])
        load("wo", 4, wo_in, b["wo"])
        load("wu", 5, wu_in, b["wu"])
        load("wd", 6, wd_in, b["wd"])

        lane = lax.broadcasted_iota(jnp.int32, (1, 128), 1)
        first_head = lane < 64
        mask_a = first_head.astype(F32).astype(BF)
        mask_b = 1.0 - mask_a

        def stacked(v):
            return jnp.concatenate([v * mask_a, v * mask_b], axis=0)

        def merged(v):
            return jnp.where(first_head, v[:SEQ], v[SEQ:])

        def norm(src, gain, bias, xh, rs, n, nt):
            def body(i):
                rows = tile(i, 32)
                v = src[rows, :].astype(F32)
                centre = v - jnp.mean(v, axis=-1, keepdims=True)
                spread = jnp.mean(centre * centre, axis=-1, keepdims=True)
                scale = lax.rsqrt(spread + 1e-05)
                hat = centre * scale
                xh[rows, :] = hat
                b["rs"][rows, rs : rs + 1] = scale
                n[rows, :] = (hat * gain[...] + bias[...]).astype(BF)

            loop(8, body)
            if nt is not None:
                for j in range(3):
                    nt[j * T : (j + 1) * T, :] = n[:, j * T : (j + 1) * T].T

        def norm_back(xh, rs, gain, row, done):
            def body(i, carry):
                sum_g, sum_b = carry
                rows = tile(i, 32)
                grad = b["dn"][rows, :]
                hat = xh[rows, :]
                sum_g = sum_g + (grad * hat).reshape(4, 8, D).sum(0)
                sum_b = sum_b + grad.reshape(4, 8, D).sum(0)
                scaled = grad * gain[...]
                mean = jnp.mean(scaled, axis=-1, keepdims=True)
                along = jnp.mean(scaled * hat, axis=-1, keepdims=True)
                done(rows, b["dx"][rows, :] + b["rs"][rows, rs : rs + 1] * (scaled - mean - hat * along))
                return sum_g, sum_b

            sums = (jnp.zeros((8, D), F32),) * 2
            for i in range(8):
                sums = body(i, sums)
            sum_g, sum_b = sums
            b["vec"][row : row + 1, :] = sum_g.sum(0, keepdims=True)
            b["vec"][row + 1 : row + 2, :] = sum_b.sum(0, keepdims=True)

        def gather_to(axis, key, src_of, dst_of, core):
            for r in (1, 3, 2):
                p, to = peer(axis, r)
                send(key, r, src_of(p), dst_of(r), (core, to))
            if core is other:
                send(key, 0, src_of(at[axis]), dst_of(0), (core, dp))
                return None
            return local(key, 0, src_of(at[axis]), dst_of(0))

        def gather_some(axis, key, src, dst_of, chosen):
            for r in (1, 3, 2):
                p, to = peer(axis, r)
                send(key, r, src, dst_of(r), (sec, to), when=chosen(p))

        def cols(ref):
            return lambda r: ref.at[:, pl.ds(r * ROWS, ROWS)]

        def rows_of(ref):
            return lambda r: ref.at[pl.ds(r * ROWS, ROWS)]

        def scatter(axis, key, src_of, dst_of, base=0, core=sec):
            for r in (1, 3, 2):
                p, to = peer(axis, r)
                send(key, base + r, src_of(p), dst_of(r - 1), (core, to))

        def scatter48(axis, key, src_of, dst_of, base=0):
            for r in (1, 3, 2):
                p, to = peer(axis, r)
                for i in range(4):
                    send(key, base + 4 * r + i, src_of(p, i), dst_of(r - 1).at[tile(i, 48)], (sec, to))

        def recv48(key, dst_of, base=0):
            for r in (1, 3, 2):
                for i in range(4):
                    recv(key, base + 4 * r + i, dst_of(r - 1).at[tile(i, 48)])

        def recv3(key, dst_of, base=0):
            for r in (1, 3, 2):
                recv(key, base + r, dst_of(r - 1))

        def send_quarter():
            q = at[group[mine]]
            for k in range(4):
                b["b4"][k : k + 1, :] = bu[:, k * D : (k + 1) * D]
            b["b4"][4:8, :] = jnp.zeros((4, D), F32)
            send("w", 0, b["b4"], b["rb4"], (other, dp))
            loads["wu"].wait()
            send("w", 1, b["wu"].at[:, tile(q, D)], b["wuq"], (other, dp))
            loads["wd"].wait()
            send("w", 2, b["wd"].at[tile(q, D), :], b["wdq"], (other, dp))

        if not cross:
            weighted, ids = [], []
            total = jnp.zeros((1, 128), F32)
            for s in range(2):
                w = jnp.where(lane < flen[s], lw[s : s + 1, :].astype(F32), 0.0)
                total = total + jnp.where(lane == gid[s], jnp.sum(w, axis=1, keepdims=True), 0.0)
                weighted.append(w)
            b["tot"][...] = jnp.broadcast_to(total, (8, 128))
        if not cross:
            pl.semaphore_wait(barrier, 1 + 2 * len(near))
            for a, axis in enumerate("xyz"):
                for r in (1, 2, 3):
                    _, to = peer(axis, r)
                    send("tot", 3 * a + r - 1, b["tot"], b["rtot"].at[a, r - 1], (sec, to))
                for r in (1, 2, 3):
                    recv("tot", 3 * a + r - 1, b["rtot"].at[a, r - 1])
                for wait in pending:
                    wait()
                pending.clear()
                b["tot"][...] += b["rtot"][a, 0] + b["rtot"][a, 1] + b["rtot"][a, 2]
            totals = b["tot"][0:1, :]
            every = jnp.sum(totals, axis=1, keepdims=True)
            factors = every / (GROUPS * jnp.maximum(totals, 1.0))
            loads["cot"].wait()
            diagonal = lax.broadcasted_iota(jnp.int32, (SEQ, SEQ), 0) == lax.broadcasted_iota(
                jnp.int32, (SEQ, SEQ), 1
            )
            for s in range(2):
                factor = jnp.sum(jnp.where(lane == gid[s], factors, 0.0), axis=1, keepdims=True)
                picked = jnp.where(diagonal, weighted[s], 0.0).astype(BF)
                rows = slice(s * SEQ, (s + 1) * SEQ)
                grad = mm(picked, b["do"][rows, :]) * factor
                b["dx"][rows, :] = grad
                b["dyb"][rows, :] = grad.astype(BF)
            gather_to(group[1], "y", lambda p: b["dyb"], rows_of(b["ry"]), other)
            send_quarter()

        if cross:
            loads["x"].wait()
        else:
            recv("act", 0, b["xb"])
        norm(b["xb"], g1, b1, b["xh1"], 0, b["n1"], b["s2t"].at[0])

        if not cross:
            own_a2 = gather_to(group_qo, "a2", lambda p: b["s2t"].at[0], cols(b["ctxt"]), sec)
        loads["wq"].wait()

        def query(i):
            b["q"][:, tile(i)] = (mm(b["n1"][...], b["wq"][:, tile(i)]).astype(BF) * 0.125).astype(BF)

        loop(3, query)

        loads["wkv"].wait()
        if cross:
            loads["ctx"].wait()

            def keyval(i):
                for m in range(4):
                    rows = slice(m * T, (m + 1) * T)
                    b["kv"][rows, tile(i)] = mm(b["ctx"][rows, :], b["wkv"][:, tile(i)]).astype(BF)
        else:

            def keyval(i):
                b["kv"][0:ROWS, tile(i)] = mm(b["n1"][...], b["wkv"][:, tile(i)]).astype(BF)

        loop(6, keyval)
        keys = CTX if cross else SEQ
        if cross:
            pl.semaphore_wait(barrier, 1 + 2 * len(near))
            gather_some(group_qo, "a", b["s2t"].at[0], cols(b["rxa"]), lambda p: p < 2)

        def blocks(i):
            s, j = i // PAIRS, i % PAIRS
            vcols = slice(D + 128 * j, D + 128 * (j + 1))
            return s, j, tile(s, SEQ), tile(s, keys), tile(j, 128), vcols

        if cross:
            key = lax.broadcasted_iota(jnp.int32, (1, keys), 1)
            masks = [jnp.where(key < clen[s], 0.0, -1e9) for s in range(2)]
        else:
            row = lax.broadcasted_iota(jnp.int32, (SEQ, keys), 0)
            mask = jnp.where(lax.broadcasted_iota(jnp.int32, (SEQ, keys), 1) <= row, 0.0, -1e9)
            masks = [jnp.concatenate([mask, mask], axis=0)] * 2
        ones = jnp.ones((keys, 128), BF)

        def attend(i):
            s, j, rows, krows, kcols, vcols = blocks(i)
            scores = mm_nt(stacked(b["q"][rows, kcols]), b["kv"][krows, kcols]) + masks[s]
            e = jnp.exp(scores - jnp.max(scores, axis=-1, keepdims=True))
            values = b["kv"][krows, vcols]
            if cross:
                e = e.astype(BF)
                b["p"][i] = e
                mixed = mm(e, jnp.concatenate([values, ones], axis=1))
                scale = 1.0 / merged(mixed[:, 128:])
                b["inv"][rows, kcols] = scale
                b["o"][rows, kcols] = (merged(mixed[:, :128]) * scale).astype(BF)
            else:
                probs = (e / jnp.sum(e, axis=-1, keepdims=True)).astype(BF)
                b["p"][i, :, 0:keys] = probs
                b["o"][rows, kcols] = merged(mm(probs, values)).astype(BF)

        loop(2 * PAIRS, attend)
        for j in range(3):
            b["s2t"][1, j * T : (j + 1) * T, :] = b["o"][:, j * T : (j + 1) * T].T
        gather_some(group_qo, "a", b["s2t"].at[1], cols(b["rxa"]), lambda p: p >= 2)
        own_a = local("a", 0, b["s2t"].at[at[group_qo] // 2], cols(b["rxa"])(0))

        loads["wo"].wait()

        def project(i):
            b["x2"][:, tile(i)] = b["xb"][:, tile(i)].astype(F32) + mm(b["o"][...], b["wo"][:, tile(i)])

        loop(3, project)
        norm(b["x2"], g2, b2, b["xh2"], 1, b["n2"], None)
        gather_to(group[mine], "n", lambda p: b["n2"], rows_of(b["rn"]), other)
        if cross:
            send_quarter()

        def gelu(u):
            square = u * u
            th = jnp.tanh(u * (GELU_C + (GELU_C * GELU_A) * square))
            half = 0.5 + 0.5 * th
            slope = half + (u * (0.5 - 0.5 * th * th)) * (GELU_C + (3.0 * GELU_A * GELU_C) * square)
            return (u * half).astype(BF), slope.astype(BF)

        def up(i):
            u = mm(b["n2"][...], b["wu"][:, tile(i)]) + bu[:, tile(i)]
            k, at_cols = i // 3, tile(i % 3)
            b["hm"][k, :, at_cols], b["gp"][k, :, at_cols] = gelu(u)

        loop(12, up)

        def down(i):
            y = b["x2"][:, tile(i)]
            for k in range(4):
                y = y + mm(b["hm"][k], b["wd"][k * D : (k + 1) * D, tile(i)])
            acts[:, tile(i)] = y.astype(BF)

        loop(3, down)
        if cross:
            send("act", 0, acts, b["xb"], (other, dp))

        def add4(own, parts):
            total = own.astype(F32)
            for part in parts:
                total = total + part.astype(F32)
            return total

        def plane(key, axis, src_of, dst, base=0, core=sec):
            for r in (1, 3, 2, 0):
                for r2 in (1, 3, 2, 0):
                    if r or r2 or core is other:
                        p, p2, to = peer2(axis, r, "x", r2)
                        send(key, base + 4 * r + r2, src_of(p, p2), dst(r, r2), (core, to))

        def recv_plane(key, ref, base=0, first=1):
            for i in range(first, 16):
                recv(key, base + i, ref)

        def cut(dst, cols):
            for k in range(4):
                for j in range(4):
                    start = 48 * k + 12 * j
                    dst[k, j, :, cols] = b["pad"][start : start + 16, cols].astype(BF)

        full = slice(0, D)

        theirs = 1 - mine

        def ffn_forward():
            for i, name in enumerate(("rb4", "wuq", "wdq")):
                recv("w", i, b[name])
            for r in range(4):
                recv("n", r, rows_of(b["rn"])(r))
            bias = b["rb4"][pl.ds(at[group[theirs]], 1), :]
            for m in range(4):
                for i in range(3):
                    u = mm(b["rn"][tile(m), :], b["wuq"][:, tile(i)]) + bias[:, tile(i)]
                    hidden, b["gx"][tile(m), tile(i)] = gelu(u)
                    b["hxt"][tile(i), tile(m)] = hidden.T
                    b["rnt"][tile(i), tile(m)] = b["rn"][tile(m), tile(i)].T

        def down_a():
            for r in range(4):
                recv("y", r, rows_of(b["ry"])(r))
            for i in range(3):
                v = mm(b["hxt"][...], b["ry"][:, tile(i)]).astype(BF)
                b["gd"][:, :, tile(i)] = v.reshape(4, 192, T)
            scatter("x", "d1", lambda p: b["gd"].at[:, rows48(p)], lambda r: b["rd1"].at[r])

        def down_b():
            recv3("d1", lambda r: b["rd1"].at[r])
            for i in range(4):
                b["hd"][i] = add4(b["gd"][i, rows48(at["x"])], [b["rd1"][r, i] for r in range(3)]).astype(BF)
            if theirs == 0:
                for r in (1, 3, 2, 0):
                    p, to = peer("z", r)
                    send("d2", r, b["hd"].at[p], b["rd2"].at[r], (other, to))
            else:
                to = dp + (at["z"] - at["y"]) * step["y"]
                for r in (1, 3, 2, 0):
                    p, there = peer("z", r)
                    send("d2", r, b["hd"].at[p], b["rd2"].at[at["y"]], (other, to + there - dp), at["y"])

        def down_end():
            for r in range(4):
                recv("d2", r, b["rd2"].at[r])
            odn[...] = add4(b["rd2"][0], [b["rd2"][r] for r in (1, 2, 3)])

        def up_axes(layer):
            return ("y", "z") if layer == 1 else ("z", "y")

        def up_a():
            axis = up_axes(theirs)[0]
            for m in range(4):
                for i in range(3):
                    grad = mm_nt(b["ry"][tile(m), :], b["wdq"][tile(i), :])
                    b["gx"][tile(m), tile(i)] = (b["gx"][tile(m), tile(i)].astype(F32) * grad).astype(BF)
            for i in range(3):
                v = mm(b["rnt"][...], b["gx"][:, tile(i)]).astype(BF)
                b["gu"][:, :, tile(i)] = v.reshape(4, 192, T)
            if axis == "y":
                scatter(axis, "u1", lambda p: b["gu"].at[p], lambda r: b["ru1"].at[r])
            else:
                scatter48(axis, "u1", lambda p, i: b["gu"].at[i, rows48(p)], lambda r: b["ru1"].at[r])

        def up_b():
            axis, rest = up_axes(theirs)
            (recv3 if axis == "y" else recv48)("u1", lambda r: b["ru1"].at[r])
            for i in range(4):
                if axis == "y":
                    own, parts = b["gu"][at["y"], tile(i, 48)], [b["ru1"][r, tile(i, 48)] for r in range(3)]
                else:
                    own, parts = b["gu"][i, rows48(at["z"])], [b["ru1"][r, tile(i, 48)] for r in range(3)]
                b["pad"][tile(i, 48), :] = add4(own, parts)
            cut(b["hu"], full)
            plane(
                "u2", rest, lambda p, p2: b["hu"].at[p, p2],
                lambda r, r2: b["ru2"].at[at[rest], r2], core=other,
            )

        def up_end():
            recv_plane("u2", b["ru2"].at[0, 0], first=0)
            for k in range(4):
                total = add4(b["ru2"][k, 0], [b["ru2"][k, r] for r in (1, 2, 3)])
                oup[:, k * D : (k + 1) * D] = total[:12]

        width = 384 if cross else D
        part = slice(0, width)

        def qo_a():
            own_a.wait()
            own_b.wait()
            makes_out = at[group_qo] >= 2

            def recv_a():
                for r in range(1, 4):
                    recv("a", r, cols(b["rxa"])(r))

            if cross:
                recv_a()
            else:
                pl.when(makes_out)(recv_a)
            for r in range(1, 4):
                recv("b", r, rows_of(b["rxb"])(r))
            if not cross:
                own_a2.wait()
                own_b2.wait()
                for r in range(1, 4):
                    recv("a2", r, cols(b["ctxt"])(r))
                    recv("b2", r, b["dkvt"].at[pl.ds(r * ROWS, ROWS), pl.ds(0, 384)])

            def make(from_ref):
                for i in range(2):
                    v = mm(from_ref[tile(i, 384), :], b["rxb"][...]).astype(BF)
                    b["gq"][2 * i : 2 * i + 2, :, 0:384] = v.reshape(2, 192, 384)

            if cross:
                make(b["rxa"])
            else:
                pl.when(makes_out)(lambda: make(b["rxa"]))
                pl.when(jnp.logical_not(makes_out))(lambda: make(b["ctxt"]))
                for i in range(2):
                    v = mm(b["ctxt"][tile(i, 384), :], b["dkvt"][0:1024, 0:384]).astype(BF)
                    b["gq"][2 * i : 2 * i + 2, :, 384:768] = v.reshape(2, 192, 384)
            scatter("y", "q1", lambda p: b["gq"].at[p, :, pl.ds(0, width)], lambda r: b["rq1"].at[r, :, pl.ds(0, width)])

        def qo_b():
            recv3("q1", lambda r: b["rq1"].at[r, :, pl.ds(0, width)])
            for i in range(4):
                rows = tile(i, 48)
                b["pad"][rows, part] = add4(b["gq"][at["y"], rows, part], [b["rq1"][r, rows, part] for r in range(3)])
            cut(b["hq"], part)
            if cross:
                slot = lambda r, r2: b["rq2"].at[at["z"], r2, :, pl.ds(0, width)]
            else:
                slot = lambda r, r2: b["rq2"].at[at["x"], r, :, pl.ds(0, width)]
            plane("q2", "z", lambda p, p2: b["hq"].at[p, p2, :, pl.ds(0, width)], slot)
            b["rq2"][at[group_qo], 0, :, part] = b["hq"][at["z"], at["x"], :, part]

        def qo_end():
            recv_plane("q2", b["rq2"].at[0, 0, :, pl.ds(0, width)])

            def total(k, at_cols):
                return add4(b["rq2"][k, 0, :, at_cols], [b["rq2"][k, r, :, at_cols] for r in (1, 2, 3)])[:12]

            for k in range(2):
                oq[:, 384 * k : 384 * (k + 1)] = total(k, slice(0, 384))
                oo[:, 384 * k : 384 * (k + 1)] = total(2 + k, slice(0, 384))
            if not cross:
                for k in range(4):
                    okv[:, 384 * k : 384 * (k + 1)] = total(k, slice(384, D))

        def kv_a(h):
            for i in range(3):
                v = mm_nt(b["ctxt"][...], b["dkvt"][tile(3 * h + i), :]).astype(BF)
                b["kv"][0:D, tile(3 * h + i)] = v
            if h:
                scatter("y", "k1", lambda p: b["kv"].at[tile(p, 192), D:], lambda r: b["rk1"].at[1, r])
            else:
                scatter48("z", "k1", lambda p, i: b["kv"].at[rows48(4 * i + p), 0:D], lambda r: b["rk1"].at[0, r], 16)

        def kv_b(h):
            if h:
                recv3("k1", lambda r: b["rk1"].at[1, r])
            else:
                recv48("k1", lambda r: b["rk1"].at[0, r], 16)
            for i in range(4):
                m = 4 * at["y"] + i if h else 4 * i + at["z"]
                own = b["kv"][rows48(m), h * D : (h + 1) * D]
                b["pad"][tile(i, 48), :] = add4(own, [b["rk1"][h, r, tile(i, 48)] for r in range(3)])
            cut(b["hk"].at[h], full)
            axis = "z" if h else "y"
            plane(
                "k2", axis, lambda p, p2: b["hk"].at[h, p, p2],
                lambda r, r2: b["rk2"].at[h, 4 * r + r2], 16 * h,
            )
            b["rk2"][h, 0] = b["hk"][h, at[axis], at["x"]]

        def kv_end(h):
            recv_plane("k2", b["rk2"].at[h, 1], 16 * h)
            total = add4(b["rk2"][h, 0], [b["rk2"][h, i] for i in range(1, 16)])
            okv[:, h * D : (h + 1) * D] = total[:12]

        vec_copies = []

        def vec_send(a):
            for r in (1, 2, 3):
                _, to = peer("xyz"[a], r)
                send("v", 3 * a + r - 1, b["vec"], b["rvec"].at[a, r - 1], (sec, to))
                vec_copies.append(pending.pop())

        def vec_add(a):
            for r in (1, 2, 3):
                recv("v", 3 * a + r - 1, b["rvec"].at[a, r - 1])
            for wait in vec_copies:
                wait()
            vec_copies.clear()
            b["vec"][...] += b["rvec"][a, 0] + b["rvec"][a, 1] + b["rvec"][a, 2]

        def vec_out():
            shift = lax.rem(D - 12 * dp, D)
            rolled = pltpu.roll(b["vec"][...], shift, axis=1)
            for row, out in enumerate((og1, ob1, og2, ob2)):
                out[...] = rolled[row : row + 1, 0:12]
            bias_row = b["vec"][pl.ds(4 + at["y"], 1), :]
            shift = lax.rem(D - 48 * lax.rem(dp, 16), D)
            rolled = pltpu.roll(jnp.broadcast_to(bias_row, (8, D)), shift, axis=1)
            oub[...] = rolled[0:1, 0:48]

        if cross:
            for j in range(3):
                for m in range(4):
                    rows, at_cols = slice(m * T, (m + 1) * T), slice(j * T, (j + 1) * T)
                    b["ctxt"][at_cols, rows] = b["ctx"][rows, at_cols].T
        if cross:
            recv("back", 0, b["dyb"])
            b["dx"][...] = b["dyb"][...].astype(F32)
            gather_to(group[0], "y", lambda p: b["dyb"], rows_of(b["ry"]), other)

        for k in range(4):

            def up_back(i):
                grad = mm_nt(b["dyb"][...], b["wd"][tile(3 * k + i), :])
                du = (b["gp"][k, :, tile(i)].astype(F32) * grad).astype(BF)
                b["gp"][k, :, tile(i)] = du
                b["vec"][4 + k : 5 + k, tile(i)] = jnp.sum(du.astype(F32), axis=0, keepdims=True)

            loop(3, up_back)

        def n2_back(i):
            grad = jnp.zeros((ROWS, T), F32)
            for k in range(4):
                grad = grad + mm_nt(b["gp"][k], b["wu"][tile(i), k * D : (k + 1) * D])
            b["dn"][:, tile(i)] = grad

        loop(3, n2_back)

        def done2(rows, value):
            b["dx"][rows, :] = value
            rounded = value.astype(BF)
            b["d4"][2, rows, :] = rounded[:, 0:384]
            b["d4"][3, rows, :] = rounded[:, 384:768]

        norm_back(b["xh2"], 1, g2, 2, done2)

        def out_back(i):
            rows = tile(i)
            grad = mm_nt(b["d4"][2], b["wo"][rows, 0:384]) + mm_nt(b["d4"][3], b["wo"][rows, 384:768])
            b["do"][:, tile(i)] = grad.astype(BF)

        loop(3, out_back)

        def attend_back(i):
            s, j, rows, krows, kcols, vcols = blocks(i)
            k2, v2 = b["kv"][krows, kcols], b["kv"][krows, vcols]
            q2 = stacked(b["q"][rows, kcols])
            probs = b["p"][i, :, 0:keys]
            grad = b["do"][rows, kcols].astype(F32)
            if cross:
                grad = grad * b["inv"][rows, kcols]
            along = grad * b["o"][rows, kcols].astype(F32)
            along = jnp.concatenate([jnp.where(first_head, along, 0.0), jnp.where(first_head, 0.0, along)], axis=0)
            along = jnp.sum(along, axis=-1, keepdims=True)
            do2 = stacked(grad.astype(BF))
            ds = (probs.astype(F32) * (mm_nt(do2, v2) - along)).astype(BF)
            half, at_cols = j // 3, tile(j % 3, 128)
            b["d4"][half, rows, at_cols] = (merged(mm(ds, k2)) * 0.125).astype(BF)
            if cross:
                b["dkvt"][tile(j, 128), krows] = mm_tn(q2, ds).astype(BF)
                b["dkvt"][vcols, krows] = mm_tn(do2, probs).astype(BF)
            else:
                b["ctx"][tile(2 * half + s, SEQ), at_cols] = mm_tn(ds, q2).astype(BF)
                b["ctx"][tile(4 + 2 * half + s, SEQ), at_cols] = mm_tn(probs, do2).astype(BF)

        loop(2 * PAIRS, attend_back)
        own_b = gather_to(group_qo, "b", lambda p: b["d4"].at[p], rows_of(b["rxb"]), sec)
        if not cross:

            def kv_quarter(p):
                return b["ctx"].at[tile(p, ROWS), pl.ds(0, 384)]

            own_b2 = gather_to(
                group_qo, "b2", kv_quarter, lambda r: b["dkvt"].at[pl.ds(r * ROWS, ROWS), pl.ds(0, 384)], sec
            )

        if cross:
            kv_a(1)
            kv_a(0)

        def n1_back(i):
            rows = tile(i)
            grad = mm_nt(b["d4"][0], b["wq"][rows, 0:384]) + mm_nt(b["d4"][1], b["wq"][rows, 384:768])
            if not cross:
                for k in range(4):
                    quarter = b["ctx"][k * ROWS : (k + 1) * ROWS, 0:384]
                    grad = grad + mm_nt(quarter, b["wkv"][rows, 384 * k : 384 * (k + 1)])
            b["dn"][:, tile(i)] = grad

        loop(3, n1_back)

        def done1(rows, value):
            ins[rows, :] = value.astype(BF)

        norm_back(b["xh1"], 0, g1, 0, done1)
        if not cross:
            send("back", 0, ins, b["dyb"], (other, dp))

        vec_send(0)
        if cross:
            ffn_forward()
            down_a()
            up_a()
            qo_a()
            kv_b(1)
            kv_b(0)
            vec_add(0)
            vec_send(1)
            qo_b()
            down_b()
            up_b()
            vec_add(1)
            vec_send(2)
            kv_end(0)
            kv_end(1)
        else:
            ffn_forward()
            down_a()
            up_a()
            qo_a()
            vec_add(0)
            vec_send(1)
            down_b()
            up_b()
            qo_b()
            vec_add(1)
            vec_send(2)
        vec_add(2)
        vec_out()
        qo_end()
        down_end()
        up_end()
        for wait in pending:
            wait()

    pl.when(sec == 0)(lambda: branch(0))
    pl.when(sec == 1)(lambda: branch(1))


def deliver(*refs):
    for a, out in zip(refs[:12], refs[12:]):
        out[...] = a[...].reshape(out.shape)


def on_device(
    tokens, context, out_cot, group_id, ctx_len, fut_len, loss_weight,
    norm_gain1, norm_bias1, w_query, w_keyval, w_out,
    norm_gain2, norm_bias2, w_up, up_bias, w_down,
):
    smem = pl.BlockSpec(memory_space=pltpu.SMEM)
    vmem = pl.BlockSpec(memory_space=pltpu.VMEM)
    hbm = pl.BlockSpec(memory_space=pl.ANY)
    shape = jax.ShapeDtypeStruct
    outs = pl.pallas_call(
        kernel,
        out_shape=(
            shape((ROWS, D), BF),
            shape((ROWS, D), BF),
            shape((1, 12), F32),
            shape((1, 12), F32),
            shape((12, D), F32),
            shape((12, 2 * D), F32),
            shape((12, D), F32),
            shape((1, 12), F32),
            shape((1, 12), F32),
            shape((12, FF), F32),
            shape((1, 48), F32),
            shape((48, D), F32),
        ),
        in_specs=[smem] * 3 + [vmem] + [hbm] * 3 + [vmem] * 5 + [hbm] * 5,
        out_specs=[vmem] * 12,
        scratch_shapes=[pltpu.VMEM(s, t) for s, t in BUFS.values()]
        + [pltpu.SemaphoreType.DMA((N_SEMS,)), pltpu.SemaphoreType.DMA((N_SEMS,))],
        compiler_params=pltpu.CompilerParams(
            collective_id=0, has_side_effects=True, vmem_limit_bytes=64 * 1024 * 1024 - 4096
        ),
    )(
        group_id, ctx_len, fut_len, loss_weight,
        tokens.reshape(ROWS, D), context.reshape(2 * CTX, D), out_cot.reshape(ROWS, D),
        norm_gain1, norm_bias1, norm_gain2, norm_bias2, up_bias,
        w_query[0], w_keyval[0], w_out[0], w_up[0], w_down[0],
    )
    outs = pl.pallas_call(
        deliver,
        out_shape=[
            shape((a.shape[0], 1, a.shape[1]) if a.shape[0] == 12 else a.shape, a.dtype) for a in outs
        ],
        in_specs=[vmem] * 12,
        out_specs=[vmem] * 12,
    )(*outs)
    acts, ins, gg1, gb1, gq, gkv, go, gg2, gb2, gup, gub, gdn = outs
    seqs = (1, 2, SEQ, D)
    rows = [g.reshape(1, 12, g.shape[-1]) for g in (gq, gkv, go, gup)]
    return (
        acts.reshape(seqs), ins.reshape(seqs), gg1, gb1, *rows[:3],
        gg2, gb2, rows[3], gub, gdn[None],
    )


def solution(mesh):
    dp, sec = "dp", "section"
    vec, mat = P(sec, None), P(sec, None, None)
    return jax.shard_map(
        on_device,
        mesh=mesh,
        in_specs=(P(dp, None, None),) * 3 + (P(dp),) * 3 + (P(dp, None),)
        + (vec, vec, mat, mat, mat, vec, vec, mat, vec, mat),
        out_specs=(P(sec, dp, None, None),) * 2 + (P(sec, dp),) * 2 + (P(sec, dp, None),) * 3
        + (P(sec, dp),) * 2 + (P(sec, dp, None), P(sec, dp), P(sec, dp, None)),
        check_vma=False,
    )
```

```python
import math

import jax
import jax.numpy as jnp
from jax import lax
from jax.experimental import pallas as pl
from jax.experimental.pallas import tpu as pltpu
from jax.sharding import PartitionSpec as P

MESH = pl.DeviceIdType.MESH
BF = jnp.bfloat16
F32 = jnp.float32
GROUPS = 8
D = 768
FF = 3072
SEQ = 128
ROWS = 256
CTX = 512
PAIRS = 6
T = 256
GELU_C = math.sqrt(2.0 / math.pi)
GELU_A = 0.044715


def mm(a, b):
    return jnp.dot(a, b, preferred_element_type=F32)


def mm_nt(a, b):
    return lax.dot_general(a, b, (((1,), (1,)), ((), ())), preferred_element_type=F32)


def mm_tn(a, b):
    return lax.dot_general(a, b, (((0,), (0,)), ((), ())), preferred_element_type=F32)


def loop(n, body):
    for i in range(n):
        body(i)


def rows48(i):
    return pl.ds(pl.multiple_of(i * 48, 16), 48)


def tile(i, size=T):
    if isinstance(i, int):
        return slice(i * size, (i + 1) * size)
    return pl.ds(pl.multiple_of(i * size, size), size)


BUFS = dict(
    wq=((D, D), BF),
    wkv=((D, 2 * D), BF),
    wo=((D, D), BF),
    wu=((D, FF), BF),
    wd=((FF, D), BF),
    xb=((ROWS, D), BF),
    ctx=((2 * CTX, D), BF),
    ctxt=((D, 2 * CTX), BF),
    n1=((ROWS, D), BF),
    q=((ROWS, D), BF),
    kv=((2 * CTX, 2 * D), BF),
    p=((2 * PAIRS, ROWS, CTX), BF),
    inv=((ROWS, D), F32),
    o=((ROWS, D), BF),
    s2t=((2, D, ROWS), BF),
    n2=((ROWS, D), BF),
    x2=((ROWS, D), F32),
    xh1=((ROWS, D), F32),
    xh2=((ROWS, D), F32),
    rs=((ROWS, 2), F32),
    gp=((4, ROWS, D), BF),
    hm=((4, ROWS, D), BF),
    dyb=((ROWS, D), BF),
    dx=((ROWS, D), F32),
    d4=((4, ROWS, 384), BF),
    dkvt=((2 * D, 2 * CTX), BF),
    vec=((8, D), F32),
    rvec=((3, 3, 8, D), F32),
    tot=((8, 128), F32),
    rtot=((3, 3, 8, 128), F32),
    b4=((8, D), F32),
    rb4=((8, D), F32),
    wuq=((D, D), BF),
    wdq=((D, D), BF),
    rn=((4 * ROWS, D), BF),
    rnt=((D, 4 * ROWS), BF),
    ry=((4 * ROWS, D), BF),
    hxt=((D, 4 * ROWS), BF),
    gx=((4 * ROWS, D), BF),
    rd1=((3, 4, 48, D), BF),
    hd=((4, 48, D), BF),
    rd2=((4, 48, D), BF),
    ru1=((3, 192, D), BF),
    hu=((4, 4, 16, D), BF),
    ru2=((4, 4, 16, D), BF),
    rxa=((D, 4 * ROWS), BF),
    rxb=((4 * ROWS, 384), BF),
    gq=((4, 192, D), BF),
    rq1=((3, 192, D), BF),
    hq=((4, 4, 16, D), BF),
    rq2=((4, 4, 16, D), BF),
    rk1=((2, 3, 192, D), BF),
    hk=((2, 4, 4, 16, D), BF),
    rk2=((2, 16, 16, D), BF),
)
KEYS = {}
for _name, _n in dict(
    tot=9, act=1, back=1, a=4, n=4, y=4, w=3, b=4, a2=4, b2=4,
    d1=4, d2=4, u1=16, u2=16, q1=4, q2=16, k1=32, k2=32, v=9, load=8,
).items():
    KEYS[_name] = sum(KEYS.values()) if not KEYS else _total
    _total = KEYS[_name] + _n
N_SEMS = _total
NAMES = list(BUFS)


def kernel(*refs):
    (gid, clen, flen, lw, tokens, ctx_in, cot_in, g1, b1, g2, b2, bu, wq_in, wkv_in, wo_in, wu_in, wd_in) = refs[:17]
    (acts, ins, og1, ob1, oq, okv, oo, og2, ob2, oup, oub, odn) = refs[17:29]
    b = dict(zip(NAMES, refs[29 : 29 + len(NAMES)]))
    b["do"] = b["n1"]
    b["dn"] = b["x2"]
    b["pad"] = b["x2"].at[pl.ds(0, 208)]
    b["gd"] = b["gp"].at[:, pl.ds(0, 192)]
    b["gu"] = b["hm"].at[:, pl.ds(0, 192)]
    ssem, rsem = refs[29 + len(NAMES) :]

    sec = lax.axis_index("section")
    dp = lax.axis_index("dp")
    at = {"y": dp // 16, "z": (dp // 4) % 4, "x": dp % 4}
    step = {"y": 16, "z": 4, "x": 1}
    other = 1 - sec

    def peer(axis, r):
        p = lax.rem(at[axis] + r, 4)
        return p, dp + (p - at[axis]) * step[axis]

    def peer2(axis, r, axis2, r2):
        p, to = peer(axis, r)
        p2, to2 = peer(axis2, r2)
        return p, p2, to + to2 - dp

    barrier = pltpu.get_barrier_semaphore()
    pl.semaphore_signal(barrier, inc=1, device_id=(other, dp), device_id_type=MESH)
    near = [peer(axis, r)[1] for axis in "xyz" for r in (1, 2, 3)]
    for axis, axis2 in ("yx", "zx", "yz"):
        near += [peer2(axis, r, axis2, r2)[2] for r in (1, 2, 3) for r2 in (1, 2, 3)]
    for to in near:
        for core in (sec, other):
            pl.semaphore_signal(barrier, inc=1, device_id=(core, to), device_id_type=MESH)

    def branch(mine):
        cross = mine == 0
        group = {0: "y", 1: "z"}
        group_qo = "z" if cross else "x"
        pending = []

        def send(key, i, src, dst, device, slot=None):
            k = KEYS[key] + i
            copy = pltpu.make_async_remote_copy(
                src_ref=src, dst_ref=dst, send_sem=ssem.at[k],
                recv_sem=rsem.at[k if slot is None else KEYS[key] + slot],
                device_id=device, device_id_type=MESH,
            )
            copy.start()
            pending.append(copy)

        def recv(key, i, ref):
            k = KEYS[key] + i
            pltpu.make_async_remote_copy(
                src_ref=ref, dst_ref=ref, send_sem=ssem.at[k], recv_sem=rsem.at[k],
                device_id=(other, dp), device_id_type=MESH,
            ).wait_recv()

        def local(key, i, src, dst):
            copy = pltpu.make_async_copy(src, dst, rsem.at[KEYS[key] + i])
            copy.start()
            return copy

        loads = {}

        def load(name, i, src, dst):
            loads[name] = local("load", i, src, dst)

        if cross:
            load("x", 0, tokens, b["xb"])
            load("wq", 3, wq_in, b["wq"])
            load("ctx", 1, ctx_in, b["ctx"])
            load("wkv", 2, wkv_in, b["wkv"])
        else:
            load("cot", 0, cot_in, b["do"])
            load("wq", 3, wq_in, b["wq"])
            load("wkv", 2, wkv_in, b["wkv"])
        load("wo", 4, wo_in, b["wo"])
        load("wu", 5, wu_in, b["wu"])
        load("wd", 6, wd_in, b["wd"])

        lane = lax.broadcasted_iota(jnp.int32, (1, 128), 1)
        first_head = lane < 64
        mask_a = first_head.astype(F32).astype(BF)
        mask_b = 1.0 - mask_a

        def stacked(v):
            return jnp.concatenate([v * mask_a, v * mask_b], axis=0)

        def merged(v):
            return jnp.where(first_head, v[:SEQ], v[SEQ:])

        def norm(src, gain, bias, xh, rs, n, nt):
            def body(i):
                rows = tile(i, 32)
                v = src[rows, :].astype(F32)
                centre = v - jnp.mean(v, axis=-1, keepdims=True)
                spread = jnp.mean(centre * centre, axis=-1, keepdims=True)
                scale = lax.rsqrt(spread + 1e-05)
                hat = centre * scale
                xh[rows, :] = hat
                b["rs"][rows, rs : rs + 1] = scale
                n[rows, :] = (hat * gain[...] + bias[...]).astype(BF)

            loop(8, body)
            if nt is not None:
                for j in range(3):
                    nt[j * T : (j + 1) * T, :] = n[:, j * T : (j + 1) * T].T

        def norm_back(xh, rs, gain, row, done):
            def body(i, carry):
                sum_g, sum_b = carry
                rows = tile(i, 32)
                grad = b["dn"][rows, :]
                hat = xh[rows, :]
                sum_g = sum_g + (grad * hat).reshape(4, 8, D).sum(0)
                sum_b = sum_b + grad.reshape(4, 8, D).sum(0)
                scaled = grad * gain[...]
                mean = jnp.mean(scaled, axis=-1, keepdims=True)
                along = jnp.mean(scaled * hat, axis=-1, keepdims=True)
                done(rows, b["dx"][rows, :] + b["rs"][rows, rs : rs + 1] * (scaled - mean - hat * along))
                return sum_g, sum_b

            sums = (jnp.zeros((8, D), F32),) * 2
            for i in range(8):
                sums = body(i, sums)
            sum_g, sum_b = sums
            b["vec"][row : row + 1, :] = sum_g.sum(0, keepdims=True)
            b["vec"][row + 1 : row + 2, :] = sum_b.sum(0, keepdims=True)

        def gather_to(axis, key, src_of, dst_of, core):
            for r in (1, 3, 2):
                p, to = peer(axis, r)
                send(key, r, src_of(p), dst_of(r), (core, to))
            if core is other:
                send(key, 0, src_of(at[axis]), dst_of(0), (core, dp))
                return None
            return local(key, 0, src_of(at[axis]), dst_of(0))

        def cols(ref):
            return lambda r: ref.at[:, pl.ds(r * ROWS, ROWS)]

        def rows_of(ref):
            return lambda r: ref.at[pl.ds(r * ROWS, ROWS)]

        def scatter(axis, key, src_of, dst_of, base=0, core=sec):
            for r in (1, 3, 2):
                p, to = peer(axis, r)
                send(key, base + r, src_of(p), dst_of(r - 1), (core, to))

        def scatter48(axis, key, src_of, dst_of, base=0):
            for r in (1, 3, 2):
                p, to = peer(axis, r)
                for i in range(4):
                    send(key, base + 4 * r + i, src_of(p, i), dst_of(r - 1).at[tile(i, 48)], (sec, to))

        def recv48(key, dst_of, base=0):
            for r in (1, 3, 2):
                for i in range(4):
                    recv(key, base + 4 * r + i, dst_of(r - 1).at[tile(i, 48)])

        def recv3(key, dst_of, base=0):
            for r in (1, 3, 2):
                recv(key, base + r, dst_of(r - 1))

        def send_quarter():
            q = at[group[mine]]
            for k in range(4):
                b["b4"][k : k + 1, :] = bu[:, k * D : (k + 1) * D]
            b["b4"][4:8, :] = jnp.zeros((4, D), F32)
            send("w", 0, b["b4"], b["rb4"], (other, dp))
            loads["wu"].wait()
            send("w", 1, b["wu"].at[:, tile(q, D)], b["wuq"], (other, dp))
            loads["wd"].wait()
            send("w", 2, b["wd"].at[tile(q, D), :], b["wdq"], (other, dp))

        if not cross:
            weighted, ids = [], []
            total = jnp.zeros((1, 128), F32)
            for s in range(2):
                w = jnp.where(lane < flen[s], lw[s : s + 1, :].astype(F32), 0.0)
                total = total + jnp.where(lane == gid[s], jnp.sum(w, axis=1, keepdims=True), 0.0)
                weighted.append(w)
            b["tot"][...] = jnp.broadcast_to(total, (8, 128))
        pl.semaphore_wait(barrier, 1 + 2 * len(near))
        if not cross:
            for a, axis in enumerate("xyz"):
                for r in (1, 2, 3):
                    _, to = peer(axis, r)
                    send("tot", 3 * a + r - 1, b["tot"], b["rtot"].at[a, r - 1], (sec, to))
                for r in (1, 2, 3):
                    recv("tot", 3 * a + r - 1, b["rtot"].at[a, r - 1])
                for copy in pending:
                    copy.wait_send()
                pending.clear()
                b["tot"][...] += b["rtot"][a, 0] + b["rtot"][a, 1] + b["rtot"][a, 2]
            totals = b["tot"][0:1, :]
            every = jnp.sum(totals, axis=1, keepdims=True)
            factors = every / (GROUPS * jnp.maximum(totals, 1.0))
            loads["cot"].wait()
            diagonal = lax.broadcasted_iota(jnp.int32, (SEQ, SEQ), 0) == lax.broadcasted_iota(
                jnp.int32, (SEQ, SEQ), 1
            )
            for s in range(2):
                factor = jnp.sum(jnp.where(lane == gid[s], factors, 0.0), axis=1, keepdims=True)
                picked = jnp.where(diagonal, weighted[s], 0.0).astype(BF)
                rows = slice(s * SEQ, (s + 1) * SEQ)
                grad = mm(picked, b["do"][rows, :]) * factor
                b["dx"][rows, :] = grad
                b["dyb"][rows, :] = grad.astype(BF)
            gather_to(group[1], "y", lambda p: b["dyb"], rows_of(b["ry"]), other)
            send_quarter()

        if cross:
            loads["x"].wait()
        else:
            recv("act", 0, b["xb"])
        norm(b["xb"], g1, b1, b["xh1"], 0, b["n1"], b["s2t"].at[0])

        loads["wq"].wait()

        def query(i):
            b["q"][:, tile(i)] = (mm(b["n1"][...], b["wq"][:, tile(i)]).astype(BF) * 0.125).astype(BF)

        loop(3, query)

        loads["wkv"].wait()
        if cross:
            loads["ctx"].wait()

            def keyval(i):
                for m in range(4):
                    rows = slice(m * T, (m + 1) * T)
                    b["kv"][rows, tile(i)] = mm(b["ctx"][rows, :], b["wkv"][:, tile(i)]).astype(BF)
        else:

            def keyval(i):
                b["kv"][0:ROWS, tile(i)] = mm(b["n1"][...], b["wkv"][:, tile(i)]).astype(BF)

        loop(6, keyval)
        keys = CTX if cross else SEQ

        def blocks(i):
            s, j = i // PAIRS, i % PAIRS
            vcols = slice(D + 128 * j, D + 128 * (j + 1))
            return s, j, tile(s, SEQ), tile(s, keys), tile(j, 128), vcols

        if cross:
            key = lax.broadcasted_iota(jnp.int32, (1, keys), 1)
            masks = [jnp.where(key < clen[s], 0.0, -1e9) for s in range(2)]
        else:
            row = lax.broadcasted_iota(jnp.int32, (SEQ, keys), 0)
            mask = jnp.where(lax.broadcasted_iota(jnp.int32, (SEQ, keys), 1) <= row, 0.0, -1e9)
            masks = [jnp.concatenate([mask, mask], axis=0)] * 2
        ones = jnp.ones((keys, 128), BF)

        def attend(i):
            s, j, rows, krows, kcols, vcols = blocks(i)
            scores = mm_nt(stacked(b["q"][rows, kcols]), b["kv"][krows, kcols]) + masks[s]
            e = jnp.exp(scores - jnp.max(scores, axis=-1, keepdims=True))
            values = b["kv"][krows, vcols]
            if cross:
                e = e.astype(BF)
                b["p"][i] = e
                mixed = mm(e, jnp.concatenate([values, ones], axis=1))
                scale = 1.0 / merged(mixed[:, 128:])
                b["inv"][rows, kcols] = scale
                b["o"][rows, kcols] = (merged(mixed[:, :128]) * scale).astype(BF)
            else:
                probs = (e / jnp.sum(e, axis=-1, keepdims=True)).astype(BF)
                b["p"][i, :, 0:keys] = probs
                b["o"][rows, kcols] = merged(mm(probs, values)).astype(BF)

        loop(2 * PAIRS, attend)
        for j in range(3):
            b["s2t"][1, j * T : (j + 1) * T, :] = b["o"][:, j * T : (j + 1) * T].T
        own_a = gather_to(group_qo, "a", lambda p: b["s2t"].at[p // 2], cols(b["rxa"]), sec)
        if not cross:
            own_a2 = gather_to(group_qo, "a2", lambda p: b["s2t"].at[0], cols(b["ctxt"]), sec)

        loads["wo"].wait()

        def project(i):
            b["x2"][:, tile(i)] = b["xb"][:, tile(i)].astype(F32) + mm(b["o"][...], b["wo"][:, tile(i)])

        loop(3, project)
        norm(b["x2"], g2, b2, b["xh2"], 1, b["n2"], None)
        gather_to(group[mine], "n", lambda p: b["n2"], rows_of(b["rn"]), other)
        if cross:
            send_quarter()

        def gelu(u):
            square = u * u
            th = jnp.tanh(u * (GELU_C + (GELU_C * GELU_A) * square))
            half = 0.5 + 0.5 * th
            slope = half + (u * (0.5 - 0.5 * th * th)) * (GELU_C + (3.0 * GELU_A * GELU_C) * square)
            return (u * half).astype(BF), slope.astype(BF)

        def up(i):
            u = mm(b["n2"][...], b["wu"][:, tile(i)]) + bu[:, tile(i)]
            k, at_cols = i // 3, tile(i % 3)
            b["hm"][k, :, at_cols], b["gp"][k, :, at_cols] = gelu(u)

        loop(12, up)

        def down(i):
            y = b["x2"][:, tile(i)]
            for k in range(4):
                y = y + mm(b["hm"][k], b["wd"][k * D : (k + 1) * D, tile(i)])
            acts[:, tile(i)] = y.astype(BF)

        loop(3, down)
        if cross:
            send("act", 0, acts, b["xb"], (other, dp))

        def add4(own, parts):
            total = own.astype(F32)
            for part in parts:
                total = total + part.astype(F32)
            return total

        def plane(key, axis, src_of, dst, base=0, core=sec):
            for r in (1, 3, 2, 0):
                for r2 in (1, 3, 2, 0):
                    if r or r2 or core is other:
                        p, p2, to = peer2(axis, r, "x", r2)
                        send(key, base + 4 * r + r2, src_of(p, p2), dst(r, r2), (core, to))

        def recv_plane(key, ref, base=0, first=1):
            for i in range(first, 16):
                recv(key, base + i, ref)

        def cut(dst, cols):
            for k in range(4):
                for j in range(4):
                    start = 48 * k + 12 * j
                    dst[k, j, :, cols] = b["pad"][start : start + 16, cols].astype(BF)

        full = slice(0, D)

        theirs = 1 - mine

        def ffn_forward():
            for i, name in enumerate(("rb4", "wuq", "wdq")):
                recv("w", i, b[name])
            for r in range(4):
                recv("n", r, rows_of(b["rn"])(r))
            bias = b["rb4"][pl.ds(at[group[theirs]], 1), :]
            for m in range(4):
                for i in range(3):
                    u = mm(b["rn"][tile(m), :], b["wuq"][:, tile(i)]) + bias[:, tile(i)]
                    hidden, b["gx"][tile(m), tile(i)] = gelu(u)
                    b["hxt"][tile(i), tile(m)] = hidden.T
                    b["rnt"][tile(i), tile(m)] = b["rn"][tile(m), tile(i)].T

        def down_a():
            for r in range(4):
                recv("y", r, rows_of(b["ry"])(r))
            for i in range(3):
                v = mm(b["hxt"][...], b["ry"][:, tile(i)]).astype(BF)
                b["gd"][:, :, tile(i)] = v.reshape(4, 192, T)
            scatter("x", "d1", lambda p: b["gd"].at[:, rows48(p)], lambda r: b["rd1"].at[r])

        def down_b():
            recv3("d1", lambda r: b["rd1"].at[r])
            for i in range(4):
                b["hd"][i] = add4(b["gd"][i, rows48(at["x"])], [b["rd1"][r, i] for r in range(3)]).astype(BF)
            if theirs == 0:
                for r in (1, 3, 2, 0):
                    p, to = peer("z", r)
                    send("d2", r, b["hd"].at[p], b["rd2"].at[r], (other, to))
            else:
                to = dp + (at["z"] - at["y"]) * step["y"]
                for r in (1, 3, 2, 0):
                    p, there = peer("z", r)
                    send("d2", r, b["hd"].at[p], b["rd2"].at[at["y"]], (other, to + there - dp), at["y"])

        def down_end():
            for r in range(4):
                recv("d2", r, b["rd2"].at[r])
            odn[...] = add4(b["rd2"][0], [b["rd2"][r] for r in (1, 2, 3)])

        def up_axes(layer):
            return ("y", "z") if layer == 1 else ("z", "y")

        def up_a():
            axis = up_axes(theirs)[0]
            for m in range(4):
                for i in range(3):
                    grad = mm_nt(b["ry"][tile(m), :], b["wdq"][tile(i), :])
                    b["gx"][tile(m), tile(i)] = (b["gx"][tile(m), tile(i)].astype(F32) * grad).astype(BF)
            for i in range(3):
                v = mm(b["rnt"][...], b["gx"][:, tile(i)]).astype(BF)
                b["gu"][:, :, tile(i)] = v.reshape(4, 192, T)
            if axis == "y":
                scatter(axis, "u1", lambda p: b["gu"].at[p], lambda r: b["ru1"].at[r])
            else:
                scatter48(axis, "u1", lambda p, i: b["gu"].at[i, rows48(p)], lambda r: b["ru1"].at[r])

        def up_b():
            axis, rest = up_axes(theirs)
            (recv3 if axis == "y" else recv48)("u1", lambda r: b["ru1"].at[r])
            for i in range(4):
                if axis == "y":
                    own, parts = b["gu"][at["y"], tile(i, 48)], [b["ru1"][r, tile(i, 48)] for r in range(3)]
                else:
                    own, parts = b["gu"][i, rows48(at["z"])], [b["ru1"][r, tile(i, 48)] for r in range(3)]
                b["pad"][tile(i, 48), :] = add4(own, parts)
            cut(b["hu"], full)
            plane(
                "u2", rest, lambda p, p2: b["hu"].at[p, p2],
                lambda r, r2: b["ru2"].at[at[rest], r2], core=other,
            )

        def up_end():
            recv_plane("u2", b["ru2"].at[0, 0], first=0)
            for k in range(4):
                total = add4(b["ru2"][k, 0], [b["ru2"][k, r] for r in (1, 2, 3)])
                oup[:, k * D : (k + 1) * D] = total[:12]

        width = 384 if cross else D
        part = slice(0, width)

        def qo_a():
            own_a.wait()
            own_b.wait()
            for r in range(1, 4):
                recv("a", r, cols(b["rxa"])(r))
                recv("b", r, rows_of(b["rxb"])(r))
            if not cross:
                own_a2.wait()
                own_b2.wait()
                for r in range(1, 4):
                    recv("a2", r, cols(b["ctxt"])(r))
                    recv("b2", r, b["dkvt"].at[pl.ds(r * ROWS, ROWS), pl.ds(0, 384)])
            for i in range(2):
                rows = tile(i, 384)
                v = mm(b["rxa"][rows, :], b["rxb"][...]).astype(BF)
                b["gq"][2 * i : 2 * i + 2, :, 0:384] = v.reshape(2, 192, 384)
                if not cross:
                    v = mm(b["ctxt"][rows, :], b["dkvt"][0:1024, 0:384]).astype(BF)
                    b["gq"][2 * i : 2 * i + 2, :, 384:768] = v.reshape(2, 192, 384)
            scatter("y", "q1", lambda p: b["gq"].at[p, :, pl.ds(0, width)], lambda r: b["rq1"].at[r, :, pl.ds(0, width)])

        def qo_b():
            recv3("q1", lambda r: b["rq1"].at[r, :, pl.ds(0, width)])
            for i in range(4):
                rows = tile(i, 48)
                b["pad"][rows, part] = add4(b["gq"][at["y"], rows, part], [b["rq1"][r, rows, part] for r in range(3)])
            cut(b["hq"], part)
            if cross:
                slot = lambda r, r2: b["rq2"].at[at["z"], r2, :, pl.ds(0, width)]
            else:
                slot = lambda r, r2: b["rq2"].at[at["x"], r, :, pl.ds(0, width)]
            plane("q2", "z", lambda p, p2: b["hq"].at[p, p2, :, pl.ds(0, width)], slot)
            b["rq2"][at[group_qo], 0, :, part] = b["hq"][at["z"], at["x"], :, part]

        def qo_end():
            recv_plane("q2", b["rq2"].at[0, 0, :, pl.ds(0, width)])

            def total(k, at_cols):
                return add4(b["rq2"][k, 0, :, at_cols], [b["rq2"][k, r, :, at_cols] for r in (1, 2, 3)])[:12]

            for k in range(2):
                oq[:, 384 * k : 384 * (k + 1)] = total(k, slice(0, 384))
                oo[:, 384 * k : 384 * (k + 1)] = total(2 + k, slice(0, 384))
            if not cross:
                for k in range(4):
                    okv[:, 384 * k : 384 * (k + 1)] = total(k, slice(384, D))

        def kv_a(h):
            for i in range(3):
                v = mm_nt(b["ctxt"][...], b["dkvt"][tile(3 * h + i), :]).astype(BF)
                b["kv"][0:D, tile(3 * h + i)] = v
            if h:
                scatter("y", "k1", lambda p: b["kv"].at[tile(p, 192), D:], lambda r: b["rk1"].at[1, r])
            else:
                scatter48("z", "k1", lambda p, i: b["kv"].at[rows48(4 * i + p), 0:D], lambda r: b["rk1"].at[0, r], 16)

        def kv_b(h):
            if h:
                recv3("k1", lambda r: b["rk1"].at[1, r])
            else:
                recv48("k1", lambda r: b["rk1"].at[0, r], 16)
            for i in range(4):
                m = 4 * at["y"] + i if h else 4 * i + at["z"]
                own = b["kv"][rows48(m), h * D : (h + 1) * D]
                b["pad"][tile(i, 48), :] = add4(own, [b["rk1"][h, r, tile(i, 48)] for r in range(3)])
            cut(b["hk"].at[h], full)
            axis = "z" if h else "y"
            plane(
                "k2", axis, lambda p, p2: b["hk"].at[h, p, p2],
                lambda r, r2: b["rk2"].at[h, 4 * r + r2], 16 * h,
            )
            b["rk2"][h, 0] = b["hk"][h, at[axis], at["x"]]

        def kv_end(h):
            recv_plane("k2", b["rk2"].at[h, 1], 16 * h)
            total = add4(b["rk2"][h, 0], [b["rk2"][h, i] for i in range(1, 16)])
            okv[:, h * D : (h + 1) * D] = total[:12]

        vec_copies = []

        def vec_send(a):
            for r in (1, 2, 3):
                _, to = peer("xyz"[a], r)
                send("v", 3 * a + r - 1, b["vec"], b["rvec"].at[a, r - 1], (sec, to))
                vec_copies.append(pending.pop())

        def vec_add(a):
            for r in (1, 2, 3):
                recv("v", 3 * a + r - 1, b["rvec"].at[a, r - 1])
            for copy in vec_copies:
                copy.wait_send()
            vec_copies.clear()
            b["vec"][...] += b["rvec"][a, 0] + b["rvec"][a, 1] + b["rvec"][a, 2]

        def vec_out():
            shift = lax.rem(D - 12 * dp, D)
            rolled = pltpu.roll(b["vec"][...], shift, axis=1)
            for row, out in enumerate((og1, ob1, og2, ob2)):
                out[...] = rolled[row : row + 1, 0:12]
            bias_row = b["vec"][pl.ds(4 + at["y"], 1), :]
            shift = lax.rem(D - 48 * lax.rem(dp, 16), D)
            rolled = pltpu.roll(jnp.broadcast_to(bias_row, (8, D)), shift, axis=1)
            oub[...] = rolled[0:1, 0:48]

        if cross:
            for j in range(3):
                for m in range(4):
                    rows, at_cols = slice(m * T, (m + 1) * T), slice(j * T, (j + 1) * T)
                    b["ctxt"][at_cols, rows] = b["ctx"][rows, at_cols].T
        if cross:
            recv("back", 0, b["dyb"])
            b["dx"][...] = b["dyb"][...].astype(F32)
            gather_to(group[0], "y", lambda p: b["dyb"], rows_of(b["ry"]), other)

        for k in range(4):

            def up_back(i):
                grad = mm_nt(b["dyb"][...], b["wd"][tile(3 * k + i), :])
                du = (b["gp"][k, :, tile(i)].astype(F32) * grad).astype(BF)
                b["gp"][k, :, tile(i)] = du
                b["vec"][4 + k : 5 + k, tile(i)] = jnp.sum(du.astype(F32), axis=0, keepdims=True)

            loop(3, up_back)

        def n2_back(i):
            grad = jnp.zeros((ROWS, T), F32)
            for k in range(4):
                grad = grad + mm_nt(b["gp"][k], b["wu"][tile(i), k * D : (k + 1) * D])
            b["dn"][:, tile(i)] = grad

        loop(3, n2_back)

        def done2(rows, value):
            b["dx"][rows, :] = value
            rounded = value.astype(BF)
            b["d4"][2, rows, :] = rounded[:, 0:384]
            b["d4"][3, rows, :] = rounded[:, 384:768]

        norm_back(b["xh2"], 1, g2, 2, done2)

        def out_back(i):
            rows = tile(i)
            grad = mm_nt(b["d4"][2], b["wo"][rows, 0:384]) + mm_nt(b["d4"][3], b["wo"][rows, 384:768])
            b["do"][:, tile(i)] = grad.astype(BF)

        loop(3, out_back)

        def attend_back(i):
            s, j, rows, krows, kcols, vcols = blocks(i)
            k2, v2 = b["kv"][krows, kcols], b["kv"][krows, vcols]
            q2 = stacked(b["q"][rows, kcols])
            probs = b["p"][i, :, 0:keys]
            grad = b["do"][rows, kcols].astype(F32)
            if cross:
                grad = grad * b["inv"][rows, kcols]
            along = grad * b["o"][rows, kcols].astype(F32)
            along = jnp.concatenate([jnp.where(first_head, along, 0.0), jnp.where(first_head, 0.0, along)], axis=0)
            along = jnp.sum(along, axis=-1, keepdims=True)
            do2 = stacked(grad.astype(BF))
            ds = (probs.astype(F32) * (mm_nt(do2, v2) - along)).astype(BF)
            half, at_cols = j // 3, tile(j % 3, 128)
            b["d4"][half, rows, at_cols] = (merged(mm(ds, k2)) * 0.125).astype(BF)
            if cross:
                b["dkvt"][tile(j, 128), krows] = mm_tn(q2, ds).astype(BF)
                b["dkvt"][vcols, krows] = mm_tn(do2, probs).astype(BF)
            else:
                b["ctx"][tile(2 * half + s, SEQ), at_cols] = mm_tn(ds, q2).astype(BF)
                b["ctx"][tile(4 + 2 * half + s, SEQ), at_cols] = mm_tn(probs, do2).astype(BF)

        loop(2 * PAIRS, attend_back)
        own_b = gather_to(group_qo, "b", lambda p: b["d4"].at[p], rows_of(b["rxb"]), sec)
        if not cross:

            def kv_quarter(p):
                return b["ctx"].at[tile(p, ROWS), pl.ds(0, 384)]

            own_b2 = gather_to(
                group_qo, "b2", kv_quarter, lambda r: b["dkvt"].at[pl.ds(r * ROWS, ROWS), pl.ds(0, 384)], sec
            )

        if cross:
            kv_a(0)
            kv_a(1)

        def n1_back(i):
            rows = tile(i)
            grad = mm_nt(b["d4"][0], b["wq"][rows, 0:384]) + mm_nt(b["d4"][1], b["wq"][rows, 384:768])
            if not cross:
                for k in range(4):
                    quarter = b["ctx"][k * ROWS : (k + 1) * ROWS, 0:384]
                    grad = grad + mm_nt(quarter, b["wkv"][rows, 384 * k : 384 * (k + 1)])
            b["dn"][:, tile(i)] = grad

        loop(3, n1_back)

        def done1(rows, value):
            ins[rows, :] = value.astype(BF)

        norm_back(b["xh1"], 0, g1, 0, done1)
        if not cross:
            send("back", 0, ins, b["dyb"], (other, dp))

        vec_send(0)
        if cross:
            ffn_forward()
            down_a()
            up_a()
            vec_add(0)
            vec_send(1)
            qo_a()
            kv_b(0)
            kv_b(1)
            vec_add(1)
            vec_send(2)
            down_b()
            up_b()
            qo_b()
            vec_add(2)
            vec_out()
            kv_end(0)
            kv_end(1)
        else:
            ffn_forward()
            down_a()
            up_a()
            qo_a()
            vec_add(0)
            vec_send(1)
            down_b()
            up_b()
            qo_b()
            vec_add(1)
            vec_send(2)
            vec_add(2)
            vec_out()
        qo_end()
        down_end()
        up_end()
        for copy in pending:
            copy.wait_send()

    pl.when(sec == 0)(lambda: branch(0))
    pl.when(sec == 1)(lambda: branch(1))


def deliver(*refs):
    for a, out in zip(refs[:12], refs[12:]):
        out[...] = a[...].reshape(out.shape)


def on_device(
    tokens, context, out_cot, group_id, ctx_len, fut_len, loss_weight,
    norm_gain1, norm_bias1, w_query, w_keyval, w_out,
    norm_gain2, norm_bias2, w_up, up_bias, w_down,
):
    smem = pl.BlockSpec(memory_space=pltpu.SMEM)
    vmem = pl.BlockSpec(memory_space=pltpu.VMEM)
    hbm = pl.BlockSpec(memory_space=pl.ANY)
    shape = jax.ShapeDtypeStruct
    outs = pl.pallas_call(
        kernel,
        out_shape=(
            shape((ROWS, D), BF),
            shape((ROWS, D), BF),
            shape((1, 12), F32),
            shape((1, 12), F32),
            shape((12, D), F32),
            shape((12, 2 * D), F32),
            shape((12, D), F32),
            shape((1, 12), F32),
            shape((1, 12), F32),
            shape((12, FF), F32),
            shape((1, 48), F32),
            shape((48, D), F32),
        ),
        in_specs=[smem] * 3 + [vmem] + [hbm] * 3 + [vmem] * 5 + [hbm] * 5,
        out_specs=[vmem] * 12,
        scratch_shapes=[pltpu.VMEM(s, t) for s, t in BUFS.values()]
        + [pltpu.SemaphoreType.DMA((N_SEMS,)), pltpu.SemaphoreType.DMA((N_SEMS,))],
        compiler_params=pltpu.CompilerParams(
            collective_id=0, has_side_effects=True, vmem_limit_bytes=64 * 1024 * 1024 - 4096
        ),
    )(
        group_id, ctx_len, fut_len, loss_weight,
        tokens.reshape(ROWS, D), context.reshape(2 * CTX, D), out_cot.reshape(ROWS, D),
        norm_gain1, norm_bias1, norm_gain2, norm_bias2, up_bias,
        w_query[0], w_keyval[0], w_out[0], w_up[0], w_down[0],
    )
    outs = pl.pallas_call(
        deliver,
        out_shape=[
            shape((a.shape[0], 1, a.shape[1]) if a.shape[0] == 12 else a.shape, a.dtype) for a in outs
        ],
        in_specs=[vmem] * 12,
        out_specs=[vmem] * 12,
    )(*outs)
    acts, ins, gg1, gb1, gq, gkv, go, gg2, gb2, gup, gub, gdn = outs
    seqs = (1, 2, SEQ, D)
    rows = [g.reshape(1, 12, g.shape[-1]) for g in (gq, gkv, go, gup)]
    return (
        acts.reshape(seqs), ins.reshape(seqs), gg1, gb1, *rows[:3],
        gg2, gb2, rows[3], gub, gdn[None],
    )


def solution(mesh):
    dp, sec = "dp", "section"
    vec, mat = P(sec, None), P(sec, None, None)
    return jax.shard_map(
        on_device,
        mesh=mesh,
        in_specs=(P(dp, None, None),) * 3 + (P(dp),) * 3 + (P(dp, None),)
        + (vec, vec, mat, mat, mat, vec, vec, mat, vec, mat),
        out_specs=(P(sec, dp, None, None),) * 2 + (P(sec, dp),) * 2 + (P(sec, dp, None),) * 3
        + (P(sec, dp),) * 2 + (P(sec, dp, None), P(sec, dp), P(sec, dp, None)),
        check_vma=False,
    )
```
